256 devices in a mesh: series: 8 (over y, core), tm: 32 (over x, z).
Axes of the slice: x: 4, y: 4, z: 8, core: 2. Of those that a mesh axis runs over, the one named last changes fastest.
Arguments:
- series_data: float32 [8, 131072, 128], P('series', 'tm'), may hold values from -600 to 600, as said below
- cotangent: float32 [8, 131072, 128], P('series', 'tm'), may hold values from -40 to 40, as said below
- in_weight: bfloat16 [128, 128], replicated, may hold values from -0.5 to 0.5
- convolution_weight: bfloat16 [2, 2, 128, 256], replicated, may hold values from -0.375 to 0.375
- convolution_bias: float32 [2, 256], replicated, may hold values from -3 to 3
- res_weight: bfloat16 [128, 128], replicated, may hold values from -0.5 to 0.5
- skip_weight: bfloat16 [2, 128, 256], replicated, may hold values from -0.5 to 0.5
- output_weight: bfloat16 [256, 128], replicated, may hold values from -0.375 to 0.375
- norm_gain_vector: float32 [128], replicated, may hold values from 0.5 to 1.5
- norm_offset_vector: float32 [128], replicated, may hold values from -3 to 3
Outputs:
- series_gradient: float32 [8, 131072, 128], P('series', 'tm')
- conv_grad: float32 [2, 2, 128, 256], replicated
- bias_grad: float32 [2, 256], replicated
- res_grad: float32 [128, 128], replicated
- skip_grad: float32 [2, 128, 256], replicated
- out_grad: float32 [256, 128], replicated
- in_grad: float32 [128, 128], replicated
- gain_grad: float32 [128], replicated
- shift_grad: float32 [128], replicated
The draws below stay inside these ranges and needn't reach their ends.
Inputs may be any that keep to these rules, and one draw needn't show every extreme that they name: `series_data`: readings of the sensor channels of each series. `cotangent`: loss gradients for each channel and step.
All inputs are finite; a program needn't handle non-finite values.
Results may differ from the reference program's by a relative error of at most 0.0084.
The reference program's roundings to bfloat16 on the way count: a program that leaves them out, or rounds other values in their place, can miss the bound.
Values may be sent and summed in bfloat16 or wider, within the bound.
A program may use at most 64 MiB of HBM per device.

```python
import math
import jax
import jax.numpy as jnp
from jax import lax

F = 128
C = 128
S = 256
FIRST_DILATION = 256
SECOND_DILATION = 512
STEPS = 131072
SERIES = 8


def sensor_parts(key, noise, rise, row_spread, col_low, col_high):
    row_key, col_key, level_key = jax.random.split(key, 3)
    positions = jnp.arange(STEPS, dtype=jnp.float32) / (STEPS - 1)
    row_scale = jnp.exp(math.log(rise) * positions[None, :, None] + math.log(row_spread) * jax.random.uniform(row_key, (SERIES, STEPS, 1), dtype=jnp.float32))
    col_scale = jnp.exp(math.log(col_low) + (math.log(col_high) - math.log(col_low)) * jax.random.uniform(col_key, (SERIES, 1, F), dtype=jnp.float32))
    level = jax.random.uniform(level_key, (SERIES, 1, F), dtype=jnp.float32, minval=-2.0, maxval=2.0)
    return (col_scale, level, row_scale * noise)


def draw_series_data(key, part):
    key = jax.random.fold_in(key, 11)
    field_key, noise_key = jax.random.split(key, 2)
    noise = jnp.clip(jax.random.normal(noise_key, (SERIES, STEPS, F), dtype=jnp.float32), -4.0, 4.0)
    row_spread = 4.0
    col_scale, level, varying = sensor_parts(field_key, noise, 3.0, row_spread, 1.0, 10.0)
    return col_scale * (level + varying)


def draw_cotangent(key, part):
    key = jax.random.fold_in(key, 23)
    field_key, noise_key = jax.random.split(key, 2)
    noise = jnp.clip(jax.random.normal(noise_key, (SERIES, STEPS, F), dtype=jnp.float32), -4.0, 4.0)
    row_spread = 4.0
    col_scale, level, varying = sensor_parts(field_key, noise, 3.0, row_spread, 0.03, 0.3)
    return col_scale * (level + varying)


def centred(rng, dims, deviation, bound, kind=jnp.bfloat16):
    return jnp.clip(deviation * jax.random.normal(rng, dims, jnp.float32), -bound, bound).astype(kind)


def setup_inputs(seed: int = 0) -> dict:
    key_of = jax.random.split(jax.random.key(seed), 11)
    return {
        "series_data": draw_series_data(jax.random.fold_in(key_of[10], 71), 0),
        "cotangent": draw_cotangent(jax.random.fold_in(key_of[10], 71), 0),
        "in_weight": centred(key_of[2], (F, C), F ** -0.5, 0.5),
        "convolution_weight": centred(key_of[3], (2, 2, C, 2 * C), (2 * C) ** -0.5, 0.375),
        "convolution_bias": centred(key_of[4], (2, 2 * C), 0.5, 3.0, jnp.float32),
        "res_weight": centred(key_of[5], (C, C), C ** -0.5, 0.5),
        "skip_weight": centred(key_of[6], (2, C, S), C ** -0.5, 0.5),
        "output_weight": centred(key_of[7], (S, F), S ** -0.5, 0.375),
        "norm_gain_vector": jnp.clip(1.0 + 0.1 * jax.random.normal(key_of[8], (F,), jnp.float32), 0.5, 1.5),
        "norm_offset_vector": centred(key_of[9], (F,), 0.5, 3.0, jnp.float32),
    }


epsilon = 1e-05
gelu_coeff = 0.7978845608
cubic_coeff = 0.044715

def gelu_pair(values):
    inner = gelu_coeff * (values + cubic_coeff * values * values * values)
    tangent = jnp.tanh(inner)
    output = 0.5 * values * (1.0 + tangent)
    slope = 0.5 * (1.0 + tangent) + 0.5 * values * (1.0 - tangent * tangent) * gelu_coeff * (1.0 + 3.0 * cubic_coeff * values * values)
    return (output, slope)

def matrix_product(left, right):
    return jnp.dot(left, right, preferred_element_type=jnp.float32)

def row_contraction(left, right):
    return lax.dot_general(left, right, (((0,), (0,)), ((), ())), preferred_element_type=jnp.float32)

def transposed_product(left, right):
    return lax.dot_general(left, right, (((1,), (1,)), ((), ())), preferred_element_type=jnp.float32)

def shifted_backward(values, span):
    padding = jnp.zeros((span, values.shape[1]), values.dtype)
    return jnp.concatenate([padding, values[:values.shape[0] - span]], axis=0)

def shifted_forward(values, span):
    padding = jnp.zeros((span, values.shape[1]), values.dtype)
    return jnp.concatenate([values[span:], padding], axis=0)

def gate_forward_step(layer_in, weights, bias, span):
    pre_act = matrix_product(shifted_backward(layer_in, span), weights[0]) + matrix_product(layer_in, weights[1]) + bias
    half_cols = pre_act.shape[1] // 2
    gated = (jnp.tanh(pre_act[:, :half_cols]) * jax.nn.sigmoid(pre_act[:, half_cols:])).astype(jnp.bfloat16)
    return (pre_act, gated)

def gate_backward(pre_act, incoming):
    half_cols = pre_act.shape[1] // 2
    tanh_part = jnp.tanh(pre_act[:, :half_cols])
    sigm_part = jax.nn.sigmoid(pre_act[:, half_cols:])
    return jnp.concatenate([incoming * sigm_part * (1.0 - tanh_part * tanh_part), incoming * tanh_part * sigm_part * (1.0 - sigm_part)], axis=1)

def one_series(readings, loss_gradient, in_weight, convolution_weight, convolution_bias, res_weight, skip_weight, output_weight, norm_gain_vector, norm_offset_vector):
    total_timesteps = readings.shape[0]
    level_mean = lax.optimization_barrier(jnp.sum(readings, axis=0)) / total_timesteps
    mean_removed = readings - level_mean
    variance = lax.optimization_barrier(jnp.sum(mean_removed * mean_removed, axis=0)) / total_timesteps
    inverse_deviation = lax.rsqrt(variance + epsilon)
    spread = jnp.sqrt(variance + epsilon)
    normalized_input = mean_removed * inverse_deviation
    normalized_series = (normalized_input * norm_gain_vector + norm_offset_vector).astype(jnp.bfloat16)
    zeroth_level = matrix_product(normalized_series, in_weight).astype(jnp.bfloat16)
    first_activation, first_gated = gate_forward_step(zeroth_level, convolution_weight[0], convolution_bias[0], FIRST_DILATION)
    first_level = (zeroth_level.astype(jnp.float32) + matrix_product(first_gated, res_weight)).astype(jnp.bfloat16)
    second_activation, second_gated = gate_forward_step(first_level, convolution_weight[1], convolution_bias[1], SECOND_DILATION)
    skip_total = matrix_product(first_gated, skip_weight[0]) + matrix_product(second_gated, skip_weight[1])
    skip_value, skip_slope = gelu_pair(skip_total)
    relu_output = skip_value.astype(jnp.bfloat16)
    prediction = matrix_product(relu_output, output_weight)
    scaled = (loss_gradient * spread / norm_gain_vector).astype(jnp.bfloat16)
    out_grad = row_contraction(relu_output, scaled)
    back_skip = (transposed_product(scaled, output_weight) * skip_slope).astype(jnp.bfloat16)
    skip_grad = jnp.stack([row_contraction(first_gated, back_skip), row_contraction(second_gated, back_skip)])
    pre_two = gate_backward(second_activation, transposed_product(back_skip, skip_weight[1]))
    second_preactivation_second = pre_two.astype(jnp.bfloat16)
    second_convolved = jnp.stack([row_contraction(shifted_backward(first_level, SECOND_DILATION), second_preactivation_second), row_contraction(first_level, second_preactivation_second)])
    bias_two = lax.optimization_barrier(jnp.sum(pre_two, axis=0))
    first_gradient = (transposed_product(second_preactivation_second, convolution_weight[1, 1]) + transposed_product(shifted_forward(second_preactivation_second, SECOND_DILATION), convolution_weight[1, 0])).astype(jnp.bfloat16)
    res_grad = row_contraction(first_gated, first_gradient)
    pre_one = gate_backward(first_activation, transposed_product(back_skip, skip_weight[0]) + transposed_product(first_gradient, res_weight))
    first_preactivation_second = pre_one.astype(jnp.bfloat16)
    first_convolved = jnp.stack([row_contraction(shifted_backward(zeroth_level, FIRST_DILATION), first_preactivation_second), row_contraction(zeroth_level, first_preactivation_second)])
    bias_one = lax.optimization_barrier(jnp.sum(pre_one, axis=0))
    zeroth_gradient = (first_gradient.astype(jnp.float32) + transposed_product(first_preactivation_second, convolution_weight[0, 1]) + transposed_product(shifted_forward(first_preactivation_second, FIRST_DILATION), convolution_weight[0, 0])).astype(jnp.bfloat16)
    in_grad = row_contraction(normalized_series, zeroth_gradient)
    normalized_gradient = transposed_product(zeroth_gradient, in_weight) * norm_gain_vector
    first_total = lax.optimization_barrier(jnp.sum(normalized_gradient, axis=0))
    second_total = lax.optimization_barrier(jnp.sum(normalized_gradient * normalized_input, axis=0))
    output_first = lax.optimization_barrier(jnp.sum(loss_gradient, axis=0))
    output_second = lax.optimization_barrier(jnp.sum(loss_gradient * (prediction - norm_offset_vector) / norm_gain_vector, axis=0))
    series_gradient = inverse_deviation * (normalized_gradient - first_total / total_timesteps - normalized_input * second_total / total_timesteps) + output_first / total_timesteps + output_second * normalized_input / total_timesteps
    gain_grad = second_total / norm_gain_vector - output_second * spread / norm_gain_vector
    shift_grad = first_total / norm_gain_vector - output_first * spread / norm_gain_vector
    conv_grad = jnp.stack([first_convolved, second_convolved])
    bias_grad = jnp.stack([bias_one, bias_two])
    return (series_gradient, conv_grad, bias_grad, res_grad, skip_grad, out_grad, in_grad, gain_grad, shift_grad)

def reference(series_data, cotangent, in_weight, convolution_weight, convolution_bias, res_weight, skip_weight, output_weight, norm_gain_vector, norm_offset_vector):

    def single(inputs_pair):
        return one_series(inputs_pair[0], inputs_pair[1], in_weight, convolution_weight, convolution_bias, res_weight, skip_weight, output_weight, norm_gain_vector, norm_offset_vector)
    results = lax.map(single, (series_data, cotangent))
    return (results[0], lax.optimization_barrier(jnp.sum(results[1], axis=0)), lax.optimization_barrier(jnp.sum(results[2], axis=0)), lax.optimization_barrier(jnp.sum(results[3], axis=0)), lax.optimization_barrier(jnp.sum(results[4], axis=0)), lax.optimization_barrier(jnp.sum(results[5], axis=0)), lax.optimization_barrier(jnp.sum(results[6], axis=0)), lax.optimization_barrier(jnp.sum(results[7], axis=0)), lax.optimization_barrier(jnp.sum(results[8], axis=0)))
```

```python
import jax
import jax.numpy as jnp
from jax import lax
from jax.experimental import pallas as pl
from jax.experimental.pallas import tpu as pltpu
from jax.sharding import PartitionSpec as P

FIRST_DILATION = 256
SECOND_DILATION = 512


epsilon = 1e-05
gelu_coeff = 0.7978845608
cubic_coeff = 0.044715


def shifted(block, axis, distance):
    devices = range(lax.axis_size(axis))
    route = [(i - distance, i) for i in devices if i - distance in devices]
    return lax.ppermute(block, axis, route)


def gelu_pair(values):
    inner = gelu_coeff * (values + cubic_coeff * values * values * values)
    tangent = jnp.tanh(inner)
    output = 0.5 * values * (1.0 + tangent)
    slope = 0.5 * (1.0 + tangent) + 0.5 * values * (1.0 - tangent * tangent) * gelu_coeff * (
        1.0 + 3.0 * cubic_coeff * values * values
    )
    return (output, slope)


def matrix_product(left, right):
    return jnp.dot(left, right, preferred_element_type=jnp.float32)


def row_contraction(left, right):
    return lax.dot_general(
        left, right, (((0,), (0,)), ((), ())), preferred_element_type=jnp.float32
    )


def transposed_product(left, right):
    return lax.dot_general(
        left, right, (((1,), (1,)), ((), ())), preferred_element_type=jnp.float32
    )


def gate_window_step(extended, weights, bias, span):
    produced = extended.shape[0] - span
    pre_act = (
        matrix_product(extended[:produced], weights[0])
        + matrix_product(extended[span:], weights[1])
        + bias
    )
    half_cols = pre_act.shape[1] // 2
    gated = (jnp.tanh(pre_act[:, :half_cols]) * jax.nn.sigmoid(pre_act[:, half_cols:])).astype(
        jnp.bfloat16
    )
    return (pre_act, gated)


def gate_backward(pre_act, incoming):
    half_cols = pre_act.shape[1] // 2
    tanh_part = jnp.tanh(pre_act[:, :half_cols])
    sigm_part = jax.nn.sigmoid(pre_act[:, half_cols:])
    return jnp.concatenate(
        [
            incoming * sigm_part * (1.0 - tanh_part * tanh_part),
            incoming * tanh_part * sigm_part * (1.0 - sigm_part),
        ],
        axis=1,
    )


TM = 32
SER = 8
MESH = pl.DeviceIdType.MESH


def greet(pairs):
    barrier = pltpu.get_barrier_semaphore()
    total = 0
    for axis, count in pairs:
        me = lax.axis_index(axis)

        def hello(k, carry, axis=axis, count=count, me=me):
            pl.semaphore_signal(
                barrier, inc=1, device_id={axis: lax.rem(me + k, count)}, device_id_type=MESH
            )
            return carry

        lax.fori_loop(1, count, hello, 0)
        total += count - 1
    pl.semaphore_wait(barrier, total)


def exchange_kernel(own_ref, all_ref, send_sem, recv_sem):
    me = lax.axis_index("tm")
    greet([("tm", TM)])
    all_ref[pl.ds(me, 1)] = own_ref[...][None]

    def copy(peer, slot):
        return pltpu.make_async_remote_copy(
            src_ref=own_ref,
            dst_ref=all_ref.at[slot],
            send_sem=send_sem.at[peer],
            recv_sem=recv_sem.at[slot],
            device_id={"tm": peer},
            device_id_type=MESH,
        )

    def send(k, carry):
        copy(lax.rem(me + k, TM), me).start()
        return carry

    def finish(k, carry):
        peer = lax.rem(me + k, TM)
        copy(peer, peer).wait()
        return carry

    lax.fori_loop(1, TM, send, 0)
    lax.fori_loop(1, TM, finish, 0)


def exchange(own, collective_id):
    return pl.pallas_call(
        exchange_kernel,
        out_shape=jax.ShapeDtypeStruct((TM, 8, 128), jnp.float32),
        in_specs=[pl.BlockSpec(memory_space=pltpu.VMEM)],
        out_specs=pl.BlockSpec(memory_space=pltpu.VMEM),
        scratch_shapes=[pltpu.SemaphoreType.DMA((TM,)), pltpu.SemaphoreType.DMA((TM,))],
        compiler_params=pltpu.CompilerParams(collective_id=collective_id, has_side_effects=True),
    )(own)


def reduce_kernel(
    grads_ref,
    small_ref,
    out_ref,
    small_out_ref,
    recv_one,
    block,
    recv_two,
    small_all,
    s_one,
    r_one,
    s_two,
    r_two,
    s_three,
    r_three,
    s_four,
    r_four,
    s_small,
    r_small,
):
    ser = lax.axis_index("series")
    tm = lax.axis_index("tm")
    greet([("series", SER), ("tm", TM)])

    def remote(src, dst, s_sem, r_sem, axis, peer):
        return pltpu.make_async_remote_copy(
            src_ref=src,
            dst_ref=dst,
            send_sem=s_sem,
            recv_sem=r_sem,
            device_id={axis: peer},
            device_id_type=MESH,
        )

    def rows(start, size):
        return pl.ds(pl.multiple_of(start, 8), size)

    def each(lo, hi, body):
        def run(k, carry):
            body(k)
            return carry

        lax.fori_loop(lo, hi, run, 0)

    def one(g, peer, slot):
        return remote(
            grads_ref.at[rows(g * 1024 + peer * 128, 128)],
            recv_one.at[g, slot],
            s_one.at[g, peer],
            r_one.at[g, slot],
            "series",
            peer,
        )

    def small(peer, slot):
        return remote(
            small_ref, small_all.at[slot], s_small.at[peer], r_small.at[slot], "series", peer
        )

    def two(g, piece, slot):
        return remote(
            block.at[g, rows(piece * 8, 8)],
            recv_two.at[slot],
            s_two.at[g, piece],
            r_two.at[slot],
            "tm",
            g * 16 + piece,
        )

    def three(g, piece, peer):
        where = out_ref.at[rows(g * 1024 + ser * 128 + piece * 8, 8)]
        return remote(where, where, s_three.at[peer], r_three.at[g, piece], "tm", peer)

    def four(g, peer, slot):
        where = out_ref.at[rows(g * 1024 + slot * 128, 128)]
        return remote(where, where, s_four.at[g, peer], r_four.at[g, slot], "series", peer)

    small_all[pl.ds(ser, 1)] = small_ref[...][None]
    for g in range(2):
        each(1, SER, lambda k: one(g, lax.rem(ser + k, SER), ser).start())
    each(1, SER, lambda k: small(lax.rem(ser + k, SER), ser).start())
    for g in range(2):

        def take(k):
            peer = lax.rem(ser + k, SER)
            one(g, peer, peer).wait()

        each(1, SER, take)
        total = grads_ref[rows(g * 1024 + ser * 128, 128)]
        recv_one[g, pl.ds(ser, 1)] = total[None]
        total = recv_one[g, 0]
        for s in range(1, SER):
            total = total + recv_one[g, s]
        block[g] = total

        def push(piece):
            @pl.when(g * 16 + piece != tm)
            def _():
                two(g, piece, tm).start()

        each(0, 16, push)
    for g in range(2):

        @pl.when(tm // 16 == g)
        def _():
            mine = tm - g * 16

            def pull(k):
                peer = lax.rem(tm + k, TM)
                two(g, mine, peer).wait_recv()

            each(1, TM, pull)
            recv_two[pl.ds(tm, 1)] = block[g, rows(mine * 8, 8)][None]
            total = recv_two[0]
            for t in range(1, TM):
                total = total + recv_two[t]
            out_ref[rows(g * 1024 + ser * 128 + mine * 8, 8)] = total
            each(1, TM, lambda k: three(g, mine, lax.rem(tm + k, TM)).start())

    for g in range(2):

        def arrive(piece):
            @pl.when(g * 16 + piece != tm)
            def _():
                two(g, piece, tm).wait_send()
                three(g, piece, g * 16 + piece).wait_recv()

        each(0, 16, arrive)
        each(1, SER, lambda k: four(g, lax.rem(ser + k, SER), ser).start())
    for g in range(2):

        @pl.when(tm // 16 == g)
        def _():
            each(1, TM, lambda k: three(g, tm - g * 16, lax.rem(tm + k, TM)).wait_send())

    def last(k):
        peer = lax.rem(ser + k, SER)
        small(peer, peer).wait()

    each(1, SER, last)
    total = small_all[0]
    for s in range(1, SER):
        total = total + small_all[s]
    small_out_ref[...] = total
    for g in range(2):

        def done(k):
            peer = lax.rem(ser + k, SER)
            four(g, peer, ser).wait_send()
            four(g, peer, peer).wait_recv()

        each(1, SER, done)


def reduce_all(grads, small):
    vmem = pl.BlockSpec(memory_space=pltpu.VMEM)
    sem = pltpu.SemaphoreType.DMA
    return pl.pallas_call(
        reduce_kernel,
        out_shape=(
            jax.ShapeDtypeStruct((2048, 128), jnp.float32),
            jax.ShapeDtypeStruct((8, 128), jnp.float32),
        ),
        in_specs=[vmem, vmem],
        out_specs=(vmem, vmem),
        scratch_shapes=[
            pltpu.VMEM((2, SER, 128, 128), jnp.float32),
            pltpu.VMEM((2, 128, 128), jnp.float32),
            pltpu.VMEM((TM, 8, 128), jnp.float32),
            pltpu.VMEM((SER, 8, 128), jnp.float32),
            sem((2, SER)),
            sem((2, SER)),
            sem((2, 16)),
            sem((TM,)),
            sem((TM,)),
            sem((2, 16)),
            sem((2, SER)),
            sem((2, SER)),
            sem((SER,)),
            sem((SER,)),
        ],
        compiler_params=pltpu.CompilerParams(
            collective_id=2, has_side_effects=True, vmem_limit_bytes=24 * 1024 * 1024
        ),
    )(grads, small)


def on_device(
    series_data,
    cotangent,
    in_weight,
    convolution_weight,
    convolution_bias,
    res_weight,
    skip_weight,
    output_weight,
    norm_gain_vector,
    norm_offset_vector,
):
    readings = series_data[0]
    loss_gradient = cotangent[0]
    sequence_length = readings.shape[0]
    total_timesteps = sequence_length * lax.axis_size("tm")
    local_sum = jnp.sum(readings, axis=0)
    local_mean = local_sum / sequence_length
    local_centred = jnp.sum(jnp.square(readings - local_mean), axis=0)
    zero = jnp.zeros((6, 128), jnp.float32)
    parts = exchange(jnp.concatenate([local_sum[None], local_centred[None], zero]), 0)
    level_mean = jnp.sum(parts[:, 0], axis=0) / total_timesteps
    spreads = jnp.square(parts[:, 0] / sequence_length - level_mean)
    variance = (
        jnp.sum(parts[:, 1], axis=0) + sequence_length * jnp.sum(spreads, axis=0)
    ) / total_timesteps
    mean_removed = readings - level_mean
    inverse_deviation = lax.rsqrt(variance + epsilon)
    spread = jnp.sqrt(variance + epsilon)
    normalized_input = mean_removed * inverse_deviation
    normalized_series = (normalized_input * norm_gain_vector + norm_offset_vector).astype(
        jnp.bfloat16
    )
    zeroth_level = matrix_product(normalized_series, in_weight).astype(jnp.bfloat16)
    zeroth_border = shifted(zeroth_level[sequence_length - FIRST_DILATION :], "tm", 1)
    zeroth_padded = jnp.concatenate([zeroth_border, zeroth_level], axis=0)
    first_activation, first_gated = gate_window_step(
        zeroth_padded, convolution_weight[0], convolution_bias[0], FIRST_DILATION
    )
    first_level = (
        zeroth_level.astype(jnp.float32) + matrix_product(first_gated, res_weight)
    ).astype(jnp.bfloat16)
    first_border = shifted(first_level[sequence_length - SECOND_DILATION :], "tm", 1)
    first_padded = jnp.concatenate([first_border, first_level], axis=0)
    second_activation, second_gated = gate_window_step(
        first_padded, convolution_weight[1], convolution_bias[1], SECOND_DILATION
    )
    skip_total = matrix_product(first_gated, skip_weight[0]) + matrix_product(
        second_gated, skip_weight[1]
    )
    skip_value, skip_slope = gelu_pair(skip_total)
    relu_output = skip_value.astype(jnp.bfloat16)
    prediction = matrix_product(relu_output, output_weight)
    scaled = (loss_gradient * spread / norm_gain_vector).astype(jnp.bfloat16)
    local_a = jnp.sum(loss_gradient, axis=0)
    local_second = jnp.sum(
        loss_gradient * (prediction - norm_offset_vector) / norm_gain_vector, axis=0
    )
    out_grad = row_contraction(relu_output, scaled)
    back_skip = (transposed_product(scaled, output_weight) * skip_slope).astype(jnp.bfloat16)
    skip_grad = jnp.stack(
        [row_contraction(first_gated, back_skip), row_contraction(second_gated, back_skip)]
    )
    pre_two = gate_backward(second_activation, transposed_product(back_skip, skip_weight[1]))
    second_preactivation_second = pre_two.astype(jnp.bfloat16)
    second_convolved = jnp.stack(
        [
            row_contraction(first_padded[:sequence_length], second_preactivation_second),
            row_contraction(first_padded[SECOND_DILATION:], second_preactivation_second),
        ]
    )
    bias_two = jnp.sum(pre_two, axis=0)
    second_leading = shifted(second_preactivation_second[:SECOND_DILATION], "tm", -1)
    second_trailing = jnp.concatenate([second_preactivation_second, second_leading], axis=0)[
        SECOND_DILATION:
    ]
    first_gradient = (
        transposed_product(second_preactivation_second, convolution_weight[1, 1])
        + transposed_product(second_trailing, convolution_weight[1, 0])
    ).astype(jnp.bfloat16)
    res_grad = row_contraction(first_gated, first_gradient)
    pre_one = gate_backward(
        first_activation,
        transposed_product(back_skip, skip_weight[0])
        + transposed_product(first_gradient, res_weight),
    )
    first_preactivation_second = pre_one.astype(jnp.bfloat16)
    first_convolved = jnp.stack(
        [
            row_contraction(zeroth_padded[:sequence_length], first_preactivation_second),
            row_contraction(zeroth_padded[FIRST_DILATION:], first_preactivation_second),
        ]
    )
    bias_one = jnp.sum(pre_one, axis=0)
    first_leading = shifted(first_preactivation_second[:FIRST_DILATION], "tm", -1)
    first_trailing = jnp.concatenate([first_preactivation_second, first_leading], axis=0)[
        FIRST_DILATION:
    ]
    zeroth_gradient = (
        first_gradient.astype(jnp.float32)
        + transposed_product(first_preactivation_second, convolution_weight[0, 1])
        + transposed_product(first_trailing, convolution_weight[0, 0])
    ).astype(jnp.bfloat16)
    in_grad = row_contraction(normalized_series, zeroth_gradient)
    normalized_gradient = transposed_product(zeroth_gradient, in_weight) * norm_gain_vector
    part_a = jnp.sum(normalized_gradient, axis=0)
    second_portion = jnp.sum(normalized_gradient * normalized_input, axis=0)
    parts = exchange(
        jnp.concatenate(
            [
                jnp.stack([part_a, second_portion, local_a, local_second]),
                bias_one.reshape(2, 128),
                bias_two.reshape(2, 128),
            ]
        ),
        1,
    )
    parts = jnp.sum(parts, axis=0)
    first_total, second_total, output_first, output_second = parts[0], parts[1], parts[2], parts[3]
    series_gradient = (
        inverse_deviation
        * (
            normalized_gradient
            - first_total / total_timesteps
            - normalized_input * second_total / total_timesteps
        )
        + output_first / total_timesteps
        + output_second * normalized_input / total_timesteps
    )
    gain_part = second_total / norm_gain_vector - output_second * spread / norm_gain_vector
    shift_part = first_total / norm_gain_vector - output_first * spread / norm_gain_vector
    halves = lambda a: jnp.concatenate([a[..., :128], a[..., 128:]], axis=-2).reshape(-1, 128)
    grads = jnp.concatenate(
        [
            halves(second_convolved),
            halves(skip_grad),
            halves(first_convolved),
            out_grad,
            res_grad,
            in_grad,
        ]
    )
    small = jnp.concatenate(
        [gain_part[None], shift_part[None], parts[4:], jnp.zeros((2, 128), jnp.float32)]
    )
    reduced, small = reduce_all(grads, small)

    def join(block):
        block = block.reshape(-1, 2, 128, 128)
        return jnp.concatenate([block[:, 0], block[:, 1]], axis=-1)

    conv_grad = jnp.stack([join(reduced[1024:1536]), join(reduced[:512])])
    skip_total_grad = join(reduced[512:1024])
    out_total = reduced[1536:1792]
    res_total = reduced[1792:1920]
    in_total = reduced[1920:]
    gain_total = small[0]
    shift_total = small[1]
    bias_grad = small[2:6].reshape(2, 256)
    return (
        series_gradient[None],
        conv_grad,
        bias_grad,
        res_total,
        skip_total_grad,
        out_total,
        in_total,
        gain_total,
        shift_total,
    )


def solution(mesh):
    placed = (
        P("series", "tm", None),
        P("series", "tm", None),
        P(),
        P(),
        P(),
        P(),
        P(),
        P(),
        P(),
        P(),
    )
    return jax.shard_map(
        on_device,
        mesh=mesh,
        in_specs=placed,
        out_specs=(P("series", "tm", None), P(), P(), P(), P(), P(), P(), P(), P()),
        check_vma=False,
    )
```

```python
import jax
import jax.numpy as jnp
from jax import lax
from jax.experimental import pallas as pl
from jax.experimental.pallas import tpu as pltpu
from jax.sharding import PartitionSpec as P

FIRST = 256
SECOND = 512
TM = 32
SER = 8
X = 4
Z = 8
GROUP = X * SER
ROWS = 512
MESH = pl.DeviceIdType.MESH
EARLY, LATE, LAST = 40, 24, 8

epsilon = 1e-05
gelu_coeff = 0.7978845608
cubic_coeff = 0.044715


def nn(left, right):
    return jnp.dot(left, right, preferred_element_type=jnp.float32)


def nt(left, right):
    return lax.dot_general(
        left, right, (((1,), (1,)), ((), ())), preferred_element_type=jnp.float32
    )


def tn(left, right):
    return lax.dot_general(
        left, right, (((0,), (0,)), ((), ())), preferred_element_type=jnp.float32
    )


def fold(values):
    return jnp.sum(values.reshape(-1, 8, values.shape[-1]), axis=0)


def each(lo, hi, body):
    def run(k, carry):
        body(k)
        return carry

    lax.fori_loop(lo, hi, run, 0)


def at(start, size):
    return pl.ds(pl.multiple_of(start, 8), size)


def remote(src, dst, s_sem, r_sem, device):
    return pltpu.make_async_remote_copy(
        src_ref=src,
        dst_ref=dst,
        send_sem=s_sem,
        recv_sem=r_sem,
        device_id=device,
        device_id_type=MESH,
    )


def block_kernel(
    x_hbm,
    cot_hbm,
    w_in,
    w_conv,
    bias,
    w_res,
    w_skip,
    w_out,
    gain_ref,
    offset_ref,
    grad_hbm,
    early_out,
    late_out,
    last_out,
    x,
    cot,
    level_zero,
    level_one,
    gated_one,
    tanh_one,
    sigm_one,
    incoming_one,
    near_one,
    far_one,
    near_zero,
    far_zero,
    hat,
    early,
    late,
    last,
    in_grad,
    acc,
    stats,
    stats_all,
    ends,
    ends_all,
    early_one,
    late_one,
    last_one,
    early_two,
    late_two,
    last_two,
    early_block,
    late_block,
    last_block,
    load_sem,
    store_sem,
    halo_s,
    halo_r,
    stats_s,
    stats_r,
    ends_s,
    ends_r,
    one_s,
    one_r,
    two_s,
    two_r,
    three_s,
    three_r,
):
    steps = x.shape[0]
    chunks = steps // ROWS
    total_steps = float(steps * TM)
    ser = lax.axis_index("series")
    tm = lax.axis_index("tm")
    place, depth = tm // Z, lax.rem(tm, Z)
    mine = place * SER + ser

    def member(p):
        return {"series": lax.rem(p, SER), "tm": (p // SER) * Z + depth}

    def load_x(c):
        return pltpu.make_async_copy(
            x_hbm.at[at(c * ROWS, ROWS)], x.at[at(c * ROWS, ROWS)], load_sem.at[c]
        )

    load_cot = pltpu.make_async_copy(cot_hbm, cot, load_sem.at[chunks])
    each(0, chunks, lambda c: load_x(c).start())
    load_cot.start()

    barrier = pltpu.get_barrier_semaphore()

    def hello(device):
        pl.semaphore_signal(barrier, inc=1, device_id=device, device_id_type=MESH)

    each(1, TM, lambda k: hello({"tm": lax.rem(tm + k, TM)}))
    each(1, GROUP, lambda k: hello(member(lax.rem(mine + k, GROUP))))

    acc[...] = jnp.zeros_like(acc)
    early[...] = jnp.zeros_like(early)
    late[...] = jnp.zeros_like(late)
    last[...] = jnp.zeros_like(last)
    in_grad[...] = jnp.zeros_like(in_grad)

    @pl.when(tm == 0)
    def _():
        level_zero[pl.ds(0, FIRST)] = jnp.zeros((FIRST, 128), jnp.bfloat16)
        level_one[pl.ds(0, SECOND)] = jnp.zeros((SECOND, 128), jnp.bfloat16)

    @pl.when(tm == TM - 1)
    def _():
        far_one[pl.ds(steps, SECOND)] = jnp.zeros((SECOND, 128), jnp.float32)
        far_zero[pl.ds(steps, FIRST)] = jnp.zeros((FIRST, 128), jnp.float32)

    def sum_x(c):
        load_x(c).wait()
        acc[0] += fold(x[at(c * ROWS, ROWS)])

    each(0, chunks, sum_x)
    local_sum = jnp.sum(acc[0], axis=0, keepdims=True)
    local_mean = local_sum / steps

    def sum_squares(c):
        centred = x[at(c * ROWS, ROWS)] - local_mean
        acc[1] += fold(centred * centred)

    each(0, chunks, sum_squares)
    stats[0:1] = local_sum
    stats[1:2] = jnp.sum(acc[1], axis=0, keepdims=True)
    stats_all[pl.ds(tm, 1)] = stats[...][None]

    pl.semaphore_wait(barrier, TM + GROUP - 2)

    def spread_copy(src, dst, s_sem, r_sem, peer, slot):
        return remote(src, dst.at[slot], s_sem.at[peer], r_sem.at[slot], {"tm": peer})

    def stats_copy(peer, slot):
        return spread_copy(stats, stats_all, stats_s, stats_r, peer, slot)

    def ends_copy(peer, slot):
        return spread_copy(ends, ends_all, ends_s, ends_r, peer, slot)

    each(1, TM, lambda k: stats_copy(lax.rem(tm + k, TM), tm).start())

    def take_stats(k):
        peer = lax.rem(tm + k, TM)
        stats_copy(peer, peer).wait()

    each(1, TM, take_stats)

    sums, squares = stats_all[:, 0], stats_all[:, 1]
    mean = jnp.sum(sums, axis=0, keepdims=True) / total_steps
    shift = sums / steps - mean
    variance = (
        jnp.sum(squares, axis=0, keepdims=True)
        + steps * jnp.sum(shift * shift, axis=0, keepdims=True)
    ) / total_steps
    inverse = lax.rsqrt(variance + epsilon)
    spread = jnp.sqrt(variance + epsilon)
    gain, offset = gain_ref[...], offset_ref[...]
    scale = spread / gain

    later, earlier = {"tm": lax.rem(tm + 1, TM)}, {"tm": lax.rem(tm + TM - 1, TM)}
    halo = (
        remote(
            level_zero.at[pl.ds(steps, FIRST)],
            level_zero.at[pl.ds(0, FIRST)],
            halo_s.at[0],
            halo_r.at[0],
            later,
        ),
        remote(
            level_one.at[pl.ds(steps, SECOND)],
            level_one.at[pl.ds(0, SECOND)],
            halo_s.at[1],
            halo_r.at[1],
            later,
        ),
        remote(
            far_one.at[pl.ds(0, SECOND)],
            far_one.at[pl.ds(steps, SECOND)],
            halo_s.at[2],
            halo_r.at[2],
            earlier,
        ),
        remote(
            far_zero.at[pl.ds(0, FIRST)],
            far_zero.at[pl.ds(steps, FIRST)],
            halo_s.at[3],
            halo_r.at[3],
            earlier,
        ),
    )

    def normalize(c):
        hat_x = (x[at(c * ROWS, ROWS)] - mean) * inverse
        return hat_x, (hat_x * gain + offset).astype(jnp.bfloat16)

    def project(i):
        c = chunks - 1 - i
        _, normed = normalize(c)
        level_zero[at(FIRST + c * ROWS, ROWS)] = nn(normed, w_in[...]).astype(jnp.bfloat16)

        @pl.when(jnp.logical_and(i == 0, tm < TM - 1))
        def _():
            halo[0].start()

    each(0, chunks, project)

    def gates(act):
        return jnp.tanh(act[:, :128]), 0.5 * jnp.tanh(0.5 * act[:, 128:]) + 0.5

    def window_zero(c):
        return jnp.concatenate(
            [level_zero[at(c * ROWS, ROWS)], level_zero[at(c * ROWS + FIRST, ROWS)]], axis=1
        )

    def window_one(c):
        return jnp.concatenate(
            [level_one[at(c * ROWS, ROWS)], level_one[at(c * ROWS + SECOND, ROWS)]], axis=1
        )

    def layer_one(i):
        c = chunks - 1 - i

        @pl.when(jnp.logical_and(c == 0, tm > 0))
        def _():
            halo[0].wait_recv()

        now = at(c * ROWS, ROWS)
        tanh, sigm = gates(nn(window_zero(c), w_conv[0]) + bias[0:1])
        gated = (tanh * sigm).astype(jnp.bfloat16)
        tanh_one[now] = tanh
        sigm_one[now] = sigm
        gated_one[now] = gated
        level = level_zero[at(c * ROWS + FIRST, ROWS)].astype(jnp.float32)
        level_one[at(c * ROWS + SECOND, ROWS)] = (level + nn(gated, w_res[...])).astype(
            jnp.bfloat16
        )

        @pl.when(jnp.logical_and(i == 0, tm < TM - 1))
        def _():
            halo[1].start()

    each(0, chunks, layer_one)

    def gate_back(incoming, tanh, sigm):
        part = incoming * sigm
        return part * (1.0 - tanh * tanh), part * tanh * (1.0 - sigm)

    load_cot.wait()

    @pl.when(tm > 0)
    def _():
        halo[1].wait_recv()

    def layer_two(c):
        now = at(c * ROWS, ROWS)
        window = window_one(c)
        tanh, sigm = gates(nn(window, w_conv[1]) + bias[1:2])
        gated = (tanh * sigm).astype(jnp.bfloat16)
        both = jnp.concatenate([gated_one[now], gated], axis=1)
        skip = nn(both, w_skip[...])
        square = skip * skip
        half = 0.5 * jnp.tanh(
            skip * (gelu_coeff + (gelu_coeff * cubic_coeff) * square)
        ) + 0.5
        value = skip * half
        slope = half + value * (1.0 - half) * (
            2.0 * gelu_coeff + (6.0 * gelu_coeff * cubic_coeff) * square
        )
        rectified = value.astype(jnp.bfloat16)
        forecast = nn(rectified, w_out[...])
        gradient = cot[now]
        acc[2] += fold(gradient)
        acc[3] += fold(gradient * (forecast - offset))
        scaled = (gradient * scale).astype(jnp.bfloat16)
        out_part = tn(rectified, scaled)
        early[1024:1152] += out_part[:128]
        late[640:768] += out_part[128:]
        back_skip = (nt(scaled, w_out[...]) * slope).astype(jnp.bfloat16)
        skip_part = tn(both, back_skip)
        early[512:768] += skip_part[:, :128]
        early[768:1024] += skip_part[:, 128:]
        incoming = nt(back_skip, w_skip[...])
        incoming_one[now] = incoming[:, :128]
        first, second = gate_back(incoming[:, 128:], tanh, sigm)
        acc[4] += fold(first)
        acc[5] += fold(second)
        pre = jnp.concatenate([first, second], axis=1).astype(jnp.bfloat16)
        conv_part = tn(window, pre)
        early[0:256] += conv_part[:, :128]
        early[256:512] += conv_part[:, 128:]
        carried = nt(pre, w_conv[1])
        far_one[now] = carried[:, :128]
        near_one[now] = carried[:, 128:]

        @pl.when(jnp.logical_and(c == 0, tm > 0))
        def _():
            halo[2].start()

    each(0, chunks, layer_two)

    def one(g, src, dst, size, peer, slot):
        return remote(
            src.at[at(peer * size, size)],
            dst.at[slot],
            one_s.at[g, peer],
            one_r.at[g, slot],
            member(peer),
        )

    def two(g, src, dst, peer, slot):
        return remote(
            src, dst.at[slot], two_s.at[g, peer], two_r.at[g, slot], {"tm": place * Z + peer}
        )

    def three(g, out, size, peer, slot):
        where = out.at[at(slot * size, size)]
        return remote(where, where, three_s.at[g, peer], three_r.at[g, slot], member(peer))

    groups = (
        (early, early_one, early_block, early_two, early_out, EARLY),
        (late, late_one, late_block, late_two, late_out, LATE),
        (last, last_one, last_block, last_two, last_out, LAST),
    )

    def scatter(g):
        src, dst, block, _, _, size = groups[g]
        each(1, GROUP, lambda k: one(g, src, dst, size, lax.rem(mine + k, GROUP), mine).start())
        dst[pl.ds(mine, 1)] = src[at(mine * size, size)][None]

    def middle(g):
        src, dst, block, far, _, size = groups[g]

        def take(k):
            peer = lax.rem(mine + k, GROUP)
            one(g, src, dst, size, peer, peer).wait()

        each(1, GROUP, take)
        total = dst[0]
        for p in range(1, GROUP):
            total = total + dst[p]
        block[...] = total
        each(1, Z, lambda k: two(g, block, far, lax.rem(depth + k, Z), depth).start())
        far[pl.ds(depth, 1)] = total[None]

    def gather(g):
        _, _, block, far, out, size = groups[g]

        def take(k):
            peer = lax.rem(depth + k, Z)
            two(g, block, far, peer, peer).wait()

        each(1, Z, take)
        total = far[0]
        for z in range(1, Z):
            total = total + far[z]
        out[at(mine * size, size)] = total
        each(1, GROUP, lambda k: three(g, out, size, lax.rem(mine + k, GROUP), mine).start())

    def finish(g):
        _, _, _, _, out, size = groups[g]

        def take(k):
            peer = lax.rem(mine + k, GROUP)
            three(g, out, size, peer, mine).wait_send()
            three(g, out, size, peer, peer).wait_recv()

        each(1, GROUP, take)

    scatter(0)

    def back_one(c):
        @pl.when(jnp.logical_and(c == chunks - 1, tm < TM - 1))
        def _():
            halo[2].wait_recv()

        now = at(c * ROWS, ROWS)
        arrived = near_one[now] + far_one[at(c * ROWS + SECOND, ROWS)]
        grad_one = arrived.astype(jnp.bfloat16)
        late[512:640] += tn(gated_one[now], grad_one)
        incoming = incoming_one[now] + nt(grad_one, w_res[...])
        first, second = gate_back(incoming, tanh_one[now], sigm_one[now])
        acc[6] += fold(first)
        acc[7] += fold(second)
        pre = jnp.concatenate([first, second], axis=1).astype(jnp.bfloat16)
        conv_part = tn(window_zero(c), pre)
        late[0:256] += conv_part[:, :128]
        late[256:512] += conv_part[:, 128:]
        carried = nt(pre, w_conv[0])
        far_zero[now] = carried[:, :128]
        near_zero[now] = grad_one.astype(jnp.float32) + carried[:, 128:]

        @pl.when(jnp.logical_and(c == 0, tm > 0))
        def _():
            halo[3].start()

    each(0, chunks, back_one)
    scatter(1)
    middle(0)

    def back_zero(c):
        @pl.when(jnp.logical_and(c == chunks - 1, tm < TM - 1))
        def _():
            halo[3].wait_recv()

        now = at(c * ROWS, ROWS)
        grad_zero = (near_zero[now] + far_zero[at(c * ROWS + FIRST, ROWS)]).astype(jnp.bfloat16)
        hat_x, normed = normalize(c)
        in_grad[...] += tn(normed, grad_zero)
        grad_hat = nt(grad_zero, w_in[...]) * gain
        hat[now] = grad_hat
        acc[8] += fold(grad_hat)
        acc[9] += fold(grad_hat * hat_x)

    each(0, chunks, back_zero)

    def column(k):
        return jnp.sum(acc[k], axis=0, keepdims=True)

    sum_a, sum_b, out_a, out_b = column(8), column(9), column(2), column(3) / gain
    ends[0:1] = sum_a
    ends[1:2] = sum_b
    ends[2:3] = out_a
    ends[3:4] = out_b
    each(1, TM, lambda k: ends_copy(lax.rem(tm + k, TM), tm).start())
    ends_all[pl.ds(tm, 1)] = ends[...][None]
    for p in range(GROUP):
        last[8 * p : 8 * p + 4] = in_grad[4 * p : 4 * p + 4]
    last[4:5] = (sum_b - out_b * spread) / gain
    last[12:13] = (sum_a - out_a * spread) / gain
    last[20:21] = column(6)
    last[28:29] = column(7)
    last[36:37] = column(4)
    last[44:45] = column(5)
    scatter(2)
    gather(0)
    middle(1)

    def take_ends(k):
        peer = lax.rem(tm + k, TM)
        ends_copy(peer, peer).wait()

    each(1, TM, take_ends)
    totals = jnp.sum(ends_all[...], axis=0) / total_steps
    slant = inverse * (totals[3:4] - inverse * totals[1:2])
    level = totals[2:3] - inverse * totals[0:1]
    middle(2)

    def store(c):
        return pltpu.make_async_copy(
            hat.at[at(c * ROWS, ROWS)], grad_hbm.at[at(c * ROWS, ROWS)], store_sem.at[c]
        )

    def resolve(c):
        now = at(c * ROWS, ROWS)
        hat[now] = hat[now] * inverse + ((x[now] - mean) * slant + level)
        store(c).start()

    each(0, chunks, resolve)
    gather(1)
    gather(2)

    @pl.when(tm < TM - 1)
    def _():
        halo[0].wait_send()
        halo[1].wait_send()

    @pl.when(tm > 0)
    def _():
        halo[2].wait_send()
        halo[3].wait_send()

    each(0, chunks, lambda c: store(c).wait())
    finish(0)
    finish(1)
    finish(2)


def unpack_kernel(early, late, last, conv, bias, res, skip, out, into, gain, shift):
    for layer, src in ((0, late), (1, early)):
        for tap in range(2):
            for half in range(2):
                conv[layer, tap, :, half * 128 : half * 128 + 128] = src[
                    pl.ds(half * 256 + tap * 128, 128)
                ]
    for layer in range(2):
        for half in range(2):
            skip[layer, :, half * 128 : half * 128 + 128] = early[
                pl.ds(512 + half * 256 + layer * 128, 128)
            ]
            bias[layer : layer + 1, half * 128 : half * 128 + 128] = last[
                pl.ds(20 + layer * 16 + half * 8, 1)
            ]
    out[0:128] = early[1024:1152]
    out[128:256] = late[640:768]
    res[...] = late[512:640]
    for p in range(GROUP):
        into[4 * p : 4 * p + 4] = last[8 * p : 8 * p + 4]
    gain[...] = last[4:5]
    shift[...] = last[12:13]


def on_device(
    series_data,
    cotangent,
    in_weight,
    convolution_weight,
    convolution_bias,
    res_weight,
    skip_weight,
    output_weight,
    norm_gain_vector,
    norm_offset_vector,
):
    steps = series_data.shape[1]
    f32, bf16 = jnp.float32, jnp.bfloat16
    vmem = pl.BlockSpec(memory_space=pltpu.VMEM)
    hbm = pl.BlockSpec(memory_space=pl.ANY)
    sem = pltpu.SemaphoreType.DMA
    shape = jax.ShapeDtypeStruct
    field = pltpu.VMEM((steps, 128), f32)

    def sizes(lead):
        return [pltpu.VMEM((lead, size, 128), f32) for size in (EARLY, LATE, LAST)]

    grad, early, late, last = pl.pallas_call(
        block_kernel,
        name="block",
        out_shape=(
            shape((steps, 128), f32),
            shape((GROUP * EARLY, 128), f32),
            shape((GROUP * LATE, 128), f32),
            shape((GROUP * LAST, 128), f32),
        ),
        in_specs=[hbm, hbm] + [vmem] * 8,
        out_specs=(hbm, vmem, vmem, vmem),
        scratch_shapes=[
            field,
            field,
            pltpu.VMEM((steps + FIRST, 128), bf16),
            pltpu.VMEM((steps + SECOND, 128), bf16),
            pltpu.VMEM((steps, 128), bf16),
            field,
            field,
            field,
            field,
            pltpu.VMEM((steps + SECOND, 128), f32),
            field,
            pltpu.VMEM((steps + FIRST, 128), f32),
            field,
            pltpu.VMEM((GROUP * EARLY, 128), f32),
            pltpu.VMEM((GROUP * LATE, 128), f32),
            pltpu.VMEM((GROUP * LAST, 128), f32),
            pltpu.VMEM((128, 128), f32),
            pltpu.VMEM((10, 8, 128), f32),
            pltpu.VMEM((2, 128), f32),
            pltpu.VMEM((TM, 2, 128), f32),
            pltpu.VMEM((4, 128), f32),
            pltpu.VMEM((TM, 4, 128), f32),
            *sizes(GROUP),
            *sizes(Z),
            pltpu.VMEM((EARLY, 128), f32),
            pltpu.VMEM((LATE, 128), f32),
            pltpu.VMEM((LAST, 128), f32),
            sem((steps // ROWS + 1,)),
            sem((steps // ROWS,)),
            sem((4,)),
            sem((4,)),
            sem((TM,)),
            sem((TM,)),
            sem((TM,)),
            sem((TM,)),
            sem((3, GROUP)),
            sem((3, GROUP)),
            sem((3, Z)),
            sem((3, Z)),
            sem((3, GROUP)),
            sem((3, GROUP)),
        ],
        compiler_params=pltpu.CompilerParams(
            collective_id=0, has_side_effects=True, vmem_limit_bytes=60 * 1024 * 1024
        ),
    )(
        series_data[0],
        cotangent[0],
        in_weight,
        convolution_weight.reshape(2, 256, 256),
        convolution_bias,
        res_weight,
        skip_weight.reshape(256, 256),
        output_weight,
        norm_gain_vector.reshape(1, 128),
        norm_offset_vector.reshape(1, 128),
    )
    conv, bias, res, skip, out, into, gain, shift = pl.pallas_call(
        unpack_kernel,
        name="unpack",
        out_shape=(
            shape((2, 2, 128, 256), f32),
            shape((2, 256), f32),
            shape((128, 128), f32),
            shape((2, 128, 256), f32),
            shape((256, 128), f32),
            shape((128, 128), f32),
            shape((1, 128), f32),
            shape((1, 128), f32),
        ),
        in_specs=[vmem] * 3,
        out_specs=(vmem,) * 8,
    )(early, late, last)
    return grad[None], conv, bias, res, skip, out, into, gain.reshape(128), shift.reshape(128)


def solution(mesh):
    split = P("series", "tm", None)
    return jax.shard_map(
        on_device,
        mesh=mesh,
        in_specs=(split, split) + (P(),) * 8,
        out_specs=(split,) + (P(),) * 8,
        check_vma=False,
    )
```

```python
import jax
import jax.numpy as jnp
from jax import lax
from jax.experimental import pallas as pl
from jax.experimental.pallas import tpu as pltpu
from jax.sharding import PartitionSpec as P

FIRST = 256
SECOND = 512
TM = 32
SER = 8
X = 4
Z = 8
Y = 4
PLANE = X * Y
PARTS = 2 * PLANE
ROWS = 512
MESH = pl.DeviceIdType.MESH
EARLY, LATE, LAST = 40, 24, 8

epsilon = 1e-05
gelu_coeff = 0.7978845608
cubic_coeff = 0.044715


def nn(left, right):
    return jnp.dot(left, right, preferred_element_type=jnp.float32)


def nt(left, right):
    return lax.dot_general(
        left, right, (((1,), (1,)), ((), ())), preferred_element_type=jnp.float32
    )


def tn(left, right):
    return lax.dot_general(
        left, right, (((0,), (0,)), ((), ())), preferred_element_type=jnp.float32
    )


def fold(values):
    return jnp.sum(values.reshape(-1, 8, values.shape[-1]), axis=0)


def each(lo, hi, body):
    def run(k, carry):
        body(k)
        return carry

    lax.fori_loop(lo, hi, run, 0)


def at(start, size):
    return pl.ds(pl.multiple_of(start, 8), size)


def remote(src, dst, s_sem, r_sem, device):
    return pltpu.make_async_remote_copy(
        src_ref=src,
        dst_ref=dst,
        send_sem=s_sem,
        recv_sem=r_sem,
        device_id=device,
        device_id_type=MESH,
    )


def block_kernel(
    x_hbm,
    cot_hbm,
    w_in_hbm,
    w_conv_hbm,
    bias_hbm,
    w_res_hbm,
    w_skip_hbm,
    w_out_hbm,
    gain_hbm,
    offset_hbm,
    hat,
    early_out,
    late_out,
    last_out,
    w_in,
    w_conv,
    bias,
    w_res,
    w_skip,
    w_out,
    gain_ref,
    offset_ref,
    x,
    cot,
    level_zero,
    level_one,
    gated_one,
    tanh_one,
    sigm_one,
    incoming_one,
    near_one,
    far_one,
    near_zero,
    far_zero,
    early,
    late,
    last,
    in_grad,
    acc,
    stats,
    stats_z,
    stats_x,
    ends,
    ends_z,
    ends_x,
    early_pair,
    late_pair,
    last_pair,
    early_half,
    late_half,
    last_half,
    early_one,
    late_one,
    last_one,
    early_two,
    late_two,
    last_two,
    early_block,
    late_block,
    last_block,
    load_sem,
    halo_s,
    halo_r,
    line_s,
    line_r,
    pair_s,
    pair_r,
    one_s,
    one_r,
    two_s,
    two_r,
    three_s,
    three_r,
    back_s,
    back_r,
):
    steps = x.shape[0]
    chunks = steps // ROWS
    total_steps = float(steps * TM)
    ser = lax.axis_index("series")
    tm = lax.axis_index("tm")
    across, depth = tm // Z, lax.rem(tm, Z)
    up, core = ser // 2, lax.rem(ser, 2)
    mine = across * Y + up
    mate = {"series": ser + 1 - 2 * core}

    def on_z(peer):
        return {"tm": across * Z + peer}

    def on_x(peer):
        return {"tm": peer * Z + depth}

    def on_plane(peer):
        return {"series": lax.rem(peer, Y) * 2 + core, "tm": (peer // Y) * Z + depth}

    def load_x(c):
        return pltpu.make_async_copy(
            x_hbm.at[at(c * ROWS, ROWS)], x.at[at(c * ROWS, ROWS)], load_sem.at[c]
        )

    load_cot = pltpu.make_async_copy(cot_hbm, cot, load_sem.at[chunks])
    each(0, chunks, lambda c: load_x(c).start())
    load_cot.start()
    params = [
        pltpu.make_async_copy(src, dst, load_sem.at[chunks + 1 + k])
        for k, (src, dst) in enumerate(
            (
                (w_in_hbm, w_in),
                (w_conv_hbm, w_conv),
                (bias_hbm, bias),
                (w_res_hbm, w_res),
                (w_skip_hbm, w_skip),
                (w_out_hbm, w_out),
                (gain_hbm, gain_ref),
                (offset_hbm, offset_ref),
            )
        )
    ]
    for copy in params:
        copy.start()

    barrier = pltpu.get_barrier_semaphore()

    def hello(device):
        pl.semaphore_signal(barrier, inc=1, device_id=device, device_id_type=MESH)

    for k in range(1, Z):
        hello(on_z(lax.rem(depth + k, Z)))
    for k in range(1, X):
        hello(on_x(lax.rem(across + k, X)))
    for k in range(1, Y):
        hello({"series": lax.rem(up + k, Y) * 2 + core})
    hello(mate)

    acc[...] = jnp.zeros_like(acc)
    early[...] = jnp.zeros_like(early)
    late[...] = jnp.zeros_like(late)
    last[...] = jnp.zeros_like(last)
    in_grad[...] = jnp.zeros_like(in_grad)

    @pl.when(tm == 0)
    def _():
        level_zero[pl.ds(0, FIRST)] = jnp.zeros((FIRST, 128), jnp.bfloat16)
        level_one[pl.ds(0, SECOND)] = jnp.zeros((SECOND, 128), jnp.bfloat16)

    @pl.when(tm == TM - 1)
    def _():
        far_one[pl.ds(steps, SECOND)] = jnp.zeros((SECOND, 128), jnp.float32)
        far_zero[pl.ds(steps, FIRST)] = jnp.zeros((FIRST, 128), jnp.float32)

    def sum_x(c):
        load_x(c).wait()
        acc[0] += fold(x[at(c * ROWS, ROWS)])

    each(0, chunks, sum_x)
    local_sum = jnp.sum(acc[0], axis=0, keepdims=True)
    local_mean = local_sum / steps

    def sum_squares(c):
        centred = x[at(c * ROWS, ROWS)] - local_mean
        acc[1] += fold(centred * centred)

    each(0, chunks, sum_squares)
    stats[0:1] = local_sum
    stats[1:2] = jnp.sum(acc[1], axis=0, keepdims=True)
    pl.semaphore_wait(barrier, Z + X + Y - 2)

    def line(which, own, slots, count, me, device):
        def copy(peer, slot):
            return remote(own, slots.at[slot], line_s.at[which], line_r.at[which], device(peer))

        rest = slots.at[pl.ds(0, count - 1)]
        whole = remote(rest, rest, line_s.at[which], line_r.at[which], device(me))
        for k in range(1, count):
            copy(lax.rem(me + k, count), me).start()
        slots[pl.ds(me, 1)] = own[...][None]
        return whole

    def combine(slots, count):
        sums = slots[:, 0]
        total = jnp.sum(sums, axis=0, keepdims=True)
        shift = sums / count - total / (count * slots.shape[0])
        squares = slots[:, 1] + count * (shift * shift)
        return total, jnp.sum(squares, axis=0, keepdims=True)

    line(0, stats, stats_z, Z, depth, on_z).wait()
    total, squares = combine(stats_z, float(steps))
    stats[0:1] = total
    stats[1:2] = squares
    line(1, stats, stats_x, X, across, on_x).wait()
    total, squares = combine(stats_x, float(steps * Z))
    mean = total / total_steps
    variance = squares / total_steps
    inverse = lax.rsqrt(variance + epsilon)
    spread = jnp.sqrt(variance + epsilon)
    for copy in params:
        copy.wait()
    gain, offset = gain_ref[...], offset_ref[...]
    scale = spread / gain

    later, earlier = {"tm": lax.rem(tm + 1, TM)}, {"tm": lax.rem(tm + TM - 1, TM)}
    halo = (
        remote(
            level_zero.at[pl.ds(steps, FIRST)],
            level_zero.at[pl.ds(0, FIRST)],
            halo_s.at[0],
            halo_r.at[0],
            later,
        ),
        remote(
            level_one.at[pl.ds(steps, SECOND)],
            level_one.at[pl.ds(0, SECOND)],
            halo_s.at[1],
            halo_r.at[1],
            later,
        ),
        remote(
            far_one.at[pl.ds(0, SECOND)],
            far_one.at[pl.ds(steps, SECOND)],
            halo_s.at[2],
            halo_r.at[2],
            earlier,
        ),
        remote(
            far_zero.at[pl.ds(0, FIRST)],
            far_zero.at[pl.ds(steps, FIRST)],
            halo_s.at[3],
            halo_r.at[3],
            earlier,
        ),
    )

    def normalize(c):
        hat_x = (x[at(c * ROWS, ROWS)] - mean) * inverse
        return hat_x, (hat_x * gain + offset).astype(jnp.bfloat16)

    def project(i):
        c = chunks - 1 - i
        _, normed = normalize(c)
        level_zero[at(FIRST + c * ROWS, ROWS)] = nn(normed, w_in[...]).astype(jnp.bfloat16)

        @pl.when(jnp.logical_and(i == 0, tm < TM - 1))
        def _():
            halo[0].start()

    each(0, chunks, project)

    def gates(act):
        return jnp.tanh(act[:, :128]), 0.5 * jnp.tanh(0.5 * act[:, 128:]) + 0.5

    def window_zero(c):
        return jnp.concatenate(
            [level_zero[at(c * ROWS, ROWS)], level_zero[at(c * ROWS + FIRST, ROWS)]], axis=1
        )

    def window_one(c):
        return jnp.concatenate(
            [level_one[at(c * ROWS, ROWS)], level_one[at(c * ROWS + SECOND, ROWS)]], axis=1
        )

    def layer_one(i):
        c = chunks - 1 - i

        @pl.when(jnp.logical_and(c == 0, tm > 0))
        def _():
            halo[0].wait_recv()

        now = at(c * ROWS, ROWS)
        tanh, sigm = gates(nn(window_zero(c), w_conv[0]) + bias[0:1])
        gated = (tanh * sigm).astype(jnp.bfloat16)
        tanh_one[now] = tanh
        sigm_one[now] = sigm
        gated_one[now] = gated
        level = level_zero[at(c * ROWS + FIRST, ROWS)].astype(jnp.float32)
        level_one[at(c * ROWS + SECOND, ROWS)] = (level + nn(gated, w_res[...])).astype(
            jnp.bfloat16
        )

        @pl.when(jnp.logical_and(i == 0, tm < TM - 1))
        def _():
            halo[1].start()

    each(0, chunks, layer_one)

    def gate_back(incoming, tanh, sigm):
        part = incoming * sigm
        return part * (1.0 - tanh * tanh), part * tanh * (1.0 - sigm)

    load_cot.wait()

    @pl.when(tm > 0)
    def _():
        halo[1].wait_recv()

    def layer_two(c):
        now = at(c * ROWS, ROWS)
        window = window_one(c)
        tanh, sigm = gates(nn(window, w_conv[1]) + bias[1:2])
        gated = (tanh * sigm).astype(jnp.bfloat16)
        both = jnp.concatenate([gated_one[now], gated], axis=1)
        skip = nn(both, w_skip[...])
        square = skip * skip
        half = 0.5 * jnp.tanh(
            skip * (gelu_coeff + (gelu_coeff * cubic_coeff) * square)
        ) + 0.5
        value = skip * half
        slope = half + value * (1.0 - half) * (
            2.0 * gelu_coeff + (6.0 * gelu_coeff * cubic_coeff) * square
        )
        rectified = value.astype(jnp.bfloat16)
        forecast = nn(rectified, w_out[...])
        gradient = cot[now]
        acc[2] += fold(gradient)
        acc[3] += fold(gradient * (forecast - offset))
        scaled = (gradient * scale).astype(jnp.bfloat16)
        out_part = tn(rectified, scaled)
        early[1024:1152] += out_part[:128]
        late[640:768] += out_part[128:]
        back_skip = (nt(scaled, w_out[...]) * slope).astype(jnp.bfloat16)
        skip_part = tn(both, back_skip)
        early[512:768] += skip_part[:, :128]
        early[768:1024] += skip_part[:, 128:]
        incoming = nt(back_skip, w_skip[...])
        incoming_one[now] = incoming[:, :128]
        first, second = gate_back(incoming[:, 128:], tanh, sigm)
        acc[4] += fold(first)
        acc[5] += fold(second)
        pre = jnp.concatenate([first, second], axis=1).astype(jnp.bfloat16)
        conv_part = tn(window, pre)
        early[0:256] += conv_part[:, :128]
        early[256:512] += conv_part[:, 128:]
        carried = nt(pre, w_conv[1])
        far_one[now] = carried[:, :128]
        near_one[now] = carried[:, 128:]

        @pl.when(jnp.logical_and(c == 0, tm > 0))
        def _():
            halo[2].start()

    each(0, chunks, layer_two)

    groups = (
        (early, early_pair, early_half, early_one, early_block, early_two, early_out, EARLY),
        (late, late_pair, late_half, late_one, late_block, late_two, late_out, LATE),
        (last, last_pair, last_half, last_one, last_block, last_two, last_out, LAST),
    )

    def pair(g):
        src, got, size = groups[g][0], groups[g][1], groups[g][7] * PLANE
        return remote(
            src.at[at((1 - core) * size, size)], got, pair_s.at[g], pair_r.at[g], mate
        )

    def one(g, k):
        half, got, size = groups[g][2], groups[g][3], groups[g][7]
        peer = lax.rem(mine + k, PLANE)
        return remote(
            half.at[at(peer * size, size)], got.at[k], one_s.at[g], one_r.at[g], on_plane(peer)
        )

    def two(g, k):
        block, got = groups[g][4], groups[g][5]
        peer = lax.rem(depth + k, Z)
        return remote(block, got.at[depth], two_s.at[g], two_r.at[g], on_z(peer))

    def three(g, k):
        out, size = groups[g][6], groups[g][7]
        where = out.at[at((core * PLANE + mine) * size, size)]
        peer = lax.rem(mine + k, PLANE)
        return remote(where, where, three_s.at[g], three_r.at[g], on_plane(peer))

    def back(g):
        out, size = groups[g][6], groups[g][7] * PLANE
        where = out.at[at(core * size, size)]
        return remote(where, where, back_s.at[g], back_r.at[g], mate)

    def whole(g, ref, count, s_sem, r_sem):
        rest = ref.at[pl.ds(0, count)]
        return remote(rest, rest, s_sem.at[g], r_sem.at[g], mate)

    def all_one(g):
        return whole(g, groups[g][3], PLANE - 1, one_s, one_r)

    def all_two(g):
        return whole(g, groups[g][5], Z - 1, two_s, two_r)

    def all_three(g):
        return whole(g, groups[g][6], (PLANE - 1) * groups[g][7], three_s, three_r)

    def start(g):
        pair(g).start()

    def scatter(g):
        src, got, half, slots, _, _, _, size = groups[g]
        pair(g).wait_recv()
        half[...] = src[at(core * PLANE * size, PLANE * size)] + got[...]
        each(1, PLANE, lambda k: one(g, k).start())

    def middle(g):
        _, _, half, slots, block, far, _, size = groups[g]
        all_one(g).wait_recv()
        total = half[at(mine * size, size)]
        for p in range(1, PLANE):
            total = total + slots[p]
        block[...] = total
        each(1, Z, lambda k: two(g, k).start())
        far[pl.ds(depth, 1)] = total[None]

    def gather(g):
        _, _, _, _, _, far, out, size = groups[g]
        all_two(g).wait_recv()
        total = far[0]
        for z in range(1, Z):
            total = total + far[z]
        out[at((core * PLANE + mine) * size, size)] = total
        each(1, PLANE, lambda k: three(g, k).start())

    def share(g):
        all_three(g).wait_recv()
        back(g).start()

    def finish(g):
        back(g).wait_recv()
        pair(g).wait_send()
        all_one(g).wait_send()
        all_two(g).wait_send()
        all_three(g).wait_send()
        back(g).wait_send()

    start(0)

    def back_one(c):
        @pl.when(jnp.logical_and(c == chunks - 1, tm < TM - 1))
        def _():
            halo[2].wait_recv()

        now = at(c * ROWS, ROWS)
        arrived = near_one[now] + far_one[at(c * ROWS + SECOND, ROWS)]
        grad_one = arrived.astype(jnp.bfloat16)
        late[512:640] += tn(gated_one[now], grad_one)
        incoming = incoming_one[now] + nt(grad_one, w_res[...])
        first, second = gate_back(incoming, tanh_one[now], sigm_one[now])
        acc[6] += fold(first)
        acc[7] += fold(second)
        pre = jnp.concatenate([first, second], axis=1).astype(jnp.bfloat16)
        conv_part = tn(window_zero(c), pre)
        late[0:256] += conv_part[:, :128]
        late[256:512] += conv_part[:, 128:]
        carried = nt(pre, w_conv[0])
        far_zero[now] = carried[:, :128]
        near_zero[now] = grad_one.astype(jnp.float32) + carried[:, 128:]

        @pl.when(jnp.logical_and(c == 0, tm > 0))
        def _():
            halo[3].start()

    each(0, chunks, back_one)
    start(1)
    scatter(0)

    def back_zero(c):
        @pl.when(jnp.logical_and(c == chunks - 1, tm < TM - 1))
        def _():
            halo[3].wait_recv()

        now = at(c * ROWS, ROWS)
        grad_zero = (near_zero[now] + far_zero[at(c * ROWS + FIRST, ROWS)]).astype(jnp.bfloat16)
        hat_x, normed = normalize(c)
        in_grad[...] += tn(normed, grad_zero)
        grad_hat = nt(grad_zero, w_in[...]) * gain
        hat[now] = grad_hat
        acc[8] += fold(grad_hat)
        acc[9] += fold(grad_hat * hat_x)

    each(0, chunks, back_zero)

    def column(k):
        return jnp.sum(acc[k], axis=0, keepdims=True)

    sum_a, sum_b, out_a, out_b = column(8), column(9), column(2), column(3) / gain
    ends[0:1] = sum_a
    ends[1:2] = sum_b
    ends[2:3] = out_a
    ends[3:4] = out_b
    ends_line = line(2, ends, ends_z, Z, depth, on_z)
    for p in range(PARTS):
        last[8 * p : 8 * p + 4] = in_grad[4 * p : 4 * p + 4]
    last[4:5] = (sum_b - out_b * spread) / gain
    last[12:13] = (sum_a - out_a * spread) / gain
    last[20:21] = column(6)
    last[28:29] = column(7)
    last[36:37] = column(4)
    last[44:45] = column(5)
    start(2)
    scatter(1)
    middle(0)
    scatter(2)
    ends_line.wait()
    ends[...] = jnp.sum(ends_z[...], axis=0)
    ends_line = line(3, ends, ends_x, X, across, on_x)
    middle(1)
    gather(0)
    middle(2)
    ends_line.wait()
    totals = jnp.sum(ends_x[...], axis=0) / total_steps
    slant = inverse * (totals[3:4] - inverse * totals[1:2])
    level = totals[2:3] - inverse * totals[0:1]
    def resolve(c):
        now = at(c * ROWS, ROWS)
        hat[now] = hat[now] * inverse + ((x[now] - mean) * slant + level)

    each(0, chunks, resolve)
    gather(1)
    share(0)
    gather(2)
    share(1)
    share(2)

    @pl.when(tm < TM - 1)
    def _():
        halo[0].wait_send()
        halo[1].wait_send()

    @pl.when(tm > 0)
    def _():
        halo[2].wait_send()
        halo[3].wait_send()

    finish(0)
    finish(1)
    finish(2)


def unpack_kernel(
    hat, early, late, last, grad, conv, bias, res, skip, out, into, gain, shift, store_sem
):
    store = pltpu.make_async_copy(hat, grad, store_sem)
    store.start()
    for layer, src in ((0, late), (1, early)):
        for tap in range(2):
            for half in range(2):
                conv[layer, tap, :, half * 128 : half * 128 + 128] = src[
                    pl.ds(half * 256 + tap * 128, 128)
                ]
    for layer in range(2):
        for half in range(2):
            skip[layer, :, half * 128 : half * 128 + 128] = early[
                pl.ds(512 + half * 256 + layer * 128, 128)
            ]
            bias[layer : layer + 1, half * 128 : half * 128 + 128] = last[
                pl.ds(20 + layer * 16 + half * 8, 1)
            ]
    out[0:128] = early[1024:1152]
    out[128:256] = late[640:768]
    res[...] = late[512:640]
    for p in range(PARTS):
        into[4 * p : 4 * p + 4] = last[8 * p : 8 * p + 4]
    gain[...] = last[4:5]
    shift[...] = last[12:13]
    store.wait()


def on_device(
    series_data,
    cotangent,
    in_weight,
    convolution_weight,
    convolution_bias,
    res_weight,
    skip_weight,
    output_weight,
    norm_gain_vector,
    norm_offset_vector,
):
    steps = series_data.shape[1]
    f32, bf16 = jnp.float32, jnp.bfloat16
    vmem = pl.BlockSpec(memory_space=pltpu.VMEM)
    hbm = pl.BlockSpec(memory_space=pltpu.HBM)
    sem = pltpu.SemaphoreType.DMA
    shape = jax.ShapeDtypeStruct
    field = pltpu.VMEM((steps, 128), f32)

    sizes = (EARLY, LATE, LAST)

    def slots(lead):
        return [pltpu.VMEM((lead, size, 128), f32) for size in sizes]

    def blocks(count):
        return [pltpu.VMEM((count * size, 128), f32) for size in sizes]

    hat, early, late, last = pl.pallas_call(
        block_kernel,
        name="block",
        out_shape=(
            pltpu.VMEM((steps, 128), f32),
            pltpu.VMEM((PARTS * EARLY, 128), f32),
            pltpu.VMEM((PARTS * LATE, 128), f32),
            pltpu.VMEM((PARTS * LAST, 128), f32),
        ),
        in_specs=[hbm] * 10,
        out_specs=(vmem,) * 4,
        scratch_shapes=[
            pltpu.VMEM((128, 128), bf16),
            pltpu.VMEM((2, 256, 256), bf16),
            pltpu.VMEM((2, 256), f32),
            pltpu.VMEM((128, 128), bf16),
            pltpu.VMEM((256, 256), bf16),
            pltpu.VMEM((256, 128), bf16),
            pltpu.VMEM((1, 128), f32),
            pltpu.VMEM((1, 128), f32),
            field,
            field,
            pltpu.VMEM((steps + FIRST, 128), bf16),
            pltpu.VMEM((steps + SECOND, 128), bf16),
            pltpu.VMEM((steps, 128), bf16),
            field,
            field,
            field,
            field,
            pltpu.VMEM((steps + SECOND, 128), f32),
            field,
            pltpu.VMEM((steps + FIRST, 128), f32),
            *blocks(PARTS),
            pltpu.VMEM((128, 128), f32),
            pltpu.VMEM((10, 8, 128), f32),
            pltpu.VMEM((2, 128), f32),
            pltpu.VMEM((Z, 2, 128), f32),
            pltpu.VMEM((X, 2, 128), f32),
            pltpu.VMEM((4, 128), f32),
            pltpu.VMEM((Z, 4, 128), f32),
            pltpu.VMEM((X, 4, 128), f32),
            *blocks(PLANE),
            *blocks(PLANE),
            *slots(PLANE),
            *slots(Z),
            *blocks(1),
            sem((steps // ROWS + 9,)),
            sem((4,)),
            sem((4,)),
            sem((4,)),
            sem((4,)),
            *[sem((3,))] * 10,
        ],
        compiler_params=pltpu.CompilerParams(
            collective_id=0, has_side_effects=True, vmem_limit_bytes=56 * 1024 * 1024
        ),
    )(
        series_data[0],
        cotangent[0],
        in_weight,
        convolution_weight.reshape(2, 256, 256),
        convolution_bias,
        res_weight,
        skip_weight.reshape(256, 256),
        output_weight,
        norm_gain_vector.reshape(1, 128),
        norm_offset_vector.reshape(1, 128),
    )
    grad, conv, bias, res, skip, out, into, gain, shift = pl.pallas_call(
        unpack_kernel,
        name="unpack",
        out_shape=(
            shape((steps, 128), f32),
            shape((2, 2, 128, 256), f32),
            shape((2, 256), f32),
            shape((128, 128), f32),
            shape((2, 128, 256), f32),
            shape((256, 128), f32),
            shape((128, 128), f32),
            shape((1, 128), f32),
            shape((1, 128), f32),
        ),
        in_specs=[vmem] * 4,
        out_specs=(hbm,) + (vmem,) * 8,
        scratch_shapes=[sem],
        compiler_params=pltpu.CompilerParams(vmem_limit_bytes=8 * 1024 * 1024),
    )(hat, early, late, last)
    return grad[None], conv, bias, res, skip, out, into, gain.reshape(128), shift.reshape(128)


def solution(mesh):
    split = P("series", "tm", None)
    return jax.shard_map(
        on_device,
        mesh=mesh,
        in_specs=(split, split) + (P(),) * 8,
        out_specs=(split,) + (P(),) * 8,
        check_vma=False,
    )
```

```python
import jax
import jax.numpy as jnp
from jax import lax
from jax.experimental import pallas as pl
from jax.experimental.pallas import tpu as pltpu
from jax.sharding import PartitionSpec as P

FIRST = 256
SECOND = 512
TM = 32
SER = 8
X = 4
Z = 8
Y = 4
PLANE = X * Y
PARTS = 2 * PLANE
ROWS = 2048
MESH = pl.DeviceIdType.MESH
EARLY, LATE, LAST = 32, 32, 8

epsilon = 1e-05
gelu_coeff = 0.7978845608
cubic_coeff = 0.044715


def nn(left, right):
    return jnp.dot(left, right, preferred_element_type=jnp.float32)


def nt(left, right):
    return lax.dot_general(
        left, right, (((1,), (1,)), ((), ())), preferred_element_type=jnp.float32
    )


def tn(left, right):
    return lax.dot_general(
        left, right, (((0,), (0,)), ((), ())), preferred_element_type=jnp.float32
    )


def fold(values):
    return jnp.sum(values.reshape(-1, 8, values.shape[-1]), axis=0)


def each(lo, hi, body):
    def run(k, carry):
        body(k)
        return carry

    lax.fori_loop(lo, hi, run, 0)


def at(start, size):
    return pl.ds(pl.multiple_of(start, 8), size)


def remote(src, dst, s_sem, r_sem, device):
    return pltpu.make_async_remote_copy(
        src_ref=src,
        dst_ref=dst,
        send_sem=s_sem,
        recv_sem=r_sem,
        device_id=device,
        device_id_type=MESH,
    )


def block_kernel(
    x_hbm,
    cot_hbm,
    w_in_hbm,
    w_conv_hbm,
    bias_hbm,
    w_res_hbm,
    w_skip_hbm,
    w_out_hbm,
    gain_hbm,
    offset_hbm,
    hat,
    early_out,
    late_out,
    last_out,
    w_in,
    w_conv,
    bias,
    w_res,
    w_skip,
    w_out,
    gain_ref,
    offset_ref,
    x,
    cot,
    level_zero,
    level_one,
    gated_one,
    tanh_one,
    sigm_one,
    incoming_one,
    near_one,
    far_one,
    near_zero,
    far_zero,
    early,
    late,
    last,
    in_grad,
    acc,
    stats,
    stats_z,
    stats_x,
    ends,
    ends_z,
    ends_x,
    early_pair,
    late_pair,
    last_pair,
    early_half,
    late_half,
    last_half,
    early_send,
    late_send,
    last_send,
    early_one,
    late_one,
    last_one,
    early_two,
    late_two,
    last_two,
    early_block,
    late_block,
    last_block,
    load_sem,
    halo_s,
    halo_r,
    line_s,
    line_r,
    pair_s,
    pair_r,
    one_s,
    one_r,
    two_s,
    two_r,
    three_s,
    three_r,
    back_s,
    back_r,
):
    steps = x.shape[0]
    chunks = steps // ROWS
    total_steps = float(steps * TM)
    ser = lax.axis_index("series")
    tm = lax.axis_index("tm")
    across, depth = tm // Z, lax.rem(tm, Z)
    up, core = ser // 2, lax.rem(ser, 2)
    mine = across * Y + up
    mate = {"series": ser + 1 - 2 * core}

    def on_z(peer):
        return {"tm": across * Z + peer}

    def on_x(peer):
        return {"tm": peer * Z + depth}

    def on_plane(peer):
        return {"series": lax.rem(peer, Y) * 2 + core, "tm": (peer // Y) * Z + depth}

    def load_x(c):
        return pltpu.make_async_copy(
            x_hbm.at[at(c * ROWS, ROWS)], x.at[at(c * ROWS, ROWS)], load_sem.at[c]
        )

    load_cot = pltpu.make_async_copy(cot_hbm, cot, load_sem.at[chunks])
    each(0, chunks, lambda c: load_x(c).start())
    load_cot.start()
    params = [
        pltpu.make_async_copy(src, dst, load_sem.at[chunks + 1 + k])
        for k, (src, dst) in enumerate(
            (
                (w_in_hbm, w_in),
                (w_conv_hbm, w_conv),
                (bias_hbm, bias),
                (w_res_hbm, w_res),
                (w_skip_hbm, w_skip),
                (w_out_hbm, w_out),
                (gain_hbm, gain_ref),
                (offset_hbm, offset_ref),
            )
        )
    ]
    for copy in params:
        copy.start()

    barrier = pltpu.get_barrier_semaphore()

    def hello(device):
        pl.semaphore_signal(barrier, inc=1, device_id=device, device_id_type=MESH)

    for k in range(1, Z):
        hello(on_z(lax.rem(depth + k, Z)))
    for k in range(1, X):
        hello(on_x(lax.rem(across + k, X)))
    for k in range(1, Y):
        hello({"series": lax.rem(up + k, Y) * 2 + core})
    hello(mate)

    acc[...] = jnp.zeros_like(acc)
    early[...] = jnp.zeros_like(early)
    late[...] = jnp.zeros_like(late)
    last[...] = jnp.zeros_like(last)
    in_grad[...] = jnp.zeros_like(in_grad)

    @pl.when(tm == 0)
    def _():
        level_zero[pl.ds(0, FIRST)] = jnp.zeros((FIRST, 128), jnp.bfloat16)
        level_one[pl.ds(0, SECOND)] = jnp.zeros((SECOND, 128), jnp.bfloat16)

    @pl.when(tm == TM - 1)
    def _():
        far_one[pl.ds(steps, SECOND)] = jnp.zeros((SECOND, 128), jnp.float32)
        far_zero[pl.ds(steps, FIRST)] = jnp.zeros((FIRST, 128), jnp.float32)

    def sum_x(c):
        load_x(c).wait()
        acc[0] += fold(x[at(c * ROWS, ROWS)])

    each(0, chunks, sum_x)
    local_sum = jnp.sum(acc[0], axis=0, keepdims=True)
    local_mean = local_sum / steps

    def sum_squares(c):
        centred = x[at(c * ROWS, ROWS)] - local_mean
        acc[1] += fold(centred * centred)

    each(0, chunks, sum_squares)
    stats[0:1] = local_sum
    stats[1:2] = jnp.sum(acc[1], axis=0, keepdims=True)
    pl.semaphore_wait(barrier, Z + X + Y - 2)

    def line(which, own, slots, count, me, device):
        def copy(peer, slot):
            return remote(own, slots.at[slot], line_s.at[which], line_r.at[which], device(peer))

        rest = slots.at[pl.ds(0, count - 1)]
        whole = remote(rest, rest, line_s.at[which], line_r.at[which], device(me))
        for k in range(1, count):
            copy(lax.rem(me + k, count), me).start()
        slots[pl.ds(me, 1)] = own[...][None]
        return whole

    def combine(slots, count):
        sums = slots[:, 0]
        total = jnp.sum(sums, axis=0, keepdims=True)
        shift = sums / count - total / (count * slots.shape[0])
        squares = slots[:, 1] + count * (shift * shift)
        return total, jnp.sum(squares, axis=0, keepdims=True)

    line(0, stats, stats_z, Z, depth, on_z).wait()
    total, squares = combine(stats_z, float(steps))
    stats[0:1] = total
    stats[1:2] = squares
    line(1, stats, stats_x, X, across, on_x).wait()
    total, squares = combine(stats_x, float(steps * Z))
    mean = total / total_steps
    variance = squares / total_steps
    inverse = lax.rsqrt(variance + epsilon)
    spread = jnp.sqrt(variance + epsilon)
    for copy in params:
        copy.wait()
    gain, offset = gain_ref[...], offset_ref[...]
    scale = spread / gain

    later, earlier = {"tm": lax.rem(tm + 1, TM)}, {"tm": lax.rem(tm + TM - 1, TM)}
    halo = (
        remote(
            level_zero.at[pl.ds(steps, FIRST)],
            level_zero.at[pl.ds(0, FIRST)],
            halo_s.at[0],
            halo_r.at[0],
            later,
        ),
        remote(
            level_one.at[pl.ds(steps, SECOND)],
            level_one.at[pl.ds(0, SECOND)],
            halo_s.at[1],
            halo_r.at[1],
            later,
        ),
        remote(
            far_one.at[pl.ds(0, SECOND)],
            far_one.at[pl.ds(steps, SECOND)],
            halo_s.at[2],
            halo_r.at[2],
            earlier,
        ),
        remote(
            far_zero.at[pl.ds(0, FIRST)],
            far_zero.at[pl.ds(steps, FIRST)],
            halo_s.at[3],
            halo_r.at[3],
            earlier,
        ),
    )

    def normalize(c):
        hat_x = (x[at(c * ROWS, ROWS)] - mean) * inverse
        return hat_x, (hat_x * gain + offset).astype(jnp.bfloat16)

    def project(i):
        c = chunks - 1 - i
        _, normed = normalize(c)
        level_zero[at(FIRST + c * ROWS, ROWS)] = nn(normed, w_in[...]).astype(jnp.bfloat16)

        @pl.when(jnp.logical_and(i == 0, tm < TM - 1))
        def _():
            halo[0].start()

    each(0, chunks, project)

    def gates(act):
        return jnp.tanh(act[:, :128]), 0.5 * jnp.tanh(0.5 * act[:, 128:]) + 0.5

    def window_zero(c):
        return jnp.concatenate(
            [level_zero[at(c * ROWS, ROWS)], level_zero[at(c * ROWS + FIRST, ROWS)]], axis=1
        )

    def window_one(c):
        return jnp.concatenate(
            [level_one[at(c * ROWS, ROWS)], level_one[at(c * ROWS + SECOND, ROWS)]], axis=1
        )

    def layer_one(i):
        c = chunks - 1 - i

        @pl.when(jnp.logical_and(c == 0, tm > 0))
        def _():
            halo[0].wait_recv()

        now = at(c * ROWS, ROWS)
        tanh, sigm = gates(nn(window_zero(c), w_conv[0]) + bias[0:1])
        gated = (tanh * sigm).astype(jnp.bfloat16)
        tanh_one[now] = tanh
        sigm_one[now] = sigm
        gated_one[now] = gated
        level = level_zero[at(c * ROWS + FIRST, ROWS)].astype(jnp.float32)
        level_one[at(c * ROWS + SECOND, ROWS)] = (level + nn(gated, w_res[...])).astype(
            jnp.bfloat16
        )

        @pl.when(jnp.logical_and(i == 0, tm < TM - 1))
        def _():
            halo[1].start()

    each(0, chunks, layer_one)

    def gate_back(incoming, tanh, sigm):
        part = incoming * sigm
        return part * (1.0 - tanh * tanh), part * tanh * (1.0 - sigm)

    load_cot.wait()

    @pl.when(tm > 0)
    def _():
        halo[1].wait_recv()

    def layer_two(c):
        now = at(c * ROWS, ROWS)
        window = window_one(c)
        tanh, sigm = gates(nn(window, w_conv[1]) + bias[1:2])
        gated = (tanh * sigm).astype(jnp.bfloat16)
        both = jnp.concatenate([gated_one[now], gated], axis=1)
        skip = nn(both, w_skip[...])
        square = skip * skip
        half = 0.5 * jnp.tanh(
            skip * (gelu_coeff + (gelu_coeff * cubic_coeff) * square)
        ) + 0.5
        value = skip * half
        slope = half + value * (1.0 - half) * (
            2.0 * gelu_coeff + (6.0 * gelu_coeff * cubic_coeff) * square
        )
        rectified = value.astype(jnp.bfloat16)
        forecast = nn(rectified, w_out[...])
        gradient = cot[now]
        acc[2] += fold(gradient)
        acc[3] += fold(gradient * (forecast - offset))
        scaled = (gradient * scale).astype(jnp.bfloat16)
        out_part = tn(rectified, scaled)
        late[640:896] += out_part
        back_skip = (nt(scaled, w_out[...]) * slope).astype(jnp.bfloat16)
        skip_part = tn(both, back_skip)
        early[512:768] += skip_part[:, :128]
        early[768:1024] += skip_part[:, 128:]
        incoming = nt(back_skip, w_skip[...])
        incoming_one[now] = incoming[:, :128]
        first, second = gate_back(incoming[:, 128:], tanh, sigm)
        acc[4] += fold(first)
        acc[5] += fold(second)
        pre = jnp.concatenate([first, second], axis=1).astype(jnp.bfloat16)
        conv_part = tn(window, pre)
        early[0:256] += conv_part[:, :128]
        early[256:512] += conv_part[:, 128:]
        carried = nt(pre, w_conv[1])
        far_one[now] = carried[:, :128]
        near_one[now] = carried[:, 128:]

        @pl.when(jnp.logical_and(c == 0, tm > 0))
        def _():
            halo[2].start()

    each(0, chunks, layer_two)

    groups = (
        (early, early_pair, early_half, early_one, early_block, early_two, early_out, EARLY),
        (late, late_pair, late_half, late_one, late_block, late_two, late_out, LATE),
        (last, last_pair, last_half, last_one, last_block, last_two, last_out, LAST),
    )
    sends = (early_send, late_send, last_send)

    def pair(g):
        return remote(sends[g], groups[g][1], pair_s.at[g], pair_r.at[g], mate)

    def one(g, k):
        got, size = groups[g][3], groups[g][7]
        peer = lax.rem(mine + k, PLANE)
        return remote(
            sends[g].at[at(peer * size, size)],
            got.at[k],
            one_s.at[g],
            one_r.at[g],
            on_plane(peer),
        )

    def two(g, k):
        block, got = groups[g][4], groups[g][5]
        peer = lax.rem(depth + k, Z)
        return remote(block, got.at[depth], two_s.at[g], two_r.at[g], on_z(peer))

    def three(g, k):
        out, size = groups[g][6], groups[g][7]
        where = out.at[at((core * PLANE + mine) * size, size)]
        peer = lax.rem(mine + k, PLANE)
        return remote(where, where, three_s.at[g], three_r.at[g], on_plane(peer))

    def back(g):
        out, size = groups[g][6], groups[g][7] * PLANE
        where = out.at[at(core * size, size)]
        return remote(where, where, back_s.at[g], back_r.at[g], mate)

    def whole(g, ref, count, s_sem, r_sem):
        rest = ref.at[pl.ds(0, count)]
        return remote(rest, rest, s_sem.at[g], r_sem.at[g], mate)

    def all_one(g):
        return whole(g, groups[g][3], PLANE - 1, one_s, one_r)

    def all_two(g):
        return whole(g, groups[g][5], Z - 1, two_s, two_r)

    def all_three(g):
        return whole(g, groups[g][6], (PLANE - 1) * groups[g][7], three_s, three_r)

    def wide(values):
        return values.astype(jnp.float32)

    def start(g):
        src, size = groups[g][0], groups[g][7] * PLANE
        sends[g][...] = src[at((1 - core) * size, size)].astype(sends[g].dtype)
        pair(g).start()

    def scatter(g):
        src, got, half, slots, _, _, _, size = groups[g]
        pair(g).wait()
        total = src[at(core * PLANE * size, PLANE * size)] + wide(got[...])
        half[...] = total
        sends[g][...] = total.astype(sends[g].dtype)
        each(1, PLANE, lambda k: one(g, k).start())

    def middle(g):
        _, _, half, slots, block, far, _, size = groups[g]
        all_one(g).wait_recv()
        total = half[at(mine * size, size)]
        for p in range(1, PLANE):
            total = total + wide(slots[p])
        block[...] = total.astype(block.dtype)
        each(1, Z, lambda k: two(g, k).start())
        far[pl.ds(depth, 1)] = block[...][None]

    def gather(g):
        _, _, _, _, _, far, out, size = groups[g]
        all_two(g).wait_recv()
        total = wide(far[0])
        for z in range(1, Z):
            total = total + wide(far[z])
        out[at((core * PLANE + mine) * size, size)] = total.astype(out.dtype)
        each(1, PLANE, lambda k: three(g, k).start())

    def share(g):
        all_three(g).wait_recv()
        back(g).start()

    def finish(g):
        back(g).wait_recv()
        all_one(g).wait_send()
        all_two(g).wait_send()
        all_three(g).wait_send()
        back(g).wait_send()

    start(0)

    def back_one(c):
        @pl.when(jnp.logical_and(c == chunks - 1, tm < TM - 1))
        def _():
            halo[2].wait_recv()

        @pl.when(c == chunks - 1)
        def _():
            scatter(0)

        now = at(c * ROWS, ROWS)
        arrived = near_one[now] + far_one[at(c * ROWS + SECOND, ROWS)]
        grad_one = arrived.astype(jnp.bfloat16)
        late[512:640] += tn(gated_one[now], grad_one)
        incoming = incoming_one[now] + nt(grad_one, w_res[...])
        first, second = gate_back(incoming, tanh_one[now], sigm_one[now])
        acc[6] += fold(first)
        acc[7] += fold(second)
        pre = jnp.concatenate([first, second], axis=1).astype(jnp.bfloat16)
        conv_part = tn(window_zero(c), pre)
        late[0:256] += conv_part[:, :128]
        late[256:512] += conv_part[:, 128:]
        carried = nt(pre, w_conv[0])
        far_zero[now] = carried[:, :128]
        near_zero[now] = grad_one.astype(jnp.float32) + carried[:, 128:]

        @pl.when(jnp.logical_and(c == 0, tm > 0))
        def _():
            halo[3].start()

    each(0, chunks, back_one)
    start(1)

    def back_zero(c):
        @pl.when(jnp.logical_and(c == chunks - 1, tm < TM - 1))
        def _():
            halo[3].wait_recv()

        @pl.when(c == chunks - 1)
        def _():
            scatter(1)

        now = at(c * ROWS, ROWS)
        grad_zero = (near_zero[now] + far_zero[at(c * ROWS + FIRST, ROWS)]).astype(jnp.bfloat16)
        hat_x, normed = normalize(c)
        in_grad[...] += tn(normed, grad_zero)
        grad_hat = nt(grad_zero, w_in[...]) * gain
        hat[now] = grad_hat
        acc[8] += fold(grad_hat)
        acc[9] += fold(grad_hat * hat_x)

    each(0, chunks, back_zero)

    def column(k):
        return jnp.sum(acc[k], axis=0, keepdims=True)

    sum_a, sum_b, out_a, out_b = column(8), column(9), column(2), column(3) / gain
    ends[0:1] = sum_a
    ends[1:2] = sum_b
    ends[2:3] = out_a
    ends[3:4] = out_b
    ends_line = line(2, ends, ends_z, Z, depth, on_z)
    for p in range(PARTS):
        last[8 * p : 8 * p + 4] = in_grad[4 * p : 4 * p + 4]
    last[4:5] = (sum_b - out_b * spread) / gain
    last[12:13] = (sum_a - out_a * spread) / gain
    last[20:21] = column(6)
    last[28:29] = column(7)
    last[36:37] = column(4)
    last[44:45] = column(5)
    start(2)
    scatter(2)
    middle(0)
    ends_line.wait()
    ends[...] = jnp.sum(ends_z[...], axis=0)
    ends_line = line(3, ends, ends_x, X, across, on_x)
    middle(1)
    middle(2)
    gather(0)
    ends_line.wait()
    totals = jnp.sum(ends_x[...], axis=0) / total_steps
    slant = inverse * (totals[3:4] - inverse * totals[1:2])
    level = totals[2:3] - inverse * totals[0:1]
    def resolve(c):
        now = at(c * ROWS, ROWS)
        hat[now] = hat[now] * inverse + ((x[now] - mean) * slant + level)

    each(0, chunks, resolve)
    gather(1)
    share(0)
    gather(2)
    share(1)
    share(2)

    @pl.when(tm < TM - 1)
    def _():
        halo[0].wait_send()
        halo[1].wait_send()

    @pl.when(tm > 0)
    def _():
        halo[2].wait_send()
        halo[3].wait_send()

    finish(0)
    finish(1)
    finish(2)


def unpack_kernel(
    hat, early, late, last, grad, conv, bias, res, skip, out, into, gain, shift, store_sem
):
    store = pltpu.make_async_copy(hat, grad, store_sem)
    store.start()
    for layer, src in ((0, late), (1, early)):
        for tap in range(2):
            for half in range(2):
                conv[layer, tap, :, half * 128 : half * 128 + 128] = src[
                    pl.ds(half * 256 + tap * 128, 128)
                ].astype(jnp.float32)
    for layer in range(2):
        for half in range(2):
            skip[layer, :, half * 128 : half * 128 + 128] = early[
                pl.ds(512 + half * 256 + layer * 128, 128)
            ].astype(jnp.float32)
            bias[layer : layer + 1, half * 128 : half * 128 + 128] = last[
                pl.ds(20 + layer * 16 + half * 8, 1)
            ]
    out[...] = late[640:896].astype(jnp.float32)
    res[...] = late[512:640].astype(jnp.float32)
    for p in range(PARTS):
        into[4 * p : 4 * p + 4] = last[8 * p : 8 * p + 4]
    gain[...] = last[4:5]
    shift[...] = last[12:13]
    store.wait()


def on_device(
    series_data,
    cotangent,
    in_weight,
    convolution_weight,
    convolution_bias,
    res_weight,
    skip_weight,
    output_weight,
    norm_gain_vector,
    norm_offset_vector,
):
    steps = series_data.shape[1]
    f32, bf16 = jnp.float32, jnp.bfloat16
    vmem = pl.BlockSpec(memory_space=pltpu.VMEM)
    hbm = pl.BlockSpec(memory_space=pltpu.HBM)
    sem = pltpu.SemaphoreType.DMA
    shape = jax.ShapeDtypeStruct
    field = pltpu.VMEM((steps, 128), f32)

    sizes = (EARLY, LATE, LAST)
    wires = (bf16, bf16, f32)

    def slots(lead):
        return [pltpu.VMEM((lead, n, 128), wire) for n, wire in zip(sizes, wires)]

    def blocks(count):
        return [pltpu.VMEM((count * n, 128), wire) for n, wire in zip(sizes, wires)]

    def wide_blocks(count):
        return [pltpu.VMEM((count * n, 128), f32) for n in sizes]

    hat, early, late, last = pl.pallas_call(
        block_kernel,
        name="block",
        out_shape=(
            pltpu.VMEM((steps, 128), f32),
            *blocks(PARTS),
        ),
        in_specs=[hbm] * 10,
        out_specs=(vmem,) * 4,
        scratch_shapes=[
            pltpu.VMEM((128, 128), bf16),
            pltpu.VMEM((2, 256, 256), bf16),
            pltpu.VMEM((2, 256), f32),
            pltpu.VMEM((128, 128), bf16),
            pltpu.VMEM((256, 256), bf16),
            pltpu.VMEM((256, 128), bf16),
            pltpu.VMEM((1, 128), f32),
            pltpu.VMEM((1, 128), f32),
            field,
            field,
            pltpu.VMEM((steps + FIRST, 128), bf16),
            pltpu.VMEM((steps + SECOND, 128), bf16),
            pltpu.VMEM((steps, 128), bf16),
            field,
            field,
            field,
            field,
            pltpu.VMEM((steps + SECOND, 128), f32),
            field,
            pltpu.VMEM((steps + FIRST, 128), f32),
            *wide_blocks(PARTS),
            pltpu.VMEM((128, 128), f32),
            pltpu.VMEM((10, 8, 128), f32),
            pltpu.VMEM((2, 128), f32),
            pltpu.VMEM((Z, 2, 128), f32),
            pltpu.VMEM((X, 2, 128), f32),
            pltpu.VMEM((4, 128), f32),
            pltpu.VMEM((Z, 4, 128), f32),
            pltpu.VMEM((X, 4, 128), f32),
            *blocks(PLANE),
            *wide_blocks(PLANE),
            *blocks(PLANE),
            *slots(PLANE),
            *slots(Z),
            *blocks(1),
            sem((steps // ROWS + 9,)),
            sem((4,)),
            sem((4,)),
            sem((4,)),
            sem((4,)),
            *[sem((3,))] * 10,
        ],
        compiler_params=pltpu.CompilerParams(
            collective_id=0, has_side_effects=True, vmem_limit_bytes=56 * 1024 * 1024
        ),
    )(
        series_data[0],
        cotangent[0],
        in_weight,
        convolution_weight.reshape(2, 256, 256),
        convolution_bias,
        res_weight,
        skip_weight.reshape(256, 256),
        output_weight,
        norm_gain_vector.reshape(1, 128),
        norm_offset_vector.reshape(1, 128),
    )
    grad, conv, bias, res, skip, out, into, gain, shift = pl.pallas_call(
        unpack_kernel,
        name="unpack",
        out_shape=(
            shape((steps, 128), f32),
            shape((2, 2, 128, 256), f32),
            shape((2, 256), f32),
            shape((128, 128), f32),
            shape((2, 128, 256), f32),
            shape((256, 128), f32),
            shape((128, 128), f32),
            shape((1, 128), f32),
            shape((1, 128), f32),
        ),
        in_specs=[vmem] * 4,
        out_specs=(hbm,) + (vmem,) * 8,
        scratch_shapes=[sem],
        compiler_params=pltpu.CompilerParams(vmem_limit_bytes=8 * 1024 * 1024),
    )(hat, early, late, last)
    return grad[None], conv, bias, res, skip, out, into, gain.reshape(128), shift.reshape(128)


def solution(mesh):
    split = P("series", "tm", None)
    return jax.shard_map(
        on_device,
        mesh=mesh,
        in_specs=(split, split) + (P(),) * 8,
        out_specs=(split,) + (P(),) * 8,
        check_vma=False,
    )
```

```python
import jax
import jax.numpy as jnp
from jax import lax
from jax.experimental import pallas as pl
from jax.experimental.pallas import tpu as pltpu
from jax.sharding import PartitionSpec as P

FIRST = 256
SECOND = 512
TM = 32
SER = 8
X = 4
Z = 8
Y = 4
PLANE = X * Y
PARTS = 2 * PLANE
ROWS = 1024
MESH = pl.DeviceIdType.MESH
EARLY, LATE, LAST = 32, 32, 8

epsilon = 1e-05
gelu_coeff = 0.7978845608
cubic_coeff = 0.044715


def nn(left, right):
    return jnp.dot(left, right, preferred_element_type=jnp.float32)


def nt(left, right):
    return lax.dot_general(
        left, right, (((1,), (1,)), ((), ())), preferred_element_type=jnp.float32
    )


def tn(left, right):
    return lax.dot_general(
        left, right, (((0,), (0,)), ((), ())), preferred_element_type=jnp.float32
    )


def fold(values):
    return jnp.sum(values.reshape(-1, 8, values.shape[-1]), axis=0)


def each(lo, hi, body):
    def run(k, carry):
        body(k)
        return carry

    lax.fori_loop(lo, hi, run, 0)


def at(start, size):
    return pl.ds(pl.multiple_of(start, 8), size)


def remote(src, dst, s_sem, r_sem, device):
    return pltpu.make_async_remote_copy(
        src_ref=src,
        dst_ref=dst,
        send_sem=s_sem,
        recv_sem=r_sem,
        device_id=device,
        device_id_type=MESH,
    )


def block_kernel(
    x_hbm,
    cot_hbm,
    w_in_hbm,
    w_conv_hbm,
    bias_hbm,
    w_res_hbm,
    w_skip_hbm,
    w_out_hbm,
    gain_hbm,
    offset_hbm,
    hat,
    early_out,
    late_out,
    last_out,
    w_in,
    w_conv,
    bias,
    w_res,
    w_skip,
    w_out,
    gain_ref,
    offset_ref,
    x,
    cot,
    level_zero,
    level_one,
    gated_one,
    tanh_one,
    sigm_one,
    incoming_one,
    near_one,
    far_one,
    near_zero,
    far_zero,
    far_one_head,
    far_one_tail,
    far_zero_head,
    far_zero_tail,
    early,
    late,
    last,
    in_grad,
    acc,
    stats,
    stats_z,
    stats_x,
    ends,
    ends_z,
    ends_x,
    early_pair,
    late_pair,
    early_half,
    late_half,
    early_send,
    late_send,
    early_one,
    late_one,
    last_one,
    early_two,
    late_two,
    last_two,
    early_block,
    late_block,
    last_block,
    load_sem,
    halo_s,
    halo_r,
    line_s,
    line_r,
    pair_s,
    pair_r,
    one_s,
    one_r,
    two_s,
    two_r,
    three_s,
    three_r,
    back_s,
    back_r,
):
    steps = x.shape[0]
    chunks = steps // ROWS
    total_steps = float(steps * TM)
    ser = lax.axis_index("series")
    tm = lax.axis_index("tm")
    across, depth = tm // Z, lax.rem(tm, Z)
    up, core = ser // 2, lax.rem(ser, 2)
    mine = across * Y + up
    mate = {"series": ser + 1 - 2 * core}

    def on_z(peer):
        return {"tm": across * Z + peer}

    def on_x(peer):
        return {"tm": peer * Z + depth}

    def on_plane(peer):
        return {"series": lax.rem(peer, Y) * 2 + core, "tm": (peer // Y) * Z + depth}

    def load_x(c):
        return pltpu.make_async_copy(
            x_hbm.at[at(c * ROWS, ROWS)], x.at[at(c * ROWS, ROWS)], load_sem.at[c]
        )

    load_cot = pltpu.make_async_copy(cot_hbm, cot, load_sem.at[chunks])
    each(0, chunks, lambda c: load_x(c).start())
    load_cot.start()
    params = [
        pltpu.make_async_copy(src, dst, load_sem.at[chunks + 1 + k])
        for k, (src, dst) in enumerate(
            (
                (w_in_hbm, w_in),
                (w_conv_hbm, w_conv),
                (bias_hbm, bias),
                (w_res_hbm, w_res),
                (w_skip_hbm, w_skip),
                (w_out_hbm, w_out),
                (gain_hbm, gain_ref),
                (offset_hbm, offset_ref),
            )
        )
    ]
    for copy in params:
        copy.start()

    barrier = pltpu.get_barrier_semaphore()

    def hello(device):
        pl.semaphore_signal(barrier, inc=1, device_id=device, device_id_type=MESH)

    for k in range(1, Z):
        hello(on_z(lax.rem(depth + k, Z)))
    for k in range(1, X):
        hello(on_x(lax.rem(across + k, X)))
    for k in range(1, Y):
        hello({"series": lax.rem(up + k, Y) * 2 + core})
    hello(mate)

    acc[...] = jnp.zeros_like(acc)
    early[...] = jnp.zeros_like(early)
    late[...] = jnp.zeros_like(late)
    last[...] = jnp.zeros_like(last)
    in_grad[...] = jnp.zeros_like(in_grad)

    @pl.when(tm == 0)
    def _():
        level_zero[pl.ds(0, FIRST)] = jnp.zeros((FIRST, 128), jnp.bfloat16)
        level_one[pl.ds(0, SECOND)] = jnp.zeros((SECOND, 128), jnp.bfloat16)

    @pl.when(tm == TM - 1)
    def _():
        far_one_tail[...] = jnp.zeros_like(far_one_tail)
        far_zero_tail[...] = jnp.zeros_like(far_zero_tail)

    def sum_x(c):
        load_x(c).wait()
        acc[0] += fold(x[at(c * ROWS, ROWS)])

    each(0, chunks, sum_x)
    local_sum = jnp.sum(acc[0], axis=0, keepdims=True)
    local_mean = local_sum / steps

    def sum_squares(c):
        centred = x[at(c * ROWS, ROWS)] - local_mean
        acc[1] += fold(centred * centred)

    each(0, chunks, sum_squares)
    stats[0:1] = local_sum
    stats[1:2] = jnp.sum(acc[1], axis=0, keepdims=True)
    pl.semaphore_wait(barrier, Z + X + Y - 2)

    def line(which, own, slots, count, me, device):
        def copy(peer, slot):
            return remote(own, slots.at[slot], line_s.at[which], line_r.at[which], device(peer))

        rest = slots.at[pl.ds(0, count - 1)]
        whole = remote(rest, rest, line_s.at[which], line_r.at[which], device(me))
        for k in range(1, count):
            copy(lax.rem(me + k, count), me).start()
        slots[pl.ds(me, 1)] = own[...][None]
        return whole

    def combine(slots, count):
        sums = slots[:, 0]
        total = jnp.sum(sums, axis=0, keepdims=True)
        shift = sums / count - total / (count * slots.shape[0])
        squares = slots[:, 1] + count * (shift * shift)
        return total, jnp.sum(squares, axis=0, keepdims=True)

    line(0, stats, stats_z, Z, depth, on_z).wait()
    total, squares = combine(stats_z, float(steps))
    stats[0:1] = total
    stats[1:2] = squares
    line(1, stats, stats_x, X, across, on_x).wait()
    total, squares = combine(stats_x, float(steps * Z))
    mean = total / total_steps
    variance = squares / total_steps
    inverse = lax.rsqrt(variance + epsilon)
    spread = jnp.sqrt(variance + epsilon)
    for copy in params:
        copy.wait()
    gain, offset = gain_ref[...], offset_ref[...]
    scale = spread / gain

    later, earlier = {"tm": lax.rem(tm + 1, TM)}, {"tm": lax.rem(tm + TM - 1, TM)}
    halo = (
        remote(
            level_zero.at[pl.ds(steps, FIRST)],
            level_zero.at[pl.ds(0, FIRST)],
            halo_s.at[0],
            halo_r.at[0],
            later,
        ),
        remote(
            level_one.at[pl.ds(steps, SECOND)],
            level_one.at[pl.ds(0, SECOND)],
            halo_s.at[1],
            halo_r.at[1],
            later,
        ),
        remote(
            far_one_head,
            far_one_tail,
            halo_s.at[2],
            halo_r.at[2],
            earlier,
        ),
        remote(
            far_zero_head,
            far_zero_tail,
            halo_s.at[3],
            halo_r.at[3],
            earlier,
        ),
    )

    has_later, has_earlier = tm < TM - 1, tm > 0

    def normalize(start, size):
        hat_x = (x[pl.ds(start, size)] - mean) * inverse
        return hat_x, (hat_x * gain + offset).astype(jnp.bfloat16)

    def project(start, size):
        _, normed = normalize(start, size)
        level_zero[pl.ds(FIRST + start, size)] = nn(normed, w_in[...]).astype(jnp.bfloat16)

    def gates(act):
        return jnp.tanh(act[:, :128]), 0.5 * jnp.tanh(0.5 * act[:, 128:]) + 0.5

    def window_zero(start, size):
        return jnp.concatenate(
            [level_zero[pl.ds(start, size)], level_zero[pl.ds(start + FIRST, size)]], axis=1
        )

    def window_one(start, size):
        return jnp.concatenate(
            [level_one[pl.ds(start, size)], level_one[pl.ds(start + SECOND, size)]], axis=1
        )

    def layer_one(start, size):
        now = pl.ds(start, size)
        tanh, sigm = gates(nn(window_zero(start, size), w_conv[0]) + bias[0:1])
        gated = (tanh * sigm).astype(jnp.bfloat16)
        tanh_one[now] = tanh
        sigm_one[now] = sigm
        gated_one[now] = gated
        level = level_zero[pl.ds(start + FIRST, size)].astype(jnp.float32)
        level_one[pl.ds(start + SECOND, size)] = (level + nn(gated, w_res[...])).astype(
            jnp.bfloat16
        )

    project(steps - SECOND - FIRST, SECOND + FIRST)
    pl.when(has_later)(halo[0].start)
    layer_one(steps - SECOND, SECOND)
    pl.when(has_later)(halo[1].start)
    project(0, steps - SECOND - FIRST)
    layer_one(SECOND, steps - 2 * SECOND)
    pl.when(has_earlier)(halo[0].wait_recv)
    layer_one(0, SECOND)

    def gate_back(incoming, tanh, sigm):
        part = incoming * sigm
        return part * (1.0 - tanh * tanh), part * tanh * (1.0 - sigm)

    load_cot.wait()

    def layer_two(start, size):
        now = pl.ds(start, size)
        window = window_one(start, size)
        tanh, sigm = gates(nn(window, w_conv[1]) + bias[1:2])
        gated = (tanh * sigm).astype(jnp.bfloat16)
        both = jnp.concatenate([gated_one[now], gated], axis=1)
        skip = nn(both, w_skip[...])
        square = skip * skip
        half = 0.5 * jnp.tanh(
            skip * (gelu_coeff + (gelu_coeff * cubic_coeff) * square)
        ) + 0.5
        value = skip * half
        slope = half + value * (1.0 - half) * (
            2.0 * gelu_coeff + (6.0 * gelu_coeff * cubic_coeff) * square
        )
        rectified = value.astype(jnp.bfloat16)
        forecast = nn(rectified, w_out[...])
        gradient = cot[now]
        acc[2] += fold(gradient)
        acc[3] += fold(gradient * (forecast - offset))
        scaled = (gradient * scale).astype(jnp.bfloat16)
        out_part = tn(rectified, scaled)
        late[640:896] += out_part
        back_skip = (nt(scaled, w_out[...]) * slope).astype(jnp.bfloat16)
        skip_part = tn(both, back_skip)
        early[512:768] += skip_part[:, :128]
        early[768:1024] += skip_part[:, 128:]
        incoming = nt(back_skip, w_skip[...])
        incoming_one[now] = incoming[:, :128]
        first, second = gate_back(incoming[:, 128:], tanh, sigm)
        acc[4] += fold(first)
        acc[5] += fold(second)
        pre = jnp.concatenate([first, second], axis=1).astype(jnp.bfloat16)
        conv_part = tn(window, pre)
        early[0:256] += conv_part[:, :128]
        early[256:512] += conv_part[:, 128:]
        carried = nt(pre, w_conv[1])
        far_one[now] = carried[:, :128]
        near_one[now] = carried[:, 128:]

    layer_two(5 * SECOND, steps - 5 * SECOND)
    pl.when(has_earlier)(halo[1].wait_recv)
    layer_two(0, SECOND)
    far_one_head[...] = far_one[pl.ds(0, SECOND)].astype(jnp.bfloat16)
    pl.when(has_earlier)(halo[2].start)
    layer_two(SECOND, 4 * SECOND)

    groups = (
        (early, early_pair, early_half, early_one, early_block, early_two, early_out, EARLY),
        (late, late_pair, late_half, late_one, late_block, late_two, late_out, LATE),
        (last, None, None, last_one, last_block, last_two, last_out, LAST),
    )
    sends = (early_send, late_send)

    def pair(g):
        return remote(sends[g], groups[g][1], pair_s.at[g], pair_r.at[g], mate)

    def one(g, k):
        got, size = groups[g][3], groups[g][7]
        peer = lax.rem(mine + k, PLANE)
        return remote(
            sends[g].at[at(peer * size, size)],
            got.at[k],
            one_s.at[g],
            one_r.at[g],
            on_plane(peer),
        )

    def two(g, k):
        block, got = groups[g][4], groups[g][5]
        peer = lax.rem(depth + k, Z)
        return remote(block, got.at[depth], two_s.at[g], two_r.at[g], on_z(peer))

    def three(g, k):
        out, size = groups[g][6], groups[g][7]
        where = out.at[at(owner * size, size)]
        peer = lax.rem(mine + k, PLANE)
        return remote(where, where, three_s.at[g], three_r.at[g], on_plane(peer))

    def back(g):
        out, size = groups[g][6], groups[g][7] * PLANE
        where = out.at[at(core * size, size)]
        return remote(where, where, back_s.at[g], back_r.at[g], mate)

    def whole(g, ref, count, s_sem, r_sem):
        rest = ref.at[pl.ds(0, count)]
        return remote(rest, rest, s_sem.at[g], r_sem.at[g], mate)

    owner = core * PLANE + mine

    def on_owner(p):
        member = lax.rem(p, PLANE)
        return {
            "series": lax.rem(member, Y) * 2 + p // PLANE,
            "tm": (member // Y) * Z + depth,
        }

    def last_one_copy(k):
        peer = lax.rem(owner + k, PARTS)
        return remote(
            last.at[at(peer * LAST, LAST)], last_one.at[k], one_s.at[2], one_r.at[2], on_owner(peer)
        )

    def last_three_copy(k):
        where = last_out.at[at(owner * LAST, LAST)]
        peer = lax.rem(owner + k, PARTS)
        return remote(where, where, three_s.at[2], three_r.at[2], on_owner(peer))

    def all_one(g):
        return whole(g, groups[g][3], groups[g][3].shape[0] - 1, one_s, one_r)

    def all_two(g):
        return whole(g, groups[g][5], Z - 1, two_s, two_r)

    def all_three(g):
        peers = (PARTS if g == 2 else PLANE) - 1
        return whole(g, groups[g][6], peers * groups[g][7], three_s, three_r)

    def wide(values):
        return values.astype(jnp.float32)

    def start(g):
        src, size = groups[g][0], groups[g][7] * PLANE
        sends[g][...] = src[at((1 - core) * size, size)].astype(sends[g].dtype)
        pair(g).start()

    def scatter(g):
        src, got, half, slots, _, _, _, size = groups[g]
        pair(g).wait()
        total = src[at(core * PLANE * size, PLANE * size)] + wide(got[...])
        half[...] = total
        sends[g][...] = total.astype(sends[g].dtype)
        each(1, PLANE, lambda k: one(g, k).start())

    def middle(g):
        _, _, half, slots, block, far, _, size = groups[g]
        all_one(g).wait_recv()
        total = last[at(owner * size, size)] if g == 2 else half[at(mine * size, size)]
        for p in range(1, slots.shape[0]):
            total = total + wide(slots[p])
        block[...] = total.astype(block.dtype)
        each(1, Z, lambda k: two(g, k).start())
        far[pl.ds(depth, 1)] = block[...][None]

    def gather(g):
        _, _, _, _, _, far, out, size = groups[g]
        all_two(g).wait_recv()
        total = wide(far[0])
        for z in range(1, Z):
            total = total + wide(far[z])
        out[at(owner * size, size)] = total.astype(out.dtype)
        if g == 2:
            each(1, PARTS, lambda k: last_three_copy(k).start())
        else:
            each(1, PLANE, lambda k: three(g, k).start())

    def share(g):
        all_three(g).wait_recv()
        if g < 2:
            back(g).start()

    def finish(g):
        if g < 2:
            back(g).wait()
        all_one(g).wait_send()
        all_two(g).wait_send()
        all_three(g).wait_send()

    start(0)

    def back_one(start, size):
        now = pl.ds(start, size)
        last_rows = start + size == steps
        far = wide(far_one_tail[...]) if last_rows else far_one[pl.ds(start + SECOND, size)]
        grad_one = (near_one[now] + far).astype(jnp.bfloat16)
        late[512:640] += tn(gated_one[now], grad_one)
        incoming = incoming_one[now] + nt(grad_one, w_res[...])
        first, second = gate_back(incoming, tanh_one[now], sigm_one[now])
        acc[6] += fold(first)
        acc[7] += fold(second)
        pre = jnp.concatenate([first, second], axis=1).astype(jnp.bfloat16)
        conv_part = tn(window_zero(start, size), pre)
        late[0:256] += conv_part[:, :128]
        late[256:512] += conv_part[:, 128:]
        carried = nt(pre, w_conv[0])
        far_zero[now] = carried[:, :128]
        near_zero[now] = grad_one.astype(jnp.float32) + carried[:, 128:]

    back_one(0, SECOND)
    far_zero_head[...] = far_zero[pl.ds(0, FIRST)].astype(jnp.bfloat16)
    pl.when(has_earlier)(halo[3].start)
    scatter(0)
    back_one(SECOND, steps - 2 * SECOND)
    pl.when(has_later)(halo[2].wait_recv)
    back_one(steps - SECOND, SECOND)
    start(1)

    def back_zero(start, size):
        now = pl.ds(start, size)
        if start + size == steps:
            far = jnp.concatenate(
                [far_zero[pl.ds(start + FIRST, size - FIRST)], wide(far_zero_tail[...])], axis=0
            )
        else:
            far = far_zero[pl.ds(start + FIRST, size)]
        grad_zero = (near_zero[now] + far).astype(jnp.bfloat16)
        hat_x, normed = normalize(start, size)
        in_grad[...] += tn(normed, grad_zero)
        grad_hat = nt(grad_zero, w_in[...]) * gain
        hat[now] = grad_hat
        acc[8] += fold(grad_hat)
        acc[9] += fold(grad_hat * hat_x)

    back_zero(0, steps - SECOND)
    pl.when(has_later)(halo[3].wait_recv)
    scatter(1)
    back_zero(steps - SECOND, SECOND)

    def column(k):
        return jnp.sum(acc[k], axis=0, keepdims=True)

    sum_a, sum_b, out_a, out_b = column(8), column(9), column(2), column(3) / gain
    ends[0:1] = sum_a
    ends[1:2] = sum_b
    ends[2:3] = out_a
    ends[3:4] = out_b
    ends_line = line(2, ends, ends_z, Z, depth, on_z)
    for p in range(PARTS):
        last[8 * p : 8 * p + 4] = in_grad[4 * p : 4 * p + 4]
    last[4:5] = (sum_b - out_b * spread) / gain
    last[12:13] = (sum_a - out_a * spread) / gain
    last[20:21] = column(6)
    last[28:29] = column(7)
    last[36:37] = column(4)
    last[44:45] = column(5)
    each(1, PARTS, lambda k: last_one_copy(k).start())
    middle(0)
    ends_line.wait()
    ends[...] = jnp.sum(ends_z[...], axis=0)
    ends_line = line(3, ends, ends_x, X, across, on_x)
    middle(1)
    middle(2)
    gather(0)
    ends_line.wait()
    totals = jnp.sum(ends_x[...], axis=0) / total_steps
    slant = inverse * (totals[3:4] - inverse * totals[1:2])
    level = totals[2:3] - inverse * totals[0:1]
    def resolve(c):
        now = at(c * ROWS, ROWS)
        hat[now] = hat[now] * inverse + ((x[now] - mean) * slant + level)

    each(0, chunks, resolve)
    gather(1)
    share(0)
    gather(2)
    share(1)
    share(2)

    @pl.when(tm < TM - 1)
    def _():
        halo[0].wait_send()
        halo[1].wait_send()

    @pl.when(tm > 0)
    def _():
        halo[2].wait_send()
        halo[3].wait_send()

    finish(0)
    finish(1)
    finish(2)


def unpack_kernel(
    hat, early, late, last, grad, conv, bias, res, skip, out, into, gain, shift, store_sem
):
    store = pltpu.make_async_copy(hat, grad, store_sem)
    store.start()
    for layer, src in ((0, late), (1, early)):
        for tap in range(2):
            for half in range(2):
                conv[layer, tap, :, half * 128 : half * 128 + 128] = src[
                    pl.ds(half * 256 + tap * 128, 128)
                ].astype(jnp.float32)
    for layer in range(2):
        for half in range(2):
            skip[layer, :, half * 128 : half * 128 + 128] = early[
                pl.ds(512 + half * 256 + layer * 128, 128)
            ].astype(jnp.float32)
            bias[layer : layer + 1, half * 128 : half * 128 + 128] = last[
                pl.ds(20 + layer * 16 + half * 8, 1)
            ]
    out[...] = late[640:896].astype(jnp.float32)
    res[...] = late[512:640].astype(jnp.float32)
    for p in range(PARTS):
        into[4 * p : 4 * p + 4] = last[8 * p : 8 * p + 4]
    gain[...] = last[4:5]
    shift[...] = last[12:13]
    store.wait()


def on_device(
    series_data,
    cotangent,
    in_weight,
    convolution_weight,
    convolution_bias,
    res_weight,
    skip_weight,
    output_weight,
    norm_gain_vector,
    norm_offset_vector,
):
    steps = series_data.shape[1]
    f32, bf16 = jnp.float32, jnp.bfloat16
    vmem = pl.BlockSpec(memory_space=pltpu.VMEM)
    hbm = pl.BlockSpec(memory_space=pltpu.HBM)
    sem = pltpu.SemaphoreType.DMA
    shape = jax.ShapeDtypeStruct
    field = pltpu.VMEM((steps, 128), f32)

    sizes = (EARLY, LATE, LAST)
    wires = (bf16, bf16, f32)

    def slots(lead):
        return [pltpu.VMEM((lead, n, 128), wire) for n, wire in zip(sizes, wires)]

    def blocks(count):
        return [pltpu.VMEM((count * n, 128), wire) for n, wire in zip(sizes, wires)]

    def wide_blocks(count):
        return [pltpu.VMEM((count * n, 128), f32) for n in sizes]

    hat, early, late, last = pl.pallas_call(
        block_kernel,
        name="block",
        out_shape=(
            pltpu.VMEM((steps, 128), f32),
            *blocks(PARTS),
        ),
        in_specs=[hbm] * 10,
        out_specs=(vmem,) * 4,
        scratch_shapes=[
            pltpu.VMEM((128, 128), bf16),
            pltpu.VMEM((2, 256, 256), bf16),
            pltpu.VMEM((2, 256), f32),
            pltpu.VMEM((128, 128), bf16),
            pltpu.VMEM((256, 256), bf16),
            pltpu.VMEM((256, 128), bf16),
            pltpu.VMEM((1, 128), f32),
            pltpu.VMEM((1, 128), f32),
            field,
            field,
            pltpu.VMEM((steps + FIRST, 128), bf16),
            pltpu.VMEM((steps + SECOND, 128), bf16),
            pltpu.VMEM((steps, 128), bf16),
            field,
            field,
            field,
            field,
            field,
            field,
            field,
            pltpu.VMEM((SECOND, 128), bf16),
            pltpu.VMEM((SECOND, 128), bf16),
            pltpu.VMEM((FIRST, 128), bf16),
            pltpu.VMEM((FIRST, 128), bf16),
            *wide_blocks(PARTS),
            pltpu.VMEM((128, 128), f32),
            pltpu.VMEM((10, 8, 128), f32),
            pltpu.VMEM((2, 128), f32),
            pltpu.VMEM((Z, 2, 128), f32),
            pltpu.VMEM((X, 2, 128), f32),
            pltpu.VMEM((4, 128), f32),
            pltpu.VMEM((Z, 4, 128), f32),
            pltpu.VMEM((X, 4, 128), f32),
            *blocks(PLANE)[:2],
            *wide_blocks(PLANE)[:2],
            *blocks(PLANE)[:2],
            *slots(PLANE)[:2],
            pltpu.VMEM((PARTS, LAST, 128), f32),
            *slots(Z),
            *blocks(1),
            sem((steps // ROWS + 9,)),
            sem((4,)),
            sem((4,)),
            sem((4,)),
            sem((4,)),
            *[sem((3,))] * 10,
        ],
        compiler_params=pltpu.CompilerParams(
            collective_id=0, has_side_effects=True, vmem_limit_bytes=56 * 1024 * 1024
        ),
    )(
        series_data[0],
        cotangent[0],
        in_weight,
        convolution_weight.reshape(2, 256, 256),
        convolution_bias,
        res_weight,
        skip_weight.reshape(256, 256),
        output_weight,
        norm_gain_vector.reshape(1, 128),
        norm_offset_vector.reshape(1, 128),
    )
    grad, conv, bias, res, skip, out, into, gain, shift = pl.pallas_call(
        unpack_kernel,
        name="unpack",
        out_shape=(
            shape((steps, 128), f32),
            shape((2, 2, 128, 256), f32),
            shape((2, 256), f32),
            shape((128, 128), f32),
            shape((2, 128, 256), f32),
            shape((256, 128), f32),
            shape((128, 128), f32),
            shape((1, 128), f32),
            shape((1, 128), f32),
        ),
        in_specs=[vmem] * 4,
        out_specs=(hbm,) + (vmem,) * 8,
        scratch_shapes=[sem],
        compiler_params=pltpu.CompilerParams(vmem_limit_bytes=8 * 1024 * 1024),
    )(hat, early, late, last)
    return grad[None], conv, bias, res, skip, out, into, gain.reshape(128), shift.reshape(128)


def solution(mesh):
    split = P("series", "tm", None)
    return jax.shard_map(
        on_device,
        mesh=mesh,
        in_specs=(split, split) + (P(),) * 8,
        out_specs=(split,) + (P(),) * 8,
        check_vma=False,
    )
```

```python
import jax
import jax.numpy as jnp
from jax import lax
from jax.experimental import pallas as pl
from jax.experimental.pallas import tpu as pltpu
from jax.sharding import PartitionSpec as P

FIRST = 256
SECOND = 512
TM = 32
SER = 8
X = 4
Z = 8
Y = 4
PLANE = X * Y
PARTS = 2 * PLANE
ROWS = 1024
MESH = pl.DeviceIdType.MESH
EARLY, LATE, LAST = 32, 32, 8

epsilon = 1e-05
gelu_coeff = 0.7978845608
cubic_coeff = 0.044715


def nn(left, right):
    return jnp.dot(left, right, preferred_element_type=jnp.float32)


def nt(left, right):
    return lax.dot_general(
        left, right, (((1,), (1,)), ((), ())), preferred_element_type=jnp.float32
    )


def tn(left, right):
    return lax.dot_general(
        left, right, (((0,), (0,)), ((), ())), preferred_element_type=jnp.float32
    )


def fold(values):
    return jnp.sum(values.reshape(-1, 8, values.shape[-1]), axis=0)


def each(lo, hi, body):
    def run(k, carry):
        body(k)
        return carry

    lax.fori_loop(lo, hi, run, 0)


def at(start, size):
    return pl.ds(pl.multiple_of(start, 8), size)


def remote(src, dst, s_sem, r_sem, device):
    return pltpu.make_async_remote_copy(
        src_ref=src,
        dst_ref=dst,
        send_sem=s_sem,
        recv_sem=r_sem,
        device_id=device,
        device_id_type=MESH,
    )


def block_kernel(
    x_hbm,
    cot_hbm,
    w_in_hbm,
    w_conv_hbm,
    bias_hbm,
    w_res_hbm,
    w_skip_hbm,
    w_out_hbm,
    gain_hbm,
    offset_hbm,
    hat,
    early_out,
    late_out,
    last_out,
    w_in,
    w_conv,
    bias,
    w_res,
    w_skip,
    w_out,
    gain_ref,
    offset_ref,
    x,
    cot,
    level_zero,
    level_one,
    gated_one,
    tanh_one,
    sigm_one,
    incoming_one,
    near_one,
    far_one,
    near_zero,
    far_zero,
    far_one_head,
    far_one_tail,
    far_zero_head,
    far_zero_tail,
    early,
    late,
    last,
    in_grad,
    acc,
    pieces,
    stats,
    stats_all,
    ends,
    ends_z,
    ends_x,
    early_pair,
    late_pair,
    early_half,
    late_half,
    early_send,
    late_send,
    early_one,
    late_one,
    last_one,
    early_two,
    late_two,
    last_two,
    early_block,
    late_block,
    last_block,
    load_sem,
    halo_s,
    halo_r,
    line_s,
    line_r,
    pair_s,
    pair_r,
    one_s,
    one_r,
    two_s,
    two_r,
    three_s,
    three_r,
    back_s,
    back_r,
):
    steps = x.shape[0]
    chunks = steps // ROWS
    total_steps = float(steps * TM)
    ser = lax.axis_index("series")
    tm = lax.axis_index("tm")
    across, depth = tm // Z, lax.rem(tm, Z)
    up, core = ser // 2, lax.rem(ser, 2)
    mine = across * Y + up
    mate = {"series": ser + 1 - 2 * core}

    def on_z(peer):
        return {"tm": across * Z + peer}

    def on_x(peer):
        return {"tm": peer * Z + depth}

    def on_plane(peer):
        return {"series": lax.rem(peer, Y) * 2 + core, "tm": (peer // Y) * Z + depth}

    def load_x(c):
        return pltpu.make_async_copy(
            x_hbm.at[at(c * ROWS, ROWS)], x.at[at(c * ROWS, ROWS)], load_sem.at[c]
        )

    load_cot = pltpu.make_async_copy(cot_hbm, cot, load_sem.at[chunks])
    each(0, chunks, lambda c: load_x(c).start())
    load_cot.start()
    params = [
        pltpu.make_async_copy(src, dst, load_sem.at[chunks + 1 + k])
        for k, (src, dst) in enumerate(
            (
                (w_in_hbm, w_in),
                (w_conv_hbm, w_conv),
                (bias_hbm, bias),
                (w_res_hbm, w_res),
                (w_skip_hbm, w_skip),
                (w_out_hbm, w_out),
                (gain_hbm, gain_ref),
                (offset_hbm, offset_ref),
            )
        )
    ]
    for copy in params:
        copy.start()

    barrier = pltpu.get_barrier_semaphore()

    def hello(device):
        pl.semaphore_signal(barrier, inc=1, device_id=device, device_id_type=MESH)

    for k in range(1, TM):
        hello({"tm": lax.rem(tm + k, TM)})
    for k in range(1, Y):
        hello({"series": lax.rem(up + k, Y) * 2 + core})
    hello(mate)

    acc[...] = jnp.zeros_like(acc)
    early[...] = jnp.zeros_like(early)
    late[...] = jnp.zeros_like(late)
    last[...] = jnp.zeros_like(last)
    in_grad[...] = jnp.zeros_like(in_grad)

    @pl.when(tm == 0)
    def _():
        level_zero[pl.ds(0, FIRST)] = jnp.zeros((FIRST, 128), jnp.bfloat16)
        level_one[pl.ds(0, SECOND)] = jnp.zeros((SECOND, 128), jnp.bfloat16)

    @pl.when(tm == TM - 1)
    def _():
        far_one_tail[...] = jnp.zeros_like(far_one_tail)
        far_zero_tail[...] = jnp.zeros_like(far_zero_tail)

    def combine(slots, count):
        sums = slots[:, 0]
        total = jnp.sum(sums, axis=0, keepdims=True)
        shift = sums / count - total / (count * slots.shape[0])
        squares = slots[:, 1] + count * (shift * shift)
        return total, jnp.sum(squares, axis=0, keepdims=True)

    def sum_x(c):
        load_x(c).wait()
        values = x[at(c * ROWS, ROWS)]
        total = jnp.sum(fold(values), axis=0, keepdims=True)
        centred = values - total / ROWS
        squares = jnp.sum(fold(centred * centred), axis=0, keepdims=True)
        pieces[pl.ds(c, 1), 0:1] = total[None]
        pieces[pl.ds(c, 1), 1:2] = squares[None]

    each(0, chunks, sum_x)
    total, squares = combine(pieces, float(ROWS))
    stats[0:1] = total
    stats[1:2] = squares
    pl.semaphore_wait(barrier, TM + Y - 1)

    def line(which, own, slots, count, me, device):
        def copy(peer, slot):
            return remote(own, slots.at[slot], line_s.at[which], line_r.at[which], device(peer))

        rest = slots.at[pl.ds(0, count - 1)]
        whole = remote(rest, rest, line_s.at[which], line_r.at[which], device(me))
        for k in range(1, count):
            copy(lax.rem(me + k, count), me).start()
        slots[pl.ds(me, 1)] = own[...][None]
        return whole

    line(0, stats, stats_all, TM, tm, lambda peer: {"tm": peer}).wait()
    total, squares = combine(stats_all, float(steps))
    mean = total / total_steps
    variance = squares / total_steps
    inverse = lax.rsqrt(variance + epsilon)
    spread = jnp.sqrt(variance + epsilon)
    for copy in params:
        copy.wait()
    gain, offset = gain_ref[...], offset_ref[...]
    scale = spread / gain

    later, earlier = {"tm": lax.rem(tm + 1, TM)}, {"tm": lax.rem(tm + TM - 1, TM)}
    halo = (
        remote(
            level_zero.at[pl.ds(steps, FIRST)],
            level_zero.at[pl.ds(0, FIRST)],
            halo_s.at[0],
            halo_r.at[0],
            later,
        ),
        remote(
            level_one.at[pl.ds(steps, SECOND)],
            level_one.at[pl.ds(0, SECOND)],
            halo_s.at[1],
            halo_r.at[1],
            later,
        ),
        remote(
            far_one_head,
            far_one_tail,
            halo_s.at[2],
            halo_r.at[2],
            earlier,
        ),
        remote(
            far_zero_head,
            far_zero_tail,
            halo_s.at[3],
            halo_r.at[3],
            earlier,
        ),
    )

    has_later, has_earlier = tm < TM - 1, tm > 0

    def normalize(start, size):
        hat_x = (x[pl.ds(start, size)] - mean) * inverse
        return hat_x, (hat_x * gain + offset).astype(jnp.bfloat16)

    def project(start, size):
        _, normed = normalize(start, size)
        level_zero[pl.ds(FIRST + start, size)] = nn(normed, w_in[...]).astype(jnp.bfloat16)

    def gates(act):
        return jnp.tanh(act[:, :128]), 0.5 * jnp.tanh(0.5 * act[:, 128:]) + 0.5

    def window_zero(start, size):
        return jnp.concatenate(
            [level_zero[pl.ds(start, size)], level_zero[pl.ds(start + FIRST, size)]], axis=1
        )

    def window_one(start, size):
        return jnp.concatenate(
            [level_one[pl.ds(start, size)], level_one[pl.ds(start + SECOND, size)]], axis=1
        )

    def layer_one(start, size):
        now = pl.ds(start, size)
        tanh, sigm = gates(nn(window_zero(start, size), w_conv[0]) + bias[0:1])
        gated = (tanh * sigm).astype(jnp.bfloat16)
        tanh_one[now] = tanh
        sigm_one[now] = sigm
        gated_one[now] = gated
        level = level_zero[pl.ds(start + FIRST, size)].astype(jnp.float32)
        level_one[pl.ds(start + SECOND, size)] = (level + nn(gated, w_res[...])).astype(
            jnp.bfloat16
        )

    project(steps - SECOND - FIRST, SECOND + FIRST)
    pl.when(has_later)(halo[0].start)
    layer_one(steps - SECOND, SECOND)
    pl.when(has_later)(halo[1].start)
    project(0, steps - SECOND - FIRST)
    layer_one(SECOND, steps - 2 * SECOND)

    def gate_back(incoming, tanh, sigm):
        part = incoming * sigm
        return part * (1.0 - tanh * tanh), part * tanh * (1.0 - sigm)

    load_cot.wait()

    def layer_two(start, size):
        now = pl.ds(start, size)
        window = window_one(start, size)
        tanh, sigm = gates(nn(window, w_conv[1]) + bias[1:2])
        gated = (tanh * sigm).astype(jnp.bfloat16)
        both = jnp.concatenate([gated_one[now], gated], axis=1)
        skip = nn(both, w_skip[...])
        square = skip * skip
        half = 0.5 * jnp.tanh(
            skip * (gelu_coeff + (gelu_coeff * cubic_coeff) * square)
        ) + 0.5
        value = skip * half
        slope = half + value * (1.0 - half) * (
            2.0 * gelu_coeff + (6.0 * gelu_coeff * cubic_coeff) * square
        )
        rectified = value.astype(jnp.bfloat16)
        forecast = nn(rectified, w_out[...])
        gradient = cot[now]
        acc[2] += fold(gradient)
        acc[3] += fold(gradient * (forecast - offset))
        scaled = (gradient * scale).astype(jnp.bfloat16)
        out_part = tn(rectified, scaled)
        late[640:896] += out_part
        back_skip = (nt(scaled, w_out[...]) * slope).astype(jnp.bfloat16)
        skip_part = tn(both, back_skip)
        early[512:768] += skip_part[:, :128]
        early[768:1024] += skip_part[:, 128:]
        incoming = nt(back_skip, w_skip[...])
        incoming_one[now] = incoming[:, :128]
        first, second = gate_back(incoming[:, 128:], tanh, sigm)
        acc[4] += fold(first)
        acc[5] += fold(second)
        pre = jnp.concatenate([first, second], axis=1).astype(jnp.bfloat16)
        conv_part = tn(window, pre)
        early[0:256] += conv_part[:, :128]
        early[256:512] += conv_part[:, 128:]
        carried = nt(pre, w_conv[1])
        far_one[now] = carried[:, :128]
        near_one[now] = carried[:, 128:]

    layer_two(5 * SECOND, steps - 5 * SECOND)
    pl.when(has_earlier)(halo[0].wait_recv)
    layer_one(0, SECOND)
    pl.when(has_earlier)(halo[1].wait_recv)
    layer_two(0, SECOND)
    far_one_head[...] = far_one[pl.ds(0, SECOND)].astype(jnp.bfloat16)
    pl.when(has_earlier)(halo[2].start)
    layer_two(SECOND, 4 * SECOND)

    groups = (
        (early, early_pair, early_half, early_one, early_block, early_two, early_out, EARLY),
        (late, late_pair, late_half, late_one, late_block, late_two, late_out, LATE),
        (last, None, None, last_one, last_block, last_two, last_out, LAST),
    )
    sends = (early_send, late_send)

    def pair(g):
        return remote(sends[g], groups[g][1], pair_s.at[g], pair_r.at[g], mate)

    def one(g, k):
        got, size = groups[g][3], groups[g][7]
        peer = lax.rem(mine + k, PLANE)
        return remote(
            sends[g].at[at(peer * size, size)],
            got.at[k],
            one_s.at[g],
            one_r.at[g],
            on_plane(peer),
        )

    def two(g, k):
        block, got = groups[g][4], groups[g][5]
        peer = lax.rem(depth + k, Z)
        return remote(block, got.at[depth], two_s.at[g], two_r.at[g], on_z(peer))

    def three(g, k):
        out, size = groups[g][6], groups[g][7]
        where = out.at[at(owner * size, size)]
        peer = lax.rem(mine + k, PLANE)
        return remote(where, where, three_s.at[g], three_r.at[g], on_plane(peer))

    def back(g):
        out, size = groups[g][6], groups[g][7] * PLANE
        where = out.at[at(core * size, size)]
        return remote(where, where, back_s.at[g], back_r.at[g], mate)

    def whole(g, ref, count, s_sem, r_sem):
        rest = ref.at[pl.ds(0, count)]
        return remote(rest, rest, s_sem.at[g], r_sem.at[g], mate)

    owner = core * PLANE + mine

    def on_owner(p):
        member = lax.rem(p, PLANE)
        return {
            "series": lax.rem(member, Y) * 2 + p // PLANE,
            "tm": (member // Y) * Z + depth,
        }

    def last_one_copy(k):
        peer = lax.rem(owner + k, PARTS)
        return remote(
            last.at[at(peer * LAST, LAST)], last_one.at[k], one_s.at[2], one_r.at[2], on_owner(peer)
        )

    def last_three_copy(k):
        where = last_out.at[at(owner * LAST, LAST)]
        peer = lax.rem(owner + k, PARTS)
        return remote(where, where, three_s.at[2], three_r.at[2], on_owner(peer))

    def all_one(g):
        return whole(g, groups[g][3], groups[g][3].shape[0] - 1, one_s, one_r)

    def all_two(g):
        return whole(g, groups[g][5], Z - 1, two_s, two_r)

    def all_three(g):
        peers = (PARTS if g == 2 else PLANE) - 1
        return whole(g, groups[g][6], peers * groups[g][7], three_s, three_r)

    def wide(values):
        return values.astype(jnp.float32)

    def start(g):
        src, size = groups[g][0], groups[g][7] * PLANE
        sends[g][...] = src[at((1 - core) * size, size)].astype(sends[g].dtype)
        pair(g).start()

    def scatter(g):
        src, got, half, slots, _, _, _, size = groups[g]
        pair(g).wait()
        total = src[at(core * PLANE * size, PLANE * size)] + wide(got[...])
        half[...] = total
        sends[g][...] = total.astype(sends[g].dtype)
        each(1, PLANE, lambda k: one(g, k).start())

    def middle(g):
        _, _, half, slots, block, far, _, size = groups[g]
        all_one(g).wait_recv()
        total = last[at(owner * size, size)] if g == 2 else half[at(mine * size, size)]
        for p in range(1, slots.shape[0]):
            total = total + wide(slots[p])
        block[...] = total.astype(block.dtype)
        each(1, Z, lambda k: two(g, k).start())
        far[pl.ds(depth, 1)] = block[...][None]

    def gather(g):
        _, _, _, _, _, far, out, size = groups[g]
        all_two(g).wait_recv()
        total = wide(far[0])
        for z in range(1, Z):
            total = total + wide(far[z])
        out[at(owner * size, size)] = total.astype(out.dtype)
        if g == 2:
            each(1, PARTS, lambda k: last_three_copy(k).start())
        else:
            each(1, PLANE, lambda k: three(g, k).start())

    def share(g):
        all_three(g).wait_recv()
        if g < 2:
            back(g).start()

    def finish(g):
        if g < 2:
            back(g).wait()
        all_one(g).wait_send()
        all_two(g).wait_send()
        all_three(g).wait_send()

    start(0)

    def back_one(start, size):
        now = pl.ds(start, size)
        last_rows = start + size == steps
        far = wide(far_one_tail[...]) if last_rows else far_one[pl.ds(start + SECOND, size)]
        grad_one = (near_one[now] + far).astype(jnp.bfloat16)
        late[512:640] += tn(gated_one[now], grad_one)
        incoming = incoming_one[now] + nt(grad_one, w_res[...])
        first, second = gate_back(incoming, tanh_one[now], sigm_one[now])
        acc[6] += fold(first)
        acc[7] += fold(second)
        pre = jnp.concatenate([first, second], axis=1).astype(jnp.bfloat16)
        conv_part = tn(window_zero(start, size), pre)
        late[0:256] += conv_part[:, :128]
        late[256:512] += conv_part[:, 128:]
        carried = nt(pre, w_conv[0])
        far_zero[now] = carried[:, :128]
        near_zero[now] = grad_one.astype(jnp.float32) + carried[:, 128:]

    back_one(0, SECOND)
    far_zero_head[...] = far_zero[pl.ds(0, FIRST)].astype(jnp.bfloat16)
    pl.when(has_earlier)(halo[3].start)
    back_one(SECOND, steps // 2 - SECOND)
    scatter(0)
    back_one(steps // 2, steps // 2 - SECOND)
    pl.when(has_later)(halo[2].wait_recv)
    back_one(steps - SECOND, SECOND)
    start(1)

    def back_zero(start, size):
        now = pl.ds(start, size)
        if start + size == steps:
            far = jnp.concatenate(
                [far_zero[pl.ds(start + FIRST, size - FIRST)], wide(far_zero_tail[...])], axis=0
            )
        else:
            far = far_zero[pl.ds(start + FIRST, size)]
        grad_zero = (near_zero[now] + far).astype(jnp.bfloat16)
        hat_x, normed = normalize(start, size)
        in_grad[...] += tn(normed, grad_zero)
        grad_hat = nt(grad_zero, w_in[...]) * gain
        hat[now] = grad_hat
        acc[8] += fold(grad_hat)
        acc[9] += fold(grad_hat * hat_x)

    back_zero(0, steps - SECOND)
    pl.when(has_later)(halo[3].wait_recv)
    back_zero(steps - SECOND, SECOND)
    scatter(1)

    def column(k):
        return jnp.sum(acc[k], axis=0, keepdims=True)

    sum_a, sum_b, out_a, out_b = column(8), column(9), column(2), column(3) / gain
    ends[0:1] = sum_a
    ends[1:2] = sum_b
    ends[2:3] = out_a
    ends[3:4] = out_b
    ends_line = line(2, ends, ends_z, Z, depth, on_z)
    for p in range(PARTS):
        last[8 * p : 8 * p + 4] = in_grad[4 * p : 4 * p + 4]
    last[4:5] = (sum_b - out_b * spread) / gain
    last[12:13] = (sum_a - out_a * spread) / gain
    last[20:21] = column(6)
    last[28:29] = column(7)
    last[36:37] = column(4)
    last[44:45] = column(5)
    each(1, PARTS, lambda k: last_one_copy(k).start())
    middle(0)
    ends_line.wait()
    ends[...] = jnp.sum(ends_z[...], axis=0)
    ends_line = line(3, ends, ends_x, X, across, on_x)
    middle(1)
    middle(2)
    gather(0)
    ends_line.wait()
    totals = jnp.sum(ends_x[...], axis=0) / total_steps
    slant = inverse * (totals[3:4] - inverse * totals[1:2])
    level = totals[2:3] - inverse * totals[0:1]
    def resolve(c):
        now = at(c * ROWS, ROWS)
        hat[now] = hat[now] * inverse + ((x[now] - mean) * slant + level)

    each(0, chunks, resolve)
    gather(1)
    gather(2)
    share(0)
    share(1)
    share(2)

    @pl.when(tm < TM - 1)
    def _():
        halo[0].wait_send()
        halo[1].wait_send()

    @pl.when(tm > 0)
    def _():
        halo[2].wait_send()
        halo[3].wait_send()

    finish(0)
    finish(1)
    finish(2)


def unpack_kernel(
    hat, early, late, last, grad, conv, bias, res, skip, out, into, gain, shift, store_sem
):
    store = pltpu.make_async_copy(hat, grad, store_sem)
    store.start()
    for layer, src in ((0, late), (1, early)):
        for tap in range(2):
            for half in range(2):
                conv[layer, tap, :, half * 128 : half * 128 + 128] = src[
                    pl.ds(half * 256 + tap * 128, 128)
                ].astype(jnp.float32)
    for layer in range(2):
        for half in range(2):
            skip[layer, :, half * 128 : half * 128 + 128] = early[
                pl.ds(512 + half * 256 + layer * 128, 128)
            ].astype(jnp.float32)
            bias[layer : layer + 1, half * 128 : half * 128 + 128] = last[
                pl.ds(20 + layer * 16 + half * 8, 1)
            ]
    out[...] = late[640:896].astype(jnp.float32)
    res[...] = late[512:640].astype(jnp.float32)
    for p in range(PARTS):
        into[4 * p : 4 * p + 4] = last[8 * p : 8 * p + 4]
    gain[...] = last[4:5]
    shift[...] = last[12:13]
    store.wait()


def on_device(
    series_data,
    cotangent,
    in_weight,
    convolution_weight,
    convolution_bias,
    res_weight,
    skip_weight,
    output_weight,
    norm_gain_vector,
    norm_offset_vector,
):
    steps = series_data.shape[1]
    f32, bf16 = jnp.float32, jnp.bfloat16
    vmem = pl.BlockSpec(memory_space=pltpu.VMEM)
    hbm = pl.BlockSpec(memory_space=pltpu.HBM)
    sem = pltpu.SemaphoreType.DMA
    shape = jax.ShapeDtypeStruct
    field = pltpu.VMEM((steps, 128), f32)

    sizes = (EARLY, LATE, LAST)
    wires = (bf16, bf16, f32)

    def slots(lead):
        return [pltpu.VMEM((lead, n, 128), wire) for n, wire in zip(sizes, wires)]

    def blocks(count):
        return [pltpu.VMEM((count * n, 128), wire) for n, wire in zip(sizes, wires)]

    def wide_blocks(count):
        return [pltpu.VMEM((count * n, 128), f32) for n in sizes]

    hat, early, late, last = pl.pallas_call(
        block_kernel,
        name="block",
        out_shape=(
            pltpu.VMEM((steps, 128), f32),
            *blocks(PARTS),
        ),
        in_specs=[hbm] * 10,
        out_specs=(vmem,) * 4,
        scratch_shapes=[
            pltpu.VMEM((128, 128), bf16),
            pltpu.VMEM((2, 256, 256), bf16),
            pltpu.VMEM((2, 256), f32),
            pltpu.VMEM((128, 128), bf16),
            pltpu.VMEM((256, 256), bf16),
            pltpu.VMEM((256, 128), bf16),
            pltpu.VMEM((1, 128), f32),
            pltpu.VMEM((1, 128), f32),
            field,
            field,
            pltpu.VMEM((steps + FIRST, 128), bf16),
            pltpu.VMEM((steps + SECOND, 128), bf16),
            pltpu.VMEM((steps, 128), bf16),
            field,
            field,
            field,
            field,
            field,
            field,
            field,
            pltpu.VMEM((SECOND, 128), bf16),
            pltpu.VMEM((SECOND, 128), bf16),
            pltpu.VMEM((FIRST, 128), bf16),
            pltpu.VMEM((FIRST, 128), bf16),
            *wide_blocks(PARTS),
            pltpu.VMEM((128, 128), f32),
            pltpu.VMEM((10, 8, 128), f32),
            pltpu.VMEM((steps // ROWS, 2, 128), f32),
            pltpu.VMEM((2, 128), f32),
            pltpu.VMEM((TM, 2, 128), f32),
            pltpu.VMEM((4, 128), f32),
            pltpu.VMEM((Z, 4, 128), f32),
            pltpu.VMEM((X, 4, 128), f32),
            *blocks(PLANE)[:2],
            *wide_blocks(PLANE)[:2],
            *blocks(PLANE)[:2],
            *slots(PLANE)[:2],
            pltpu.VMEM((PARTS, LAST, 128), f32),
            *slots(Z),
            *blocks(1),
            sem((steps // ROWS + 9,)),
            sem((4,)),
            sem((4,)),
            sem((4,)),
            sem((4,)),
            *[sem((3,))] * 10,
        ],
        compiler_params=pltpu.CompilerParams(
            collective_id=0, has_side_effects=True, vmem_limit_bytes=56 * 1024 * 1024
        ),
    )(
        series_data[0],
        cotangent[0],
        in_weight,
        convolution_weight.reshape(2, 256, 256),
        convolution_bias,
        res_weight,
        skip_weight.reshape(256, 256),
        output_weight,
        norm_gain_vector.reshape(1, 128),
        norm_offset_vector.reshape(1, 128),
    )
    grad, conv, bias, res, skip, out, into, gain, shift = pl.pallas_call(
        unpack_kernel,
        name="unpack",
        out_shape=(
            shape((steps, 128), f32),
            shape((2, 2, 128, 256), f32),
            shape((2, 256), f32),
            shape((128, 128), f32),
            shape((2, 128, 256), f32),
            shape((256, 128), f32),
            shape((128, 128), f32),
            shape((1, 128), f32),
            shape((1, 128), f32),
        ),
        in_specs=[vmem] * 4,
        out_specs=(hbm,) + (vmem,) * 8,
        scratch_shapes=[sem],
        compiler_params=pltpu.CompilerParams(vmem_limit_bytes=8 * 1024 * 1024),
    )(hat, early, late, last)
    return grad[None], conv, bias, res, skip, out, into, gain.reshape(128), shift.reshape(128)


def solution(mesh):
    split = P("series", "tm", None)
    return jax.shard_map(
        on_device,
        mesh=mesh,
        in_specs=(split, split) + (P(),) * 8,
        out_specs=(split,) + (P(),) * 8,
        check_vma=False,
    )
```

```python
import jax
import jax.numpy as jnp
from jax import lax
from jax.experimental import pallas as pl
from jax.experimental.pallas import tpu as pltpu
from jax.sharding import PartitionSpec as P

FIRST = 256
SECOND = 512
TM = 32
SER = 8
X = 4
Z = 8
Y = 4
PLANE = X * Y
PARTS = 2 * PLANE
ROWS = 1024
MESH = pl.DeviceIdType.MESH
EARLY, LATE, LAST = 32, 32, 8

epsilon = 1e-05
gelu_coeff = 0.7978845608
cubic_coeff = 0.044715


def nn(left, right):
    return jnp.dot(left, right, preferred_element_type=jnp.float32)


def nt(left, right):
    return lax.dot_general(
        left, right, (((1,), (1,)), ((), ())), preferred_element_type=jnp.float32
    )


def tn(left, right):
    return lax.dot_general(
        left, right, (((0,), (0,)), ((), ())), preferred_element_type=jnp.float32
    )


def fold(values):
    return jnp.sum(values.reshape(-1, 8, values.shape[-1]), axis=0)


def each(lo, hi, body):
    def run(k, carry):
        body(k)
        return carry

    lax.fori_loop(lo, hi, run, 0)


def at(start, size):
    return pl.ds(pl.multiple_of(start, 8), size)


def remote(src, dst, s_sem, r_sem, device):
    return pltpu.make_async_remote_copy(
        src_ref=src,
        dst_ref=dst,
        send_sem=s_sem,
        recv_sem=r_sem,
        device_id=device,
        device_id_type=MESH,
    )


def block_kernel(
    x_hbm,
    cot_hbm,
    w_in_hbm,
    w_conv_hbm,
    bias_hbm,
    w_res_hbm,
    w_skip_hbm,
    w_out_hbm,
    gain_hbm,
    offset_hbm,
    hat,
    early_out,
    late_out,
    last_out,
    w_in,
    w_conv,
    bias,
    w_res,
    w_skip,
    w_out,
    gain_ref,
    offset_ref,
    x,
    cot,
    level_zero,
    level_one,
    gated_one,
    tanh_one,
    sigm_one,
    incoming_one,
    near_one,
    far_one,
    near_zero,
    far_zero,
    far_one_head,
    far_one_tail,
    far_zero_head,
    far_zero_tail,
    early,
    late,
    last,
    in_grad,
    acc,
    pieces,
    stats,
    stats_all,
    ends,
    ends_z,
    ends_x,
    early_pair,
    late_pair,
    early_half,
    late_half,
    early_send,
    late_send,
    early_one,
    late_one,
    last_one,
    early_two,
    late_two,
    last_two,
    early_block,
    late_block,
    last_block,
    load_sem,
    halo_s,
    halo_r,
    line_s,
    line_r,
    pair_s,
    pair_r,
    one_s,
    one_r,
    two_s,
    two_r,
    three_s,
    three_r,
    back_s,
    back_r,
):
    steps = x.shape[0]
    chunks = steps // ROWS
    total_steps = float(steps * TM)
    ser = lax.axis_index("series")
    tm = lax.axis_index("tm")
    across, depth = tm // Z, lax.rem(tm, Z)
    up, core = ser // 2, lax.rem(ser, 2)
    mine = across * Y + up
    mate = {"series": ser + 1 - 2 * core}

    def on_z(peer):
        return {"tm": across * Z + peer}

    def on_x(peer):
        return {"tm": peer * Z + depth}

    def on_plane(peer):
        return {"series": lax.rem(peer, Y) * 2 + core, "tm": (peer // Y) * Z + depth}

    def load_x(c):
        return pltpu.make_async_copy(
            x_hbm.at[at(c * ROWS, ROWS)], x.at[at(c * ROWS, ROWS)], load_sem.at[c]
        )

    load_cot = pltpu.make_async_copy(cot_hbm, cot, load_sem.at[chunks])
    each(0, chunks, lambda c: load_x(c).start())
    load_cot.start()
    params = [
        pltpu.make_async_copy(src, dst, load_sem.at[chunks + 1 + k])
        for k, (src, dst) in enumerate(
            (
                (w_in_hbm, w_in),
                (w_conv_hbm, w_conv),
                (bias_hbm, bias),
                (w_res_hbm, w_res),
                (w_skip_hbm, w_skip),
                (w_out_hbm, w_out),
                (gain_hbm, gain_ref),
                (offset_hbm, offset_ref),
            )
        )
    ]
    for copy in params:
        copy.start()

    barrier = pltpu.get_barrier_semaphore()

    def hello(device):
        pl.semaphore_signal(barrier, inc=1, device_id=device, device_id_type=MESH)

    for k in range(1, TM):
        hello({"tm": lax.rem(tm + k, TM)})
    for k in range(1, Y):
        hello({"series": lax.rem(up + k, Y) * 2 + core})
    hello(mate)

    acc[...] = jnp.zeros_like(acc)
    early[...] = jnp.zeros_like(early)
    late[...] = jnp.zeros_like(late)
    last[...] = jnp.zeros_like(last)
    in_grad[...] = jnp.zeros_like(in_grad)

    @pl.when(tm == 0)
    def _():
        level_zero[pl.ds(0, FIRST)] = jnp.zeros((FIRST, 128), jnp.bfloat16)
        level_one[pl.ds(0, SECOND)] = jnp.zeros((SECOND, 128), jnp.bfloat16)

    @pl.when(tm == TM - 1)
    def _():
        far_one_tail[...] = jnp.zeros_like(far_one_tail)
        far_zero_tail[...] = jnp.zeros_like(far_zero_tail)

    def combine(slots, count):
        sums = slots[:, 0]
        total = jnp.sum(sums, axis=0, keepdims=True)
        shift = sums / count - total / (count * slots.shape[0])
        squares = slots[:, 1] + count * (shift * shift)
        return total, jnp.sum(squares, axis=0, keepdims=True)

    def sum_x(c):
        load_x(c).wait()
        values = x[at(c * ROWS, ROWS)]
        total = jnp.sum(fold(values), axis=0, keepdims=True)
        centred = values - total / ROWS
        squares = jnp.sum(fold(centred * centred), axis=0, keepdims=True)
        pieces[pl.ds(c, 1), 0:1] = total[None]
        pieces[pl.ds(c, 1), 1:2] = squares[None]

    each(0, chunks, sum_x)
    total, squares = combine(pieces, float(ROWS))
    stats[0:1] = total
    stats[1:2] = squares
    pl.semaphore_wait(barrier, TM + Y - 1)

    def line(which, own, slots, count, me, device):
        def copy(peer, slot):
            return remote(own, slots.at[slot], line_s.at[which], line_r.at[which], device(peer))

        rest = slots.at[pl.ds(0, count - 1)]
        whole = remote(rest, rest, line_s.at[which], line_r.at[which], device(me))
        for k in range(1, count):
            copy(lax.rem(me + k, count), me).start()
        slots[pl.ds(me, 1)] = own[...][None]
        return whole

    line(0, stats, stats_all, TM, tm, lambda peer: {"tm": peer}).wait()
    total, squares = combine(stats_all, float(steps))
    mean = total / total_steps
    variance = squares / total_steps
    inverse = lax.rsqrt(variance + epsilon)
    spread = jnp.sqrt(variance + epsilon)
    for copy in params:
        copy.wait()
    gain, offset = gain_ref[...], offset_ref[...]
    scale = spread / gain

    later, earlier = {"tm": lax.rem(tm + 1, TM)}, {"tm": lax.rem(tm + TM - 1, TM)}
    halo = (
        remote(
            level_zero.at[pl.ds(steps, FIRST)],
            level_zero.at[pl.ds(0, FIRST)],
            halo_s.at[0],
            halo_r.at[0],
            later,
        ),
        remote(
            level_one.at[pl.ds(steps, SECOND)],
            level_one.at[pl.ds(0, SECOND)],
            halo_s.at[1],
            halo_r.at[1],
            later,
        ),
        remote(
            far_one_head,
            far_one_tail,
            halo_s.at[2],
            halo_r.at[2],
            earlier,
        ),
        remote(
            far_zero_head,
            far_zero_tail,
            halo_s.at[3],
            halo_r.at[3],
            earlier,
        ),
    )

    has_later, has_earlier = tm < TM - 1, tm > 0

    def normalize(start, size):
        hat_x = (x[pl.ds(start, size)] - mean) * inverse
        return hat_x, (hat_x * gain + offset).astype(jnp.bfloat16)

    def project(start, size):
        _, normed = normalize(start, size)
        level_zero[pl.ds(FIRST + start, size)] = nn(normed, w_in[...]).astype(jnp.bfloat16)

    def gates(act):
        return jnp.tanh(act[:, :128]), 0.5 * jnp.tanh(0.5 * act[:, 128:]) + 0.5

    def window_zero(start, size):
        return jnp.concatenate(
            [level_zero[pl.ds(start, size)], level_zero[pl.ds(start + FIRST, size)]], axis=1
        )

    def window_one(start, size):
        return jnp.concatenate(
            [level_one[pl.ds(start, size)], level_one[pl.ds(start + SECOND, size)]], axis=1
        )

    def layer_one(start, size):
        now = pl.ds(start, size)
        tanh, sigm = gates(nn(window_zero(start, size), w_conv[0]) + bias[0:1])
        gated = (tanh * sigm).astype(jnp.bfloat16)
        tanh_one[now] = tanh
        sigm_one[now] = sigm
        gated_one[now] = gated
        level = level_zero[pl.ds(start + FIRST, size)].astype(jnp.float32)
        level_one[pl.ds(start + SECOND, size)] = (level + nn(gated, w_res[...])).astype(
            jnp.bfloat16
        )

    project(steps - SECOND - FIRST, SECOND + FIRST)
    pl.when(has_later)(halo[0].start)
    layer_one(steps - SECOND, SECOND)
    pl.when(has_later)(halo[1].start)
    project(0, steps - SECOND - FIRST)
    layer_one(SECOND, steps - 2 * SECOND)

    def gate_back(incoming, tanh, sigm):
        part = incoming * sigm
        return part * (1.0 - tanh * tanh), part * tanh * (1.0 - sigm)

    load_cot.wait()

    def layer_two(start, size):
        now = pl.ds(start, size)
        window = window_one(start, size)
        tanh, sigm = gates(nn(window, w_conv[1]) + bias[1:2])
        gated = (tanh * sigm).astype(jnp.bfloat16)
        both = jnp.concatenate([gated_one[now], gated], axis=1)
        skip = nn(both, w_skip[...])
        square = skip * skip
        half = 0.5 * jnp.tanh(
            skip * (gelu_coeff + (gelu_coeff * cubic_coeff) * square)
        ) + 0.5
        value = skip * half
        slope = half + value * (1.0 - half) * (
            2.0 * gelu_coeff + (6.0 * gelu_coeff * cubic_coeff) * square
        )
        rectified = value.astype(jnp.bfloat16)
        forecast = nn(rectified, w_out[...])
        gradient = cot[now]
        acc[2] += fold(gradient)
        acc[3] += fold(gradient * (forecast - offset))
        scaled = (gradient * scale).astype(jnp.bfloat16)
        out_part = tn(rectified, scaled)
        late[640:896] += out_part
        back_skip = (nt(scaled, w_out[...]) * slope).astype(jnp.bfloat16)
        skip_part = tn(both, back_skip)
        early[512:768] += skip_part[:, :128]
        early[768:1024] += skip_part[:, 128:]
        incoming = nt(back_skip, w_skip[...])
        incoming_one[now] = incoming[:, :128]
        first, second = gate_back(incoming[:, 128:], tanh, sigm)
        acc[4] += fold(first)
        acc[5] += fold(second)
        pre = jnp.concatenate([first, second], axis=1).astype(jnp.bfloat16)
        conv_part = tn(window, pre)
        early[0:256] += conv_part[:, :128]
        early[256:512] += conv_part[:, 128:]
        carried = nt(pre, w_conv[1])
        far_one[now] = carried[:, :128]
        near_one[now] = carried[:, 128:]

    layer_two(5 * SECOND, steps - 5 * SECOND)
    pl.when(has_earlier)(halo[0].wait_recv)
    layer_one(0, SECOND)
    pl.when(has_earlier)(halo[1].wait_recv)
    layer_two(0, SECOND)
    far_one_head[...] = far_one[pl.ds(0, SECOND)].astype(jnp.bfloat16)
    pl.when(has_earlier)(halo[2].start)
    layer_two(SECOND, 4 * SECOND)

    groups = (
        (early, early_pair, early_half, early_one, early_block, early_two, early_out, EARLY),
        (late, late_pair, late_half, late_one, late_block, late_two, late_out, LATE),
        (last, None, None, last_one, last_block, last_two, last_out, LAST),
    )
    sends = (early_send, late_send)

    def pair(g):
        return remote(sends[g], groups[g][1], pair_s.at[g], pair_r.at[g], mate)

    def one(g, k):
        got, size = groups[g][3], groups[g][7]
        peer = lax.rem(mine + k, PLANE)
        return remote(
            sends[g].at[at(peer * size, size)],
            got.at[k],
            one_s.at[g],
            one_r.at[g],
            on_plane(peer),
        )

    def two(g, k):
        block, got = groups[g][4], groups[g][5]
        peer = lax.rem(depth + k, Z)
        return remote(block, got.at[depth], two_s.at[g], two_r.at[g], on_z(peer))

    def three(g, k):
        out, size = groups[g][6], groups[g][7]
        where = out.at[at(owner * size, size)]
        peer = lax.rem(mine + k, PLANE)
        return remote(where, where, three_s.at[g], three_r.at[g], on_plane(peer))

    def back(g):
        out, size = groups[g][6], groups[g][7] * PLANE
        where = out.at[at(core * size, size)]
        return remote(where, where, back_s.at[g], back_r.at[g], mate)

    def whole(g, ref, count, s_sem, r_sem):
        rest = ref.at[pl.ds(0, count)]
        return remote(rest, rest, s_sem.at[g], r_sem.at[g], mate)

    owner = core * PLANE + mine

    def on_owner(p):
        member = lax.rem(p, PLANE)
        return {
            "series": lax.rem(member, Y) * 2 + p // PLANE,
            "tm": (member // Y) * Z + depth,
        }

    def last_one_copy(k):
        peer = lax.rem(owner + k, PARTS)
        return remote(
            last.at[at(peer * LAST, LAST)], last_one.at[k], one_s.at[2], one_r.at[2], on_owner(peer)
        )

    def last_three_copy(k):
        where = last_out.at[at(owner * LAST, LAST)]
        peer = lax.rem(owner + k, PARTS)
        return remote(where, where, three_s.at[2], three_r.at[2], on_owner(peer))

    def all_one(g):
        return whole(g, groups[g][3], groups[g][3].shape[0] - 1, one_s, one_r)

    def all_two(g):
        return whole(g, groups[g][5], Z - 1, two_s, two_r)

    def all_three(g):
        peers = (PARTS if g == 2 else PLANE) - 1
        return whole(g, groups[g][6], peers * groups[g][7], three_s, three_r)

    def wide(values):
        return values.astype(jnp.float32)

    def start(g):
        src, size = groups[g][0], groups[g][7] * PLANE
        sends[g][...] = src[at((1 - core) * size, size)].astype(sends[g].dtype)
        pair(g).start()

    def scatter(g):
        src, got, half, slots, _, _, _, size = groups[g]
        pair(g).wait()
        total = src[at(core * PLANE * size, PLANE * size)] + wide(got[...])
        half[...] = total
        sends[g][...] = total.astype(sends[g].dtype)
        each(1, PLANE, lambda k: one(g, k).start())

    def middle(g):
        _, _, half, slots, block, far, _, size = groups[g]
        all_one(g).wait_recv()
        total = last[at(owner * size, size)] if g == 2 else half[at(mine * size, size)]
        for p in range(1, slots.shape[0]):
            total = total + wide(slots[p])
        block[...] = total.astype(block.dtype)
        each(1, Z, lambda k: two(g, k).start())
        far[pl.ds(depth, 1)] = block[...][None]

    def gather(g):
        _, _, _, _, _, far, out, size = groups[g]
        all_two(g).wait_recv()
        total = wide(far[0])
        for z in range(1, Z):
            total = total + wide(far[z])
        out[at(owner * size, size)] = total.astype(out.dtype)
        if g == 2:
            each(1, PARTS, lambda k: last_three_copy(k).start())
        else:
            each(1, PLANE, lambda k: three(g, k).start())

    def share(g):
        all_three(g).wait_recv()
        if g < 2:
            back(g).start()

    def finish(g):
        if g < 2:
            back(g).wait()
        all_one(g).wait_send()
        all_two(g).wait_send()
        all_three(g).wait_send()

    start(0)

    def back_one(start, size):
        now = pl.ds(start, size)
        last_rows = start + size == steps
        far = wide(far_one_tail[...]) if last_rows else far_one[pl.ds(start + SECOND, size)]
        grad_one = (near_one[now] + far).astype(jnp.bfloat16)
        late[512:640] += tn(gated_one[now], grad_one)
        incoming = incoming_one[now] + nt(grad_one, w_res[...])
        first, second = gate_back(incoming, tanh_one[now], sigm_one[now])
        acc[6] += fold(first)
        acc[7] += fold(second)
        pre = jnp.concatenate([first, second], axis=1).astype(jnp.bfloat16)
        conv_part = tn(window_zero(start, size), pre)
        late[0:256] += conv_part[:, :128]
        late[256:512] += conv_part[:, 128:]
        carried = nt(pre, w_conv[0])
        far_zero[now] = carried[:, :128]
        near_zero[now] = grad_one.astype(jnp.float32) + carried[:, 128:]

    back_one(0, SECOND)
    far_zero_head[...] = far_zero[pl.ds(0, FIRST)].astype(jnp.bfloat16)
    pl.when(has_earlier)(halo[3].start)
    back_one(SECOND, steps - 2 * SECOND)
    scatter(0)
    pl.when(has_later)(halo[2].wait_recv)
    back_one(steps - SECOND, SECOND)
    start(1)

    def back_zero(start, size):
        now = pl.ds(start, size)
        if start + size == steps:
            far = jnp.concatenate(
                [far_zero[pl.ds(start + FIRST, size - FIRST)], wide(far_zero_tail[...])], axis=0
            )
        else:
            far = far_zero[pl.ds(start + FIRST, size)]
        grad_zero = (near_zero[now] + far).astype(jnp.bfloat16)
        hat_x, normed = normalize(start, size)
        in_grad[...] += tn(normed, grad_zero)
        grad_hat = nt(grad_zero, w_in[...]) * gain
        hat[now] = grad_hat
        acc[8] += fold(grad_hat)
        acc[9] += fold(grad_hat * hat_x)

    back_zero(0, steps - SECOND)
    pl.when(has_later)(halo[3].wait_recv)
    back_zero(steps - SECOND, SECOND)
    scatter(1)

    def column(k):
        return jnp.sum(acc[k], axis=0, keepdims=True)

    sum_a, sum_b, out_a, out_b = column(8), column(9), column(2), column(3) / gain
    ends[0:1] = sum_a
    ends[1:2] = sum_b
    ends[2:3] = out_a
    ends[3:4] = out_b
    ends_line = line(2, ends, ends_z, Z, depth, on_z)
    for p in range(PARTS):
        last[8 * p : 8 * p + 4] = in_grad[4 * p : 4 * p + 4]
    last[4:5] = (sum_b - out_b * spread) / gain
    last[12:13] = (sum_a - out_a * spread) / gain
    last[20:21] = column(6)
    last[28:29] = column(7)
    last[36:37] = column(4)
    last[44:45] = column(5)
    each(1, PARTS, lambda k: last_one_copy(k).start())
    middle(0)
    ends_line.wait()
    ends[...] = jnp.sum(ends_z[...], axis=0)
    ends_line = line(3, ends, ends_x, X, across, on_x)
    middle(1)
    middle(2)
    gather(0)
    ends_line.wait()
    totals = jnp.sum(ends_x[...], axis=0) / total_steps
    slant = inverse * (totals[3:4] - inverse * totals[1:2])
    level = totals[2:3] - inverse * totals[0:1]
    def resolve(c):
        now = at(c * ROWS, ROWS)
        hat[now] = hat[now] * inverse + ((x[now] - mean) * slant + level)

    each(0, chunks, resolve)
    gather(1)
    gather(2)
    share(0)
    share(1)
    share(2)

    @pl.when(tm < TM - 1)
    def _():
        halo[0].wait_send()
        halo[1].wait_send()

    @pl.when(tm > 0)
    def _():
        halo[2].wait_send()
        halo[3].wait_send()

    finish(0)
    finish(1)
    finish(2)


def unpack_kernel(
    hat, early, late, last, grad, conv, bias, res, skip, out, into, gain, shift, store_sem
):
    store = pltpu.make_async_copy(hat, grad, store_sem)
    store.start()
    for layer, src in ((0, late), (1, early)):
        for tap in range(2):
            for half in range(2):
                conv[layer, tap, :, half * 128 : half * 128 + 128] = src[
                    pl.ds(half * 256 + tap * 128, 128)
                ].astype(jnp.float32)
    for layer in range(2):
        for half in range(2):
            skip[layer, :, half * 128 : half * 128 + 128] = early[
                pl.ds(512 + half * 256 + layer * 128, 128)
            ].astype(jnp.float32)
            bias[layer : layer + 1, half * 128 : half * 128 + 128] = last[
                pl.ds(20 + layer * 16 + half * 8, 1)
            ]
    out[...] = late[640:896].astype(jnp.float32)
    res[...] = late[512:640].astype(jnp.float32)
    for p in range(PARTS):
        into[4 * p : 4 * p + 4] = last[8 * p : 8 * p + 4]
    gain[...] = last[4:5]
    shift[...] = last[12:13]
    store.wait()


def on_device(
    series_data,
    cotangent,
    in_weight,
    convolution_weight,
    convolution_bias,
    res_weight,
    skip_weight,
    output_weight,
    norm_gain_vector,
    norm_offset_vector,
):
    steps = series_data.shape[1]
    f32, bf16 = jnp.float32, jnp.bfloat16
    vmem = pl.BlockSpec(memory_space=pltpu.VMEM)
    hbm = pl.BlockSpec(memory_space=pltpu.HBM)
    sem = pltpu.SemaphoreType.DMA
    shape = jax.ShapeDtypeStruct
    field = pltpu.VMEM((steps, 128), f32)

    sizes = (EARLY, LATE, LAST)
    wires = (bf16, bf16, f32)

    def slots(lead):
        return [pltpu.VMEM((lead, n, 128), wire) for n, wire in zip(sizes, wires)]

    def blocks(count):
        return [pltpu.VMEM((count * n, 128), wire) for n, wire in zip(sizes, wires)]

    def wide_blocks(count):
        return [pltpu.VMEM((count * n, 128), f32) for n in sizes]

    hat, early, late, last = pl.pallas_call(
        block_kernel,
        name="block",
        out_shape=(
            pltpu.VMEM((steps, 128), f32),
            *blocks(PARTS),
        ),
        in_specs=[hbm] * 10,
        out_specs=(vmem,) * 4,
        scratch_shapes=[
            pltpu.VMEM((128, 128), bf16),
            pltpu.VMEM((2, 256, 256), bf16),
            pltpu.VMEM((2, 256), f32),
            pltpu.VMEM((128, 128), bf16),
            pltpu.VMEM((256, 256), bf16),
            pltpu.VMEM((256, 128), bf16),
            pltpu.VMEM((1, 128), f32),
            pltpu.VMEM((1, 128), f32),
            field,
            field,
            pltpu.VMEM((steps + FIRST, 128), bf16),
            pltpu.VMEM((steps + SECOND, 128), bf16),
            pltpu.VMEM((steps, 128), bf16),
            field,
            field,
            field,
            field,
            field,
            field,
            field,
            pltpu.VMEM((SECOND, 128), bf16),
            pltpu.VMEM((SECOND, 128), bf16),
            pltpu.VMEM((FIRST, 128), bf16),
            pltpu.VMEM((FIRST, 128), bf16),
            *wide_blocks(PARTS),
            pltpu.VMEM((128, 128), f32),
            pltpu.VMEM((10, 8, 128), f32),
            pltpu.VMEM((steps // ROWS, 2, 128), f32),
            pltpu.VMEM((2, 128), f32),
            pltpu.VMEM((TM, 2, 128), f32),
            pltpu.VMEM((4, 128), f32),
            pltpu.VMEM((Z, 4, 128), f32),
            pltpu.VMEM((X, 4, 128), f32),
            *blocks(PLANE)[:2],
            *wide_blocks(PLANE)[:2],
            *blocks(PLANE)[:2],
            *slots(PLANE)[:2],
            pltpu.VMEM((PARTS, LAST, 128), f32),
            *slots(Z),
            *blocks(1),
            sem((steps // ROWS + 9,)),
            sem((4,)),
            sem((4,)),
            sem((4,)),
            sem((4,)),
            *[sem((3,))] * 10,
        ],
        compiler_params=pltpu.CompilerParams(
            collective_id=0, has_side_effects=True, vmem_limit_bytes=56 * 1024 * 1024
        ),
    )(
        series_data[0],
        cotangent[0],
        in_weight,
        convolution_weight.reshape(2, 256, 256),
        convolution_bias,
        res_weight,
        skip_weight.reshape(256, 256),
        output_weight,
        norm_gain_vector.reshape(1, 128),
        norm_offset_vector.reshape(1, 128),
    )
    grad, conv, bias, res, skip, out, into, gain, shift = pl.pallas_call(
        unpack_kernel,
        name="unpack",
        out_shape=(
            shape((steps, 128), f32),
            shape((2, 2, 128, 256), f32),
            shape((2, 256), f32),
            shape((128, 128), f32),
            shape((2, 128, 256), f32),
            shape((256, 128), f32),
            shape((128, 128), f32),
            shape((1, 128), f32),
            shape((1, 128), f32),
        ),
        in_specs=[vmem] * 4,
        out_specs=(hbm,) + (vmem,) * 8,
        scratch_shapes=[sem],
        compiler_params=pltpu.CompilerParams(vmem_limit_bytes=8 * 1024 * 1024),
    )(hat, early, late, last)
    return grad[None], conv, bias, res, skip, out, into, gain.reshape(128), shift.reshape(128)


def solution(mesh):
    split = P("series", "tm", None)
    return jax.shard_map(
        on_device,
        mesh=mesh,
        in_specs=(split, split) + (P(),) * 8,
        out_specs=(split,) + (P(),) * 8,
        check_vma=False,
    )
```

```python
import jax
import jax.numpy as jnp
from jax import lax
from jax.experimental import pallas as pl
from jax.experimental.pallas import tpu as pltpu
from jax.sharding import PartitionSpec as P

FIRST = 256
SECOND = 512
TM = 32
SER = 8
X = 4
Z = 8
Y = 4
PLANE = X * Y
PARTS = 2 * PLANE
ROWS = 1024
MESH = pl.DeviceIdType.MESH
EARLY, LATE, LAST = 32, 32, 8

epsilon = 1e-05
gelu_coeff = 0.7978845608
cubic_coeff = 0.044715


def nn(left, right):
    return jnp.dot(left, right, preferred_element_type=jnp.float32)


def nt(left, right):
    return lax.dot_general(
        left, right, (((1,), (1,)), ((), ())), preferred_element_type=jnp.float32
    )


def tn(left, right):
    return lax.dot_general(
        left, right, (((0,), (0,)), ((), ())), preferred_element_type=jnp.float32
    )


def fold(values):
    return jnp.sum(values.reshape(-1, 8, values.shape[-1]), axis=0)


def each(lo, hi, body):
    def run(k, carry):
        body(k)
        return carry

    lax.fori_loop(lo, hi, run, 0)


def at(start, size):
    return pl.ds(pl.multiple_of(start, 8), size)


def remote(src, dst, s_sem, r_sem, device):
    return pltpu.make_async_remote_copy(
        src_ref=src,
        dst_ref=dst,
        send_sem=s_sem,
        recv_sem=r_sem,
        device_id=device,
        device_id_type=MESH,
    )


def block_kernel(
    x_hbm,
    cot_hbm,
    w_in_hbm,
    w_conv_hbm,
    bias_hbm,
    w_res_hbm,
    w_skip_hbm,
    w_out_hbm,
    gain_hbm,
    offset_hbm,
    hat,
    early_out,
    late_out,
    last_out,
    w_in,
    w_conv,
    bias,
    w_res,
    w_skip,
    w_out,
    gain_ref,
    offset_ref,
    x,
    cot,
    level_zero,
    level_one,
    gated_one,
    tanh_one,
    sigm_one,
    incoming_one,
    near_one,
    far_one,
    near_zero,
    far_zero,
    far_one_head,
    far_one_tail,
    far_zero_head,
    far_zero_tail,
    early,
    late,
    last,
    in_grad,
    acc,
    pieces,
    stats,
    stats_all,
    ends,
    ends_z,
    ends_x,
    early_pair,
    late_pair,
    early_half,
    late_half,
    early_send,
    late_send,
    early_one,
    late_one,
    last_one,
    early_two,
    late_two,
    last_two,
    early_block,
    late_block,
    last_block,
    load_sem,
    halo_s,
    halo_r,
    line_s,
    line_r,
    pair_s,
    pair_r,
    one_s,
    one_r,
    two_s,
    two_r,
    three_s,
    three_r,
    back_s,
    back_r,
):
    steps = x.shape[0]
    chunks = steps // ROWS
    total_steps = float(steps * TM)
    ser = lax.axis_index("series")
    tm = lax.axis_index("tm")
    across, depth = tm // Z, lax.rem(tm, Z)
    up, core = ser // 2, lax.rem(ser, 2)
    mine = across * Y + up
    mate = {"series": ser + 1 - 2 * core}

    def on_z(peer):
        return {"tm": across * Z + peer}

    def on_x(peer):
        return {"tm": peer * Z + depth}

    def on_plane(peer):
        return {"series": lax.rem(peer, Y) * 2 + core, "tm": (peer // Y) * Z + depth}

    def load_x(c):
        return pltpu.make_async_copy(
            x_hbm.at[at(c * ROWS, ROWS)], x.at[at(c * ROWS, ROWS)], load_sem.at[c]
        )

    load_cot = pltpu.make_async_copy(cot_hbm, cot, load_sem.at[chunks])
    each(0, chunks, lambda c: load_x(c).start())
    load_cot.start()
    params = [
        pltpu.make_async_copy(src, dst, load_sem.at[chunks + 1 + k])
        for k, (src, dst) in enumerate(
            (
                (w_in_hbm, w_in),
                (w_conv_hbm, w_conv),
                (bias_hbm, bias),
                (w_res_hbm, w_res),
                (w_skip_hbm, w_skip),
                (w_out_hbm, w_out),
                (gain_hbm, gain_ref),
                (offset_hbm, offset_ref),
            )
        )
    ]
    for copy in params:
        copy.start()

    barrier = pltpu.get_barrier_semaphore()

    def hello(device):
        pl.semaphore_signal(barrier, inc=1, device_id=device, device_id_type=MESH)

    for k in range(1, TM):
        hello({"tm": lax.rem(tm + k, TM)})
    for k in range(1, Y):
        hello({"series": lax.rem(up + k, Y) * 2 + core})
    hello(mate)

    acc[...] = jnp.zeros_like(acc)
    early[...] = jnp.zeros_like(early)
    late[...] = jnp.zeros_like(late)
    last[...] = jnp.zeros_like(last)
    in_grad[...] = jnp.zeros_like(in_grad)

    @pl.when(tm == 0)
    def _():
        level_zero[pl.ds(0, FIRST)] = jnp.zeros((FIRST, 128), jnp.bfloat16)
        level_one[pl.ds(0, SECOND)] = jnp.zeros((SECOND, 128), jnp.bfloat16)

    @pl.when(tm == TM - 1)
    def _():
        far_one_tail[...] = jnp.zeros_like(far_one_tail)
        far_zero_tail[...] = jnp.zeros_like(far_zero_tail)

    def combine(slots, count):
        sums = slots[:, 0]
        total = jnp.sum(sums, axis=0, keepdims=True)
        shift = sums / count - total / (count * slots.shape[0])
        squares = slots[:, 1] + count * (shift * shift)
        return total, jnp.sum(squares, axis=0, keepdims=True)

    def sum_x(c):
        load_x(c).wait()
        values = x[at(c * ROWS, ROWS)]
        total = jnp.sum(fold(values), axis=0, keepdims=True)
        centred = values - total / ROWS
        squares = jnp.sum(fold(centred * centred), axis=0, keepdims=True)
        pieces[pl.ds(c, 1), 0:1] = total[None]
        pieces[pl.ds(c, 1), 1:2] = squares[None]

    each(0, chunks, sum_x)
    total, squares = combine(pieces, float(ROWS))
    stats[0:1] = total
    stats[1:2] = squares
    pl.semaphore_wait(barrier, TM + Y - 1)

    def line(which, own, slots, count, me, device):
        def copy(peer, slot):
            return remote(own, slots.at[slot], line_s.at[which], line_r.at[which], device(peer))

        rest = slots.at[pl.ds(0, count - 1)]
        whole = remote(rest, rest, line_s.at[which], line_r.at[which], device(me))
        for k in range(1, count):
            copy(lax.rem(me + k, count), me).start()
        slots[pl.ds(me, 1)] = own[...][None]
        return whole

    line(0, stats, stats_all, TM, tm, lambda peer: {"tm": peer}).wait()
    total, squares = combine(stats_all, float(steps))
    mean = total / total_steps
    variance = squares / total_steps
    inverse = lax.rsqrt(variance + epsilon)
    spread = jnp.sqrt(variance + epsilon)
    for copy in params:
        copy.wait()
    gain, offset = gain_ref[...], offset_ref[...]
    scale = spread / gain

    later, earlier = {"tm": lax.rem(tm + 1, TM)}, {"tm": lax.rem(tm + TM - 1, TM)}
    halo = (
        remote(
            level_zero.at[pl.ds(steps, FIRST)],
            level_zero.at[pl.ds(0, FIRST)],
            halo_s.at[0],
            halo_r.at[0],
            later,
        ),
        remote(
            level_one.at[pl.ds(steps, SECOND)],
            level_one.at[pl.ds(0, SECOND)],
            halo_s.at[1],
            halo_r.at[1],
            later,
        ),
        remote(
            far_one_head,
            far_one_tail,
            halo_s.at[2],
            halo_r.at[2],
            earlier,
        ),
        remote(
            far_zero_head,
            far_zero_tail,
            halo_s.at[3],
            halo_r.at[3],
            earlier,
        ),
    )

    has_later, has_earlier = tm < TM - 1, tm > 0

    def normalize(start, size):
        hat_x = (x[pl.ds(start, size)] - mean) * inverse
        return hat_x, (hat_x * gain + offset).astype(jnp.bfloat16)

    def project(start, size):
        _, normed = normalize(start, size)
        level_zero[pl.ds(FIRST + start, size)] = nn(normed, w_in[...]).astype(jnp.bfloat16)

    def gates(act):
        return jnp.tanh(act[:, :128]), 0.5 * jnp.tanh(0.5 * act[:, 128:]) + 0.5

    def window_zero(start, size):
        return jnp.concatenate(
            [level_zero[pl.ds(start, size)], level_zero[pl.ds(start + FIRST, size)]], axis=1
        )

    def window_one(start, size):
        return jnp.concatenate(
            [level_one[pl.ds(start, size)], level_one[pl.ds(start + SECOND, size)]], axis=1
        )

    def layer_one(start, size):
        now = pl.ds(start, size)
        tanh, sigm = gates(nn(window_zero(start, size), w_conv[0]) + bias[0:1])
        gated = (tanh * sigm).astype(jnp.bfloat16)
        tanh_one[now] = tanh
        sigm_one[now] = sigm
        gated_one[now] = gated
        level = level_zero[pl.ds(start + FIRST, size)].astype(jnp.float32)
        level_one[pl.ds(start + SECOND, size)] = (level + nn(gated, w_res[...])).astype(
            jnp.bfloat16
        )

    project(steps - SECOND - FIRST, SECOND + FIRST)
    pl.when(has_later)(halo[0].start)
    layer_one(steps - SECOND, SECOND)
    pl.when(has_later)(halo[1].start)
    project(0, steps - SECOND - FIRST)
    layer_one(SECOND, steps - 2 * SECOND)

    def gate_back(incoming, tanh, sigm):
        part = incoming * sigm
        return part * (1.0 - tanh * tanh), part * tanh * (1.0 - sigm)

    load_cot.wait()

    def layer_two(start, size):
        now = pl.ds(start, size)
        window = window_one(start, size)
        tanh, sigm = gates(nn(window, w_conv[1]) + bias[1:2])
        gated = (tanh * sigm).astype(jnp.bfloat16)
        both = jnp.concatenate([gated_one[now], gated], axis=1)
        skip = nn(both, w_skip[...])
        square = skip * skip
        half = 0.5 * jnp.tanh(
            skip * (gelu_coeff + (gelu_coeff * cubic_coeff) * square)
        ) + 0.5
        value = skip * half
        slope = half + value * (1.0 - half) * (
            2.0 * gelu_coeff + (6.0 * gelu_coeff * cubic_coeff) * square
        )
        rectified = value.astype(jnp.bfloat16)
        forecast = nn(rectified, w_out[...])
        gradient = cot[now]
        acc[2] += fold(gradient)
        acc[3] += fold(gradient * (forecast - offset))
        scaled = (gradient * scale).astype(jnp.bfloat16)
        out_part = tn(rectified, scaled)
        late[640:896] += out_part
        back_skip = (nt(scaled, w_out[...]) * slope).astype(jnp.bfloat16)
        skip_part = tn(both, back_skip)
        early[512:768] += skip_part[:, :128]
        early[768:1024] += skip_part[:, 128:]
        incoming = nt(back_skip, w_skip[...])
        incoming_one[now] = incoming[:, :128]
        first, second = gate_back(incoming[:, 128:], tanh, sigm)
        acc[4] += fold(first)
        acc[5] += fold(second)
        pre = jnp.concatenate([first, second], axis=1).astype(jnp.bfloat16)
        conv_part = tn(window, pre)
        early[0:256] += conv_part[:, :128]
        early[256:512] += conv_part[:, 128:]
        carried = nt(pre, w_conv[1])
        far_one[now] = carried[:, :128]
        near_one[now] = carried[:, 128:]

    layer_two(4 * SECOND, steps - 4 * SECOND)
    pl.when(has_earlier)(halo[0].wait_recv)
    layer_one(0, SECOND)
    pl.when(has_earlier)(halo[1].wait_recv)
    layer_two(0, SECOND)
    far_one_head[...] = far_one[pl.ds(0, SECOND)].astype(jnp.bfloat16)
    pl.when(has_earlier)(halo[2].start)
    layer_two(SECOND, 3 * SECOND)

    groups = (
        (early, early_pair, early_half, early_one, early_block, early_two, early_out, EARLY),
        (late, late_pair, late_half, late_one, late_block, late_two, late_out, LATE),
        (last, None, None, last_one, last_block, last_two, last_out, LAST),
    )
    sends = (early_send, late_send)

    def pair(g):
        return remote(sends[g], groups[g][1], pair_s.at[g], pair_r.at[g], mate)

    def one(g, k):
        got, size = groups[g][3], groups[g][7]
        peer = lax.rem(mine + k, PLANE)
        return remote(
            sends[g].at[at(peer * size, size)],
            got.at[k],
            one_s.at[g],
            one_r.at[g],
            on_plane(peer),
        )

    def two(g, k):
        block, got = groups[g][4], groups[g][5]
        peer = lax.rem(depth + k, Z)
        return remote(block, got.at[depth], two_s.at[g], two_r.at[g], on_z(peer))

    def three(g, k):
        out, size = groups[g][6], groups[g][7]
        where = out.at[at(owner * size, size)]
        peer = lax.rem(mine + k, PLANE)
        return remote(where, where, three_s.at[g], three_r.at[g], on_plane(peer))

    def back(g):
        out, size = groups[g][6], groups[g][7] * PLANE
        where = out.at[at(core * size, size)]
        return remote(where, where, back_s.at[g], back_r.at[g], mate)

    def whole(g, ref, count, s_sem, r_sem):
        rest = ref.at[pl.ds(0, count)]
        return remote(rest, rest, s_sem.at[g], r_sem.at[g], mate)

    owner = core * PLANE + mine

    def on_owner(p):
        member = lax.rem(p, PLANE)
        return {
            "series": lax.rem(member, Y) * 2 + p // PLANE,
            "tm": (member // Y) * Z + depth,
        }

    def last_one_copy(k):
        peer = lax.rem(owner + k, PARTS)
        return remote(
            last.at[at(peer * LAST, LAST)], last_one.at[k], one_s.at[2], one_r.at[2], on_owner(peer)
        )

    def last_three_copy(k):
        where = last_out.at[at(owner * LAST, LAST)]
        peer = lax.rem(owner + k, PARTS)
        return remote(where, where, three_s.at[2], three_r.at[2], on_owner(peer))

    def all_one(g):
        return whole(g, groups[g][3], groups[g][3].shape[0] - 1, one_s, one_r)

    def all_two(g):
        return whole(g, groups[g][5], Z - 1, two_s, two_r)

    def all_three(g):
        peers = (PARTS if g == 2 else PLANE) - 1
        return whole(g, groups[g][6], peers * groups[g][7], three_s, three_r)

    def wide(values):
        return values.astype(jnp.float32)

    def start(g):
        src, size = groups[g][0], groups[g][7] * PLANE
        sends[g][...] = src[at((1 - core) * size, size)].astype(sends[g].dtype)
        pair(g).start()

    def scatter(g):
        src, got, half, slots, _, _, _, size = groups[g]
        pair(g).wait()
        total = src[at(core * PLANE * size, PLANE * size)] + wide(got[...])
        half[...] = total
        sends[g][...] = total.astype(sends[g].dtype)
        each(1, PLANE, lambda k: one(g, k).start())

    def middle(g):
        _, _, half, slots, block, far, _, size = groups[g]
        all_one(g).wait_recv()
        total = last[at(owner * size, size)] if g == 2 else half[at(mine * size, size)]
        for p in range(1, slots.shape[0]):
            total = total + wide(slots[p])
        block[...] = total.astype(block.dtype)
        each(1, Z, lambda k: two(g, k).start())
        far[pl.ds(depth, 1)] = block[...][None]

    def gather(g):
        _, _, _, _, _, far, out, size = groups[g]
        all_two(g).wait_recv()
        total = wide(far[0])
        for z in range(1, Z):
            total = total + wide(far[z])
        out[at(owner * size, size)] = total.astype(out.dtype)
        if g == 2:
            each(1, PARTS, lambda k: last_three_copy(k).start())
        else:
            each(1, PLANE, lambda k: three(g, k).start())

    def share(g):
        all_three(g).wait_recv()
        if g < 2:
            back(g).start()

    def finish(g):
        if g < 2:
            back(g).wait()
        all_one(g).wait_send()
        all_two(g).wait_send()
        all_three(g).wait_send()

    start(0)

    def back_one(start, size):
        now = pl.ds(start, size)
        last_rows = start + size == steps
        far = wide(far_one_tail[...]) if last_rows else far_one[pl.ds(start + SECOND, size)]
        grad_one = (near_one[now] + far).astype(jnp.bfloat16)
        late[512:640] += tn(gated_one[now], grad_one)
        incoming = incoming_one[now] + nt(grad_one, w_res[...])
        first, second = gate_back(incoming, tanh_one[now], sigm_one[now])
        acc[6] += fold(first)
        acc[7] += fold(second)
        pre = jnp.concatenate([first, second], axis=1).astype(jnp.bfloat16)
        conv_part = tn(window_zero(start, size), pre)
        late[0:256] += conv_part[:, :128]
        late[256:512] += conv_part[:, 128:]
        carried = nt(pre, w_conv[0])
        far_zero[now] = carried[:, :128]
        near_zero[now] = grad_one.astype(jnp.float32) + carried[:, 128:]

    back_one(0, SECOND)
    far_zero_head[...] = far_zero[pl.ds(0, FIRST)].astype(jnp.bfloat16)
    pl.when(has_earlier)(halo[3].start)
    back_one(SECOND, steps - 2 * SECOND)
    scatter(0)
    pl.when(has_later)(halo[2].wait_recv)
    back_one(steps - SECOND, SECOND)
    start(1)

    def back_zero(start, size):
        now = pl.ds(start, size)
        if start + size == steps:
            far = jnp.concatenate(
                [far_zero[pl.ds(start + FIRST, size - FIRST)], wide(far_zero_tail[...])], axis=0
            )
        else:
            far = far_zero[pl.ds(start + FIRST, size)]
        grad_zero = (near_zero[now] + far).astype(jnp.bfloat16)
        hat_x, normed = normalize(start, size)
        in_grad[...] += tn(normed, grad_zero)
        grad_hat = nt(grad_zero, w_in[...]) * gain
        hat[now] = grad_hat
        acc[8] += fold(grad_hat)
        acc[9] += fold(grad_hat * hat_x)

    back_zero(0, steps - SECOND)
    pl.when(has_later)(halo[3].wait_recv)
    back_zero(steps - SECOND, SECOND)
    scatter(1)

    def column(k):
        return jnp.sum(acc[k], axis=0, keepdims=True)

    sum_a, sum_b, out_a, out_b = column(8), column(9), column(2), column(3) / gain
    ends[0:1] = sum_a
    ends[1:2] = sum_b
    ends[2:3] = out_a
    ends[3:4] = out_b
    ends_line = line(2, ends, ends_z, Z, depth, on_z)
    for p in range(PARTS):
        last[8 * p : 8 * p + 4] = in_grad[4 * p : 4 * p + 4]
    last[4:5] = (sum_b - out_b * spread) / gain
    last[12:13] = (sum_a - out_a * spread) / gain
    last[20:21] = column(6)
    last[28:29] = column(7)
    last[36:37] = column(4)
    last[44:45] = column(5)
    each(1, PARTS, lambda k: last_one_copy(k).start())
    middle(0)
    ends_line.wait()
    ends[...] = jnp.sum(ends_z[...], axis=0)
    ends_line = line(3, ends, ends_x, X, across, on_x)
    middle(1)
    middle(2)
    gather(0)
    ends_line.wait()
    totals = jnp.sum(ends_x[...], axis=0) / total_steps
    slant = inverse * (totals[3:4] - inverse * totals[1:2])
    level = totals[2:3] - inverse * totals[0:1]
    def resolve(c):
        now = at(c * ROWS, ROWS)
        hat[now] = hat[now] * inverse + ((x[now] - mean) * slant + level)

    each(0, chunks, resolve)
    gather(1)
    gather(2)
    share(0)
    share(1)
    share(2)

    @pl.when(tm < TM - 1)
    def _():
        halo[0].wait_send()
        halo[1].wait_send()

    @pl.when(tm > 0)
    def _():
        halo[2].wait_send()
        halo[3].wait_send()

    finish(0)
    finish(1)
    finish(2)


def unpack_kernel(
    hat, early, late, last, grad, conv, bias, res, skip, out, into, gain, shift, store_sem
):
    store = pltpu.make_async_copy(hat, grad, store_sem)
    store.start()
    for layer, src in ((0, late), (1, early)):
        for tap in range(2):
            for half in range(2):
                conv[layer, tap, :, half * 128 : half * 128 + 128] = src[
                    pl.ds(half * 256 + tap * 128, 128)
                ].astype(jnp.float32)
    for layer in range(2):
        for half in range(2):
            skip[layer, :, half * 128 : half * 128 + 128] = early[
                pl.ds(512 + half * 256 + layer * 128, 128)
            ].astype(jnp.float32)
            bias[layer : layer + 1, half * 128 : half * 128 + 128] = last[
                pl.ds(20 + layer * 16 + half * 8, 1)
            ]
    out[...] = late[640:896].astype(jnp.float32)
    res[...] = late[512:640].astype(jnp.float32)
    for p in range(PARTS):
        into[4 * p : 4 * p + 4] = last[8 * p : 8 * p + 4]
    gain[...] = last[4:5]
    shift[...] = last[12:13]
    store.wait()


def on_device(
    series_data,
    cotangent,
    in_weight,
    convolution_weight,
    convolution_bias,
    res_weight,
    skip_weight,
    output_weight,
    norm_gain_vector,
    norm_offset_vector,
):
    steps = series_data.shape[1]
    f32, bf16 = jnp.float32, jnp.bfloat16
    vmem = pl.BlockSpec(memory_space=pltpu.VMEM)
    hbm = pl.BlockSpec(memory_space=pltpu.HBM)
    sem = pltpu.SemaphoreType.DMA
    shape = jax.ShapeDtypeStruct
    field = pltpu.VMEM((steps, 128), f32)

    sizes = (EARLY, LATE, LAST)
    wires = (bf16, bf16, f32)

    def slots(lead):
        return [pltpu.VMEM((lead, n, 128), wire) for n, wire in zip(sizes, wires)]

    def blocks(count):
        return [pltpu.VMEM((count * n, 128), wire) for n, wire in zip(sizes, wires)]

    def wide_blocks(count):
        return [pltpu.VMEM((count * n, 128), f32) for n in sizes]

    hat, early, late, last = pl.pallas_call(
        block_kernel,
        name="block",
        out_shape=(
            pltpu.VMEM((steps, 128), f32),
            *blocks(PARTS),
        ),
        in_specs=[hbm] * 10,
        out_specs=(vmem,) * 4,
        scratch_shapes=[
            pltpu.VMEM((128, 128), bf16),
            pltpu.VMEM((2, 256, 256), bf16),
            pltpu.VMEM((2, 256), f32),
            pltpu.VMEM((128, 128), bf16),
            pltpu.VMEM((256, 256), bf16),
            pltpu.VMEM((256, 128), bf16),
            pltpu.VMEM((1, 128), f32),
            pltpu.VMEM((1, 128), f32),
            field,
            field,
            pltpu.VMEM((steps + FIRST, 128), bf16),
            pltpu.VMEM((steps + SECOND, 128), bf16),
            pltpu.VMEM((steps, 128), bf16),
            field,
            field,
            field,
            field,
            field,
            field,
            field,
            pltpu.VMEM((SECOND, 128), bf16),
            pltpu.VMEM((SECOND, 128), bf16),
            pltpu.VMEM((FIRST, 128), bf16),
            pltpu.VMEM((FIRST, 128), bf16),
            *wide_blocks(PARTS),
            pltpu.VMEM((128, 128), f32),
            pltpu.VMEM((10, 8, 128), f32),
            pltpu.VMEM((steps // ROWS, 2, 128), f32),
            pltpu.VMEM((2, 128), f32),
            pltpu.VMEM((TM, 2, 128), f32),
            pltpu.VMEM((4, 128), f32),
            pltpu.VMEM((Z, 4, 128), f32),
            pltpu.VMEM((X, 4, 128), f32),
            *blocks(PLANE)[:2],
            *wide_blocks(PLANE)[:2],
            *blocks(PLANE)[:2],
            *slots(PLANE)[:2],
            pltpu.VMEM((PARTS, LAST, 128), f32),
            *slots(Z),
            *blocks(1),
            sem((steps // ROWS + 9,)),
            sem((4,)),
            sem((4,)),
            sem((4,)),
            sem((4,)),
            *[sem((3,))] * 10,
        ],
        compiler_params=pltpu.CompilerParams(
            collective_id=0, has_side_effects=True, vmem_limit_bytes=56 * 1024 * 1024
        ),
    )(
        series_data[0],
        cotangent[0],
        in_weight,
        convolution_weight.reshape(2, 256, 256),
        convolution_bias,
        res_weight,
        skip_weight.reshape(256, 256),
        output_weight,
        norm_gain_vector.reshape(1, 128),
        norm_offset_vector.reshape(1, 128),
    )
    grad, conv, bias, res, skip, out, into, gain, shift = pl.pallas_call(
        unpack_kernel,
        name="unpack",
        out_shape=(
            shape((steps, 128), f32),
            shape((2, 2, 128, 256), f32),
            shape((2, 256), f32),
            shape((128, 128), f32),
            shape((2, 128, 256), f32),
            shape((256, 128), f32),
            shape((128, 128), f32),
            shape((1, 128), f32),
            shape((1, 128), f32),
        ),
        in_specs=[vmem] * 4,
        out_specs=(hbm,) + (vmem,) * 8,
        scratch_shapes=[sem],
        compiler_params=pltpu.CompilerParams(vmem_limit_bytes=8 * 1024 * 1024),
    )(hat, early, late, last)
    return grad[None], conv, bias, res, skip, out, into, gain.reshape(128), shift.reshape(128)


def solution(mesh):
    split = P("series", "tm", None)
    return jax.shard_map(
        on_device,
        mesh=mesh,
        in_specs=(split, split) + (P(),) * 8,
        out_specs=(split,) + (P(),) * 8,
        check_vma=False,
    )
```
